32 devices in a mesh: dp: 8 (over z, x), tm: 4 (over y, core).
Axes of the slice: x: 2, y: 2, z: 4, core: 2. Of those that a mesh axis runs over, the one named last changes fastest.
Arguments:
- mel_pieces: bfloat16 [8, 128, 2048], P('dp', 'tm'), may hold values from -6 to 6
- dest_owner: int32 [8, 128], P('dp', 'tm'), may hold values from 0 to 7, as said below
- dest_slot: int32 [8, 128], P('dp', 'tm'), may hold values from 0 to 31, as said below
- segment_ids: int32 [8, 512], P('dp'), may hold values from 0 to 3, never falling along the last dimension, each value on 1 to 256 neighbouring positions
- out_grad: bfloat16 [8, 512, 1024], P('dp', 'tm'), may hold values from -6 to 6
- stem_weight: bfloat16 [512, 1024], P(('dp', 'tm')), may hold values from -0.25 to 0.25
- up_weight: bfloat16 [1024, 2048], P(('dp', 'tm')), may hold values from -0.1875 to 0.1875
- down_weight: bfloat16 [1024, 1024], P(('dp', 'tm')), may hold values from -0.1875 to 0.1875
- depth_kernel: bfloat16 [1024, 31], P(('dp', 'tm')), may hold values from -1 to 1
- gain_pre: bfloat16 [1024], P(('dp', 'tm')), may hold values from 0.099609375 to 1.8984375
- gain_post: bfloat16 [1024], P(('dp', 'tm')), may hold values from 0.099609375 to 1.8984375
Outputs:
- y_out: bfloat16 [8, 512, 1024], P('dp', 'tm')
- grad_stem: float32 [512, 1024], P(('dp', 'tm'))
- grad_up: float32 [1024, 2048], P('dp', 'tm')
- grad_down: float32 [1024, 1024], P('dp', 'tm')
- grad_kernel: float32 [1024, 31], P(('dp', 'tm'))
- grad_gain_pre: float32 [1024], P(('dp', 'tm'))
- grad_gain_post: float32 [1024], P(('dp', 'tm'))
The draws below stay inside these ranges and needn't reach their ends.
Inputs may be any that keep to these rules, and one draw needn't show every extreme that they name: `dest_owner`: A loader piece in time block t (columns t * 32 to (t + 1) * 32 - 1) goes to a packed row's time block t. From one loader row and time block, every packed row receives either no piece or exactly 8 pieces, and every packed row receives exactly 32 pieces in each time block. `dest_slot`: for each packed row and time block, the places of the pieces it receives are the numbers 0 to 31, each once.
All inputs are finite; a program needn't handle non-finite values.
Results may differ from the reference program's by a relative error of at most 0.018.
Values may be sent and summed in bfloat16 or wider, within the bound.
No kernel may reach another device: no remote copies, remote signals or barrier semaphores. Data moves between devices by JAX's collectives and lax.ppermute only.
A program may use at most 128 MiB of HBM per device.

```python
import math
import jax
import jax.numpy as jnp
import numpy as np
from jax import lax

D = 1024
KW = 31
SEGMENTS = 4
FEAT = 512
PIECE_FEAT = 2048
PIECES = 32
CAP = 8
SEQ = 512
N_DP = 8
N_TM = 4


def route_tables(key):
    key = jax.random.fold_in(key, 11)
    key_offset, key_rank, key_place = jax.random.split(key, 3)
    offsets = jax.vmap(lambda subkey: jax.random.permutation(subkey, N_DP))(jax.random.split(key_offset, N_TM))
    ranks = jax.vmap(lambda subkey: jax.random.permutation(subkey, PIECES))(jax.random.split(key_rank, N_DP * N_TM))
    ranks = ranks.reshape(N_DP, N_TM, PIECES)
    shuffles = jax.vmap(lambda subkey: jax.random.permutation(subkey, PIECES))(jax.random.split(key_place, N_DP * N_TM))
    shuffles = shuffles.reshape(N_DP, N_TM, PIECES)
    owners = (jnp.transpose(offsets)[:, :, None] + ranks // CAP) % N_DP
    columns = jnp.broadcast_to(jnp.arange(N_TM)[None, :, None], owners.shape)
    places = shuffles[owners, columns, ranks]
    return (owners.reshape(N_DP, N_TM * PIECES).astype(jnp.int32), places.reshape(N_DP, N_TM * PIECES).astype(jnp.int32))


def draw_dest_owner(key, part):
    return route_tables(key)[0]


def draw_dest_slot(key, part):
    return route_tables(key)[1]


def shard_levels(key, extent, cuts, low, high):
    factor_of = 1.0
    for dim, blocks in cuts:
        steps = jax.random.uniform(jax.random.fold_in(jax.random.fold_in(key, 6), dim), (blocks,), jnp.float32, low / len(cuts), high / len(cuts))
        factor_of = factor_of * jnp.repeat(jnp.exp(steps), extent[dim] // blocks).reshape((-1,) + (1,) * (len(extent) - 1 - dim))
    return factor_of


def split_up(amount, total, limit, skew):
    weights = [(1 << 20) // math.isqrt(rank ** skew) + 1 for rank in range(2, amount + 1)]
    spare, given = total - limit - (amount - 1), [1] * (amount - 1)
    while spare > 0:
        candidates = [i for i in range(amount - 1) if given[i] < limit]
        whole, left = sum([weights[i] for i in candidates]), spare
        for i in candidates:
            more = min(limit - given[i], max(1, left * weights[i] // whole), spare)
            given[i] = given[i] + more
            spare = spare - more
    return np.array([limit] + given)


def ragged(key, count, total, bound, lean):
    if count == 2:
        one = jax.random.randint(key, (), max(1, total - bound), min(bound, total - 1) + 1)
        return jnp.stack([one, total - one])
    lengths = jnp.asarray(split_up(count, total, bound, lean), jnp.int32)
    pairs = (count - 1) // 2
    source_of, sink = lengths[1:1 + 2 * pairs:2], lengths[2:2 + 2 * pairs:2]
    room = jnp.minimum(source_of - 1, bound - sink)
    shifted = jax.random.randint(jax.random.fold_in(key, 1), (pairs,), 0, 1 << 20) % (room + 1)
    lengths = lengths.at[1:1 + 2 * pairs:2].set(source_of - shifted).at[2:2 + 2 * pairs:2].set(sink + shifted)
    return lengths[jax.random.permutation(jax.random.fold_in(key, 2), count)]


def scatter_about(key, extent, deviation, reach, cuts=(), kind=jnp.bfloat16):
    values = jax.random.normal(key, extent, jnp.float32) * deviation
    if len(cuts) > 0:
        values = shard_levels(key, extent, cuts, -0.22, 0.18) * values
    return jnp.clip(values, min=-reach, max=reach).astype(kind)


def setup_inputs(seed: int = 0) -> dict:
    arg_keys = jax.random.split(jax.random.key(seed), 12)
    mel_pieces = scatter_about(arg_keys[0], (N_DP, N_TM * PIECES, PIECE_FEAT), 1.0, 6.0, ((0, 8), (1, 4)))
    dest_owner = draw_dest_owner(jax.random.fold_in(arg_keys[11], 71), 0)
    dest_slot = draw_dest_slot(jax.random.fold_in(arg_keys[11], 71), 0)
    segment_ids = jax.vmap(lambda own: jnp.searchsorted(jnp.cumsum(ragged(own, SEGMENTS, SEQ, SEQ // 2, 1)), jnp.arange(SEQ), side="right"))(jax.random.split(arg_keys[3], N_DP)).reshape((N_DP, SEQ)).astype(jnp.int32)
    out_grad = scatter_about(arg_keys[4], (N_DP, SEQ, D), 1.0, 6.0, ((0, 8), (1, 4)))
    stem_weight = scatter_about(arg_keys[5], (FEAT, D), FEAT ** -0.5, 0.25, ((0, 32),))
    up_weight = scatter_about(arg_keys[6], (D, 2 * D), D ** -0.5, 0.1875, ((0, 32),))
    down_weight = scatter_about(arg_keys[7], (D, D), D ** -0.5, 0.1875, ((0, 32),))
    depth_kernel = scatter_about(arg_keys[8], (D, KW), KW ** -0.5, 1.0, ((0, 32),))
    gain_pre = jnp.clip(1.0 + 0.18 * jax.random.normal(arg_keys[9], (D,), jnp.float32), 0.099609375, 1.8984375).astype(jnp.bfloat16)
    gain_post = jnp.clip(1.0 + 0.18 * jax.random.normal(arg_keys[10], (D,), jnp.float32), 0.099609375, 1.8984375).astype(jnp.bfloat16)
    return dict(mel_pieces=mel_pieces, dest_owner=dest_owner, dest_slot=dest_slot, segment_ids=segment_ids, out_grad=out_grad, stem_weight=stem_weight, up_weight=up_weight, down_weight=down_weight, depth_kernel=depth_kernel, gain_pre=gain_pre, gain_post=gain_post)


NORM_EPS = 1e-05

def standardize(values):
    centered = values - lax.optimization_barrier(jnp.mean(values, axis=-1, keepdims=True))
    inverse = lax.rsqrt(lax.optimization_barrier(jnp.mean(centered * centered, axis=-1, keepdims=True)) + NORM_EPS)
    return (centered * inverse, inverse)

def norm_backward(grad_hat, normed_hat, inverse):
    first = lax.optimization_barrier(jnp.mean(grad_hat, axis=-1, keepdims=True))
    second = lax.optimization_barrier(jnp.mean(grad_hat * normed_hat, axis=-1, keepdims=True))
    return (grad_hat - first - normed_hat * second) * inverse

def silu_slope(values):
    sigma = jax.nn.sigmoid(values)
    return sigma * (1.0 + values * (1.0 - sigma))

def depth_forward(padded, kernel, seg_window, seg_centre, length):
    weights = kernel.astype(jnp.float32)
    summed = jnp.zeros((length, padded.shape[1]), jnp.float32)
    for offset in range(weights.shape[1]):
        inside = (seg_window[offset:offset + length] == seg_centre)[:, None]
        summed = summed + jnp.where(inside, padded[offset:offset + length].astype(jnp.float32) * weights[:, offset], 0.0)
    return summed

def depth_backward(padded_grad, padded_in, kernel, seg_window, seg_centre, length):
    margin = (kernel.shape[1] - 1) // 2
    weights = kernel.astype(jnp.float32)
    grad_in = jnp.zeros((length, padded_grad.shape[1]), jnp.float32)
    grad_here = padded_grad[margin:margin + length].astype(jnp.float32)
    columns = []
    for offset in range(weights.shape[1]):
        start = 2 * margin - offset
        inside_back = (seg_window[start:start + length] == seg_centre)[:, None]
        grad_in = grad_in + jnp.where(inside_back, padded_grad[start:start + length].astype(jnp.float32) * weights[:, offset], 0.0)
        inside = (seg_window[offset:offset + length] == seg_centre)[:, None]
        columns.append(lax.optimization_barrier(jnp.sum(jnp.where(inside, grad_here * padded_in[offset:offset + length].astype(jnp.float32), 0.0), axis=0)))
    return (grad_in, jnp.stack(columns, axis=1))

def row_pass(frames, seg_row, grad_out, stem_weight, up_weight, down_weight, depth_kernel, gain_pre, gain_post):
    channels = down_weight.shape[0]
    margin = (depth_kernel.shape[1] - 1) // 2
    length = frames.shape[0]
    gain_one = gain_pre.astype(jnp.float32)
    gain_two = gain_post.astype(jnp.float32)
    stem_pre = jnp.dot(frames, stem_weight, preferred_element_type=jnp.float32)
    stem_out = jax.nn.silu(stem_pre).astype(jnp.bfloat16)
    stem_hat, inverse_one = standardize(stem_out.astype(jnp.float32))
    normed = (stem_hat * gain_one).astype(jnp.bfloat16)
    proj = jnp.dot(normed, up_weight, preferred_element_type=jnp.float32)
    linear = proj[:, :channels]
    gate_sig = jax.nn.sigmoid(proj[:, channels:])
    gated = (linear * gate_sig).astype(jnp.bfloat16)
    seg_window = jnp.pad(seg_row, (margin, margin), constant_values=-1)
    gated_ext = jnp.pad(gated, ((margin, margin), (0, 0)))
    conv = depth_forward(gated_ext, depth_kernel, seg_window, seg_row, length)
    conv_hat, inverse_two = standardize(conv)
    conv_scaled = conv_hat * gain_two
    activated = jax.nn.silu(conv_scaled).astype(jnp.bfloat16)
    y_full = stem_out.astype(jnp.float32) + jnp.dot(activated, down_weight, preferred_element_type=jnp.float32)
    y_out = y_full.astype(jnp.bfloat16)
    grad_act = jnp.dot(grad_out, down_weight.T, preferred_element_type=jnp.float32)
    grad_down = jnp.dot(activated.T, grad_out, preferred_element_type=jnp.float32)
    grad_scaled = grad_act * silu_slope(conv_scaled)
    grad_gain_post = lax.optimization_barrier(jnp.sum(grad_scaled * conv_hat, axis=0))
    grad_conv = norm_backward(grad_scaled * gain_two, conv_hat, inverse_two).astype(jnp.bfloat16)
    grad_ext = jnp.pad(grad_conv, ((margin, margin), (0, 0)))
    grad_gated, grad_kernel = depth_backward(grad_ext, gated_ext, depth_kernel, seg_window, seg_row, length)
    grad_proj = jnp.concatenate([grad_gated * gate_sig, grad_gated * linear * gate_sig * (1.0 - gate_sig)], axis=1).astype(jnp.bfloat16)
    grad_up = jnp.dot(normed.T, grad_proj, preferred_element_type=jnp.float32)
    grad_normed = jnp.dot(grad_proj, up_weight.T, preferred_element_type=jnp.float32)
    grad_gain_pre = lax.optimization_barrier(jnp.sum(grad_normed * stem_hat, axis=0))
    grad_stem_out = grad_out.astype(jnp.float32) + norm_backward(grad_normed * gain_one, stem_hat, inverse_one)
    grad_stem_pre = (grad_stem_out * silu_slope(stem_pre)).astype(jnp.bfloat16)
    grad_stem = jnp.dot(frames.T, grad_stem_pre, preferred_element_type=jnp.float32)
    return (y_out, (grad_stem, grad_up, grad_down, grad_kernel, grad_gain_pre, grad_gain_post))

def reference(mel_pieces, dest_owner, dest_slot, segment_ids, out_grad, stem_weight, up_weight, down_weight, depth_kernel, gain_pre, gain_post):
    blocks = jnp.broadcast_to((jnp.arange(N_TM * PIECES, dtype=jnp.int32) // PIECES)[None, :], dest_owner.shape)
    placed = jnp.zeros((N_DP, N_TM, PIECES, PIECE_FEAT), jnp.bfloat16).at[dest_owner, blocks, dest_slot].set(mel_pieces)
    frames_all = placed.reshape(N_DP, SEQ, FEAT)

    def advance(carry, row):
        frames, seg_row, grad_out = row
        y_row, terms = row_pass(frames, seg_row, grad_out, stem_weight, up_weight, down_weight, depth_kernel, gain_pre, gain_post)
        return (tuple((held + term for held, term in zip(carry, terms))), y_row)
    start = (jnp.zeros((FEAT, D), jnp.float32), jnp.zeros((D, 2 * D), jnp.float32), jnp.zeros((D, D), jnp.float32), jnp.zeros((D, KW), jnp.float32), jnp.zeros((D,), jnp.float32), jnp.zeros((D,), jnp.float32))
    totals, y_out = lax.scan(advance, start, (frames_all, segment_ids, out_grad))
    return (y_out, totals[0], totals[1], totals[2], totals[3], totals[4], totals[5])
```

```python
import jax
import jax.numpy as jnp
from jax import lax
from jax.sharding import PartitionSpec as P

NORM_EPS = 1e-05
BF16 = jnp.bfloat16
F32 = jnp.float32


def stages_of(sizes):
    if sizes["dp"] == 8 and sizes["tm"] == 4:
        return {"dp": ((2, 4), (1, 2)), "tm": ((2, 2), (1, 2))}
    if sizes["dp"] == 64 and sizes["tm"] == 4:
        return {"dp": ((8, 8), (2, 4), (1, 2)), "tm": ((1, 4),)}
    return {axis: ((1, size),) for axis, size in sizes.items()}


def swap(value, axis, mask):
    size = lax.axis_size(axis)
    return lax.ppermute(value, axis, [(i, i ^ mask) for i in range(size)])


def gather_stage(value, axis, stride, size):
    place = (lax.axis_index(axis) // stride) % size
    out = jnp.zeros((size,) + value.shape, value.dtype)
    for k in range(size):
        part = value if k == 0 else swap(value, axis, k * stride)
        out = lax.dynamic_update_slice_in_dim(out, part[None], place ^ k, 0)
    return out


def gather(value, axis, chains):
    shape = value.shape
    sizes = []
    for stride, size in chains:
        value = gather_stage(value, axis, stride, size)
        sizes.insert(0, size)
    count = len(sizes)
    order = tuple(reversed(range(count))) + tuple(range(count, value.ndim))
    return value.transpose(order).reshape((-1,) + shape)


def scatter_sum(value, axis, chains):
    index = lax.axis_index(axis)
    sizes = [size for _, size in chains]
    value = value.reshape(tuple(sizes) + value.shape[1:])
    for depth in reversed(range(len(chains))):
        stride, size = chains[depth]
        place = (index // stride) % size
        total = lax.dynamic_index_in_dim(value, place, depth, keepdims=False)
        for k in range(1, size):
            part = lax.dynamic_index_in_dim(value, place ^ k, depth, keepdims=False)
            total = total + swap(part.astype(BF16), axis, k * stride).astype(F32)
        value = total
    return value


def all_sum(value, axis):
    size = lax.axis_size(axis)
    mask = 1
    while mask < size:
        value = value + swap(value, axis, mask)
        mask *= 2
    return value


def standardize(values):
    centered = values - jnp.mean(values, axis=-1, keepdims=True)
    inverse = lax.rsqrt(jnp.mean(centered * centered, axis=-1, keepdims=True) + NORM_EPS)
    return (centered * inverse, inverse)


def shared_standardize(values, axis):
    count = values.shape[-1]
    mean = jnp.mean(values, axis=-1)
    centered = values - mean[:, None]
    squares = jnp.sum(centered * centered, axis=-1)
    both = jnp.stack([mean, squares])
    mask, held = 1, count
    while mask < lax.axis_size(axis):
        other = swap(both, axis, mask)
        gap = both[0] - other[0]
        both = jnp.stack([0.5 * (both[0] + other[0]), both[1] + other[1] + gap * gap * (0.5 * held)])
        mask *= 2
        held *= 2
    inverse = lax.rsqrt(both[1] / held + NORM_EPS)[:, None]
    return ((values - both[0][:, None]) * inverse, inverse)


def silu_slope(values):
    sigma = jax.nn.sigmoid(values)
    return sigma * (1.0 + values * (1.0 - sigma))


def depth_forward(padded, weights, seg_window, seg_centre, length):
    summed = jnp.zeros((length, padded.shape[1]), F32)
    for offset in range(weights.shape[0]):
        inside = (seg_window[offset : offset + length] == seg_centre)[:, None]
        summed = summed + jnp.where(
            inside, padded[offset : offset + length].astype(F32) * weights[offset][None, :], 0.0
        )
    return summed


def depth_backward(padded_grad, padded_in, weights, seg_window, seg_centre, length):
    taps = weights.shape[0]
    margin = (taps - 1) // 2
    grad_in = jnp.zeros((length, padded_grad.shape[1]), F32)
    grad_here = padded_grad[margin : margin + length].astype(F32)
    columns = []
    for offset in range(taps):
        start = 2 * margin - offset
        inside_back = (seg_window[start : start + length] == seg_centre)[:, None]
        grad_in = grad_in + jnp.where(
            inside_back,
            padded_grad[start : start + length].astype(F32) * weights[offset][None, :],
            0.0,
        )
        inside = (seg_window[offset : offset + length] == seg_centre)[:, None]
        columns.append(
            jnp.sum(
                jnp.where(inside, grad_here * padded_in[offset : offset + length].astype(F32), 0.0),
                axis=0,
            )
        )
    return (grad_in, jnp.stack(columns, axis=0))


def one_hot(rows, columns):
    return (rows[:, None] == columns[None, :]).astype(BF16)


def route_frames(mel_pieces, dest_owner, dest_slot, dp_count):
    pieces, piece_values = mel_pieces.shape
    capacity = max(2, 2 * pieces // dp_count)
    matches = (dest_owner[:, None] == jnp.arange(dp_count, dtype=jnp.int32)[None, :]).astype(jnp.int32)
    earlier = jnp.cumsum(matches, axis=0) - matches
    position = dest_owner * capacity + jnp.sum(earlier * matches, axis=1)
    pick = one_hot(jnp.arange(dp_count * capacity, dtype=jnp.int32), position)
    label = jnp.broadcast_to((dest_slot + 1).astype(BF16)[:, None], (pieces, 128))
    outgoing = jnp.dot(
        pick, jnp.concatenate([mel_pieces, label], axis=1), preferred_element_type=F32
    ).astype(BF16)
    arrived = lax.all_to_all(
        outgoing.reshape(dp_count, capacity, -1), "dp", split_axis=0, concat_axis=0, tiled=True
    ).reshape(dp_count * capacity, -1)
    labels = arrived[:, piece_values].astype(jnp.int32)
    put = one_hot(jnp.arange(1, pieces + 1, dtype=jnp.int32), labels)
    return jnp.dot(put, arrived[:, :piece_values], preferred_element_type=F32).astype(BF16)


def per_device(
    mel_pieces,
    dest_owner,
    dest_slot,
    segment_ids,
    out_grad,
    stem_weight,
    up_weight,
    down_weight,
    depth_kernel,
    gain_pre,
    gain_post,
):
    dp_count = lax.axis_size("dp")
    tm_count = lax.axis_size("tm")
    chains = stages_of({"dp": dp_count, "tm": tm_count})
    dp_chains, tm_chains = chains["dp"], chains["tm"]
    column = lax.axis_index("tm")
    taps = depth_kernel.shape[1]
    margin = (taps - 1) // 2
    block = out_grad.shape[1]
    channels = out_grad.shape[2]
    held = channels // tm_count
    rows = down_weight.shape[0]
    stem_rows = stem_weight.shape[0]
    features = stem_rows * dp_count * tm_count
    length = block * tm_count

    pieces = route_frames(mel_pieces[0], dest_owner[0], dest_slot[0], dp_count)
    frames = gather(pieces, "tm", tm_chains).reshape(length, features)

    gain_row = jnp.zeros((stem_rows, 128), BF16).at[0, :rows].set(gain_pre)
    stem_all = gather(jnp.concatenate([stem_weight, gain_row], axis=1), "dp", dp_chains)
    stem_all = gather(stem_all, "tm", tm_chains)
    stem_all = stem_all.transpose(1, 0, 2, 3)
    stem_full = stem_all[..., :channels].reshape(features, channels)
    gain_one = stem_all[:, :, 0, channels : channels + rows].reshape(channels).astype(F32)

    span = 128 * tm_count
    lane = jnp.arange(span, dtype=jnp.int32)
    grouped = (lane // rows) % tm_count * 128 + lane // (rows * tm_count) * rows + lane % rows
    regroup = one_hot(grouped, lane)
    groups = 2 * channels // span
    up_parts = jnp.dot(
        up_weight.reshape(rows, groups, span).transpose(1, 0, 2).reshape(groups * rows, span),
        regroup,
        preferred_element_type=F32,
    ).astype(BF16)
    up_parts = up_parts.reshape(groups, rows, tm_count, 128).transpose(2, 1, 0, 3)
    up_parts = up_parts.reshape(tm_count, rows, groups * 128)
    up_mine = lax.all_to_all(up_parts, "tm", split_axis=0, concat_axis=0, tiled=True)
    up_full = gather(up_mine.reshape(tm_count * rows, groups * 128), "dp", dp_chains)
    up_full = up_full.reshape(channels, 2 * held)

    small = jnp.concatenate(
        [depth_kernel, gain_post[:, None], jnp.zeros((rows, 128 - taps - 1), BF16)], axis=1
    )
    down_all = gather(jnp.concatenate([down_weight, small], axis=1), "dp", dp_chains)
    down_all = down_all.reshape(held, channels + 128)
    down_full = down_all[:, :channels]
    small_all = down_all[:, channels:].astype(F32).T
    taps_full = small_all[:taps]
    gain_two = small_all[taps][None, :]

    grad_out = out_grad[0]
    grad_out_all = gather(grad_out, "tm", tm_chains).reshape(length, channels)

    seg_centre = segment_ids[0]
    seg_window = jnp.pad(seg_centre, (margin, margin), constant_values=-1)

    stem_pre = jnp.dot(frames, stem_full, preferred_element_type=F32)
    stem_out = jax.nn.silu(stem_pre).astype(BF16)
    stem_hat, inverse_one = standardize(stem_out.astype(F32))
    normed = (stem_hat * gain_one).astype(BF16)
    proj = jnp.dot(normed, up_full, preferred_element_type=F32)
    linear = proj[:, :held]
    gate_sig = jax.nn.sigmoid(proj[:, held:])
    gated = (linear * gate_sig).astype(BF16)
    gated_ext = jnp.pad(gated, ((margin, margin), (0, 0)))
    conv = depth_forward(gated_ext, taps_full, seg_window, seg_centre, length)
    conv_hat, inverse_two = shared_standardize(conv, "tm")
    conv_scaled = conv_hat * gain_two
    activated = jax.nn.silu(conv_scaled).astype(BF16)
    y_terms = jnp.dot(activated, down_full, preferred_element_type=F32)
    y_part = scatter_sum(y_terms.reshape(tm_count, block, channels), "tm", tm_chains)

    def mine(value):
        return lax.dynamic_slice_in_dim(value, column * block, block, 0)

    y_out = (mine(stem_out).astype(F32) + y_part).astype(BF16)

    down_terms = jnp.dot(activated.T, grad_out_all, preferred_element_type=F32).astype(BF16)
    down_terms = down_terms.reshape(dp_count, rows, tm_count, held).transpose(0, 2, 1, 3)
    down_terms = down_terms.reshape(dp_count * tm_count, rows, held)
    down_terms = lax.all_to_all(down_terms, ("dp", "tm"), split_axis=0, concat_axis=0, tiled=True)
    grad_down = jnp.sum(
        down_terms.reshape(dp_count, tm_count * rows, held).astype(F32), axis=0
    )

    grad_act = lax.dot_general(
        grad_out_all, down_full, (((1,), (1,)), ((), ())), preferred_element_type=F32
    )
    grad_scaled = grad_act * silu_slope(conv_scaled)
    gain_post_term = jnp.sum(grad_scaled * conv_hat, axis=0)
    grad_hat = grad_scaled * gain_two
    means = all_sum(
        jnp.stack([jnp.sum(grad_hat, axis=-1), jnp.sum(grad_hat * conv_hat, axis=-1)]), "tm"
    ) * (1.0 / channels)
    grad_conv = (
        (grad_hat - means[0][:, None] - conv_hat * means[1][:, None]) * inverse_two
    ).astype(BF16)
    grad_ext = jnp.pad(grad_conv, ((margin, margin), (0, 0)))
    grad_gated, kernel_term = depth_backward(
        grad_ext, gated_ext, taps_full, seg_window, seg_centre, length
    )
    grad_proj = jnp.concatenate(
        [grad_gated * gate_sig, grad_gated * linear * gate_sig * (1.0 - gate_sig)], axis=1
    ).astype(BF16)

    up_terms = jnp.dot(normed.T, grad_proj, preferred_element_type=F32).astype(BF16)
    share = up_terms.shape[1] // tm_count
    up_terms = up_terms.reshape(dp_count, tm_count * rows, tm_count, share).transpose(0, 2, 1, 3)
    up_terms = up_terms.reshape(dp_count * tm_count, tm_count * rows, share)
    up_terms = lax.all_to_all(up_terms, ("dp", "tm"), split_axis=0, concat_axis=0, tiled=True)
    up_terms = up_terms.reshape(dp_count, tm_count, tm_count * rows, share)
    spread = one_hot(lane, grouped).reshape(tm_count, share, span)
    grad_up = jnp.einsum(
        "ijab,jbc->ac", up_terms, spread, preferred_element_type=F32
    )

    small_term = jnp.concatenate([kernel_term, gain_post_term[None, :]], axis=0)
    small_term = small_term.reshape(taps + 1, dp_count, rows).transpose(1, 2, 0)
    small_term = lax.all_to_all(small_term, "dp", split_axis=0, concat_axis=0, tiled=True)
    small_sum = jnp.sum(small_term, axis=0)
    grad_kernel, grad_gain_post = small_sum[:, :taps], small_sum[:, taps]

    normed_terms = lax.dot_general(
        grad_proj, up_full, (((1,), (1,)), ((), ())), preferred_element_type=F32
    )
    grad_normed = scatter_sum(normed_terms.reshape(tm_count, block, channels), "tm", tm_chains)
    my_hat = mine(stem_hat)
    gain_pre_term = jnp.sum(grad_normed * my_hat, axis=0).reshape(dp_count * tm_count, rows)
    gain_pre_term = lax.all_to_all(
        gain_pre_term, ("dp", "tm"), split_axis=0, concat_axis=0, tiled=True
    )
    grad_gain_pre = jnp.sum(gain_pre_term, axis=0)
    back = grad_normed * gain_one
    first = jnp.mean(back, axis=-1, keepdims=True)
    second = jnp.mean(back * my_hat, axis=-1, keepdims=True)
    grad_stem_out = grad_out.astype(F32) + (back - first - my_hat * second) * mine(inverse_one)
    grad_stem_pre = (grad_stem_out * silu_slope(mine(stem_pre))).astype(BF16)
    grad_stem_all = gather(grad_stem_pre, "tm", tm_chains).reshape(length, channels)
    chosen = jnp.arange(features // tm_count, dtype=jnp.int32)
    chosen = (chosen // stem_rows * tm_count + column) * stem_rows + chosen % stem_rows
    frames_part = jnp.dot(
        frames, one_hot(jnp.arange(features, dtype=jnp.int32), chosen), preferred_element_type=F32
    ).astype(BF16)
    stem_terms = jnp.dot(frames_part.T, grad_stem_all, preferred_element_type=F32).astype(BF16)
    stem_terms = lax.all_to_all(
        stem_terms.reshape(dp_count, stem_rows, channels),
        "dp",
        split_axis=0,
        concat_axis=0,
        tiled=True,
    )
    grad_stem = jnp.sum(stem_terms.astype(F32), axis=0)
    return (y_out[None], grad_stem, grad_up, grad_down, grad_kernel, grad_gain_pre, grad_gain_post)


def solution(mesh):
    return jax.shard_map(
        per_device,
        mesh=mesh,
        in_specs=(
            P("dp", "tm", None),
            P("dp", "tm"),
            P("dp", "tm"),
            P("dp", None),
            P("dp", "tm", None),
            P(("dp", "tm"), None),
            P(("dp", "tm"), None),
            P(("dp", "tm"), None),
            P(("dp", "tm"), None),
            P(("dp", "tm")),
            P(("dp", "tm")),
        ),
        out_specs=(
            P("dp", "tm", None),
            P(("dp", "tm"), None),
            P("dp", "tm"),
            P("dp", "tm"),
            P(("dp", "tm"), None),
            P(("dp", "tm")),
            P(("dp", "tm")),
        ),
        check_vma=False,
    )
```

```python
import jax
import jax.numpy as jnp
from jax import lax
from jax.experimental import pallas as pl
from jax.experimental.pallas import tpu as pltpu
from jax.sharding import PartitionSpec as P

NORM_EPS = 1e-05
BF16 = jnp.bfloat16
F32 = jnp.float32


def stages_of(sizes):
    if sizes["dp"] == 8 and sizes["tm"] == 4:
        return {"dp": ((2, 4), (1, 2)), "tm": ((2, 2), (1, 2))}
    if sizes["dp"] == 64 and sizes["tm"] == 4:
        return {"dp": ((8, 8), (2, 4), (1, 2)), "tm": ((1, 4),)}
    return {axis: ((1, size),) for axis, size in sizes.items()}


def swap(value, axis, mask):
    size = lax.axis_size(axis)
    return lax.ppermute(value, axis, [(i, i ^ mask) for i in range(size)])


VMEM_LIMIT = 48 << 20


def kernel_params():
    return pltpu.CompilerParams(vmem_limit_bytes=VMEM_LIMIT)


def costs(flops, moved):
    return pl.CostEstimate(flops=flops, bytes_accessed=moved, transcendentals=0)


def after(value, *others):
    return lax.optimization_barrier((value,) + others)[0]


def place_parts(parts, axis, stride, size, dim):
    shape = parts[0].shape
    out_shape = shape[:dim] + (size,) + shape[dim:]

    def kernel(*refs):
        place = (lax.axis_index(axis) // stride) % size
        for k in range(size):
            refs[size][(slice(None),) * dim + (place ^ k,)] = refs[k][...]

    return pl.pallas_call(
        kernel,
        out_shape=jax.ShapeDtypeStruct(out_shape, parts[0].dtype),
        compiler_params=kernel_params(),
        cost_estimate=pl.CostEstimate(
            flops=0, bytes_accessed=2 * size * parts[0].size * 2, transcendentals=0
        ),
    )(*parts)


def gather_stage(value, axis, stride, size, dim):
    parts = [value] + [swap(value, axis, k * stride) for k in range(1, size)]
    return place_parts(parts, axis, stride, size, dim)


def gather(value, axis, chains):
    shape = value.shape
    for dim, (stride, size) in enumerate(chains):
        value = gather_stage(value, axis, stride, size, dim)
    return value.reshape((-1,) + shape)


def block_terms(left, right, transposed, axis, count):
    block = left.shape[0] // count
    width = right.shape[0] if transposed else right.shape[1]
    dims = (((1,), (1 if transposed else 0,)), ((), ()))

    def kernel(left_ref, right_ref, own, others):
        place = lax.axis_index(axis)
        for k in range(count):
            start = pl.multiple_of((place ^ k) * block, block)
            term = lax.dot_general(
                left_ref[pl.ds(start, block), :], right_ref[...], dims, preferred_element_type=F32
            )
            if k == 0:
                own[...] = term
            else:
                others[k - 1] = term.astype(BF16)

    return pl.pallas_call(
        kernel,
        out_shape=(
            jax.ShapeDtypeStruct((block, width), F32),
            jax.ShapeDtypeStruct((count - 1, block, width), BF16),
        ),
        compiler_params=kernel_params(),
        cost_estimate=pl.CostEstimate(
            flops=2 * left.size * width,
            bytes_accessed=2 * (left.size + right.size) + 10 * block * width,
            transcendentals=0,
        ),
    )(left, right)


def block_sum(own, others, axis, chains):
    if list(chains) == [(2, 2), (1, 2)]:
        near = swap(others[0], axis, 1)
        passed = swap(others[2], axis, 1)
        far = swap((others[1].astype(F32) + passed.astype(F32)).astype(BF16), axis, 2)
        return own + near.astype(F32) + far.astype(F32)
    for k in range(others.shape[0]):
        own = own + swap(others[k], axis, k + 1).astype(F32)
    return own


def message_terms(left, right, parts, sides):
    rows, columns = left.shape[1] // parts, right.shape[1] // sides
    if rows % 16:
        terms = jnp.dot(left.T, right, preferred_element_type=F32).astype(BF16)
        terms = terms.reshape(parts, rows, sides, columns).transpose(0, 2, 1, 3)
        return terms.reshape(parts * sides, rows, columns)
    step = max(1, 128 // rows)

    def kernel(left_ref, right_ref, out):
        for i in range(0, parts, step):
            term = lax.dot_general(
                left_ref[:, i * rows : (i + step) * rows],
                right_ref[...],
                (((0,), (0,)), ((), ())),
                preferred_element_type=F32,
            ).astype(BF16)
            for k in range(step):
                for j in range(sides):
                    out[(i + k) * sides + j] = term[
                        k * rows : (k + 1) * rows, j * columns : (j + 1) * columns
                    ]

    return pl.pallas_call(
        kernel,
        out_shape=jax.ShapeDtypeStruct((parts * sides, rows, columns), BF16),
        compiler_params=kernel_params(),
        cost_estimate=pl.CostEstimate(
            flops=2 * left.size * right.shape[1],
            bytes_accessed=2 * (left.size + right.size + left.shape[1] * right.shape[1]),
            transcendentals=0,
        ),
    )(left, right)


def regroup_columns(weight, lane, grouped, axis, count):
    rows, columns = weight.shape
    span = lane.shape[0]
    groups = columns // span
    if rows % 16:
        parts = jnp.dot(
            weight.reshape(rows * groups, span), one_hot(grouped, lane), preferred_element_type=F32
        ).astype(BF16)
        parts = parts.reshape(rows, groups, count, 128).transpose(2, 0, 1, 3)
        parts = parts.reshape(count, rows, groups * 128)
        return [
            lax.dynamic_index_in_dim(parts, lax.axis_index(axis) ^ k, 0, keepdims=False)
            for k in range(count)
        ]
    small = rows

    def kernel(weight_ref, *outs):
        place = lax.axis_index(axis)
        at = lax.broadcasted_iota(jnp.int32, (span, 128), 0)
        to = lax.broadcasted_iota(jnp.int32, (span, 128), 1)
        for k in range(count):
            want = to // small * (small * count) + (place ^ k) * small + to % small
            pick = jnp.where(at == want, 1.0, 0.0).astype(BF16)
            for g in range(groups):
                outs[k][:, g * 128 : (g + 1) * 128] = jnp.dot(
                    weight_ref[:, g * span : (g + 1) * span], pick, preferred_element_type=F32
                ).astype(BF16)

    return pl.pallas_call(
        kernel,
        out_shape=[jax.ShapeDtypeStruct((rows, columns // count), BF16)] * count,
        cost_estimate=pl.CostEstimate(
            flops=2 * weight.size * span, bytes_accessed=4 * weight.size, transcendentals=0
        ),
    )(weight)


def stem_backward(grad_normed, stem_pre, grad_out, gain, extra):
    block, channels = grad_normed.shape

    def kernel(grad_ref, pre_ref, out_grad_ref, gain_ref, out):
        pre = pre_ref[...]
        sigma = jax.nn.sigmoid(pre)
        hat, inverse = standardize((pre * sigma).astype(BF16).astype(F32))
        grad = grad_ref[...]
        out[block:, :] = jnp.concatenate(
            [jnp.sum(grad * hat, axis=0, keepdims=True), jnp.zeros((extra - 1, channels), F32)]
        ).astype(BF16)
        back = grad * gain_ref[...]
        first = jnp.mean(back, axis=-1, keepdims=True)
        second = jnp.mean(back * hat, axis=-1, keepdims=True)
        stem_out = out_grad_ref[...].astype(F32) + (back - first - hat * second) * inverse
        out[:block, :] = (stem_out * (sigma * (1.0 + pre * (1.0 - sigma)))).astype(BF16)

    return pl.pallas_call(
        kernel,
        out_shape=jax.ShapeDtypeStruct((block + extra, channels), BF16),
        compiler_params=kernel_params(),
        cost_estimate=pl.CostEstimate(
            flops=30 * grad_normed.size, bytes_accessed=12 * grad_normed.size, transcendentals=0
        ),
    )(grad_normed, stem_pre, grad_out, gain)


def standardize(values):
    centered = values - jnp.mean(values, axis=-1, keepdims=True)
    inverse = lax.rsqrt(jnp.mean(centered * centered, axis=-1, keepdims=True) + NORM_EPS)
    return (centered * inverse, inverse)


def gather_parts(value, axis, chains):
    if list(chains) == [(2, 2), (1, 2)]:
        far = swap(value, axis, 2)
        return [value, swap(value, axis, 1), far, swap(far, axis, 1)]
    return [value] + [swap(value, axis, k) for k in range(1, lax.axis_size(axis))]


def swap_all(value, axis):
    return [value] + [swap(value, axis, k) for k in range(1, lax.axis_size(axis))]


def split_parts(parts, axis, stride, size, dim, cut):
    shape = parts[0].shape
    lead = shape[:dim] + (size,) + shape[dim:-2]
    rows = (cut, shape[-2] - cut)

    def kernel(*refs):
        place = (lax.axis_index(axis) // stride) % size
        for k in range(size):
            target = (slice(None),) * dim + (place ^ k,)
            refs[size][target] = refs[k][..., :cut, :]
            refs[size + 1][target] = refs[k][..., cut:, :]

    return pl.pallas_call(
        kernel,
        out_shape=[
            jax.ShapeDtypeStruct(lead + (count, shape[-1]), parts[0].dtype) for count in rows
        ],
        compiler_params=kernel_params(),
        cost_estimate=costs(0, 4 * size * parts[0].size),
    )(*parts)


def split_gather(value, axis, chains, cut):
    for dim, (stride, size) in enumerate(chains):
        parts = [value] + [swap(value, axis, k * stride) for k in range(1, size)]
        if dim == len(chains) - 1:
            upper, lower = split_parts(parts, axis, stride, size, dim, cut)
        else:
            value = place_parts(parts, axis, stride, size, dim)
    return (
        upper.reshape((-1,) + upper.shape[-2:]),
        lower.reshape((-1, lower.shape[-1])),
    )


def prepare(mel, owner, slot, stem, up, down, taps, gain_one, gain_two, dp_count, tm_count):
    pieces, values = mel.shape
    capacity = max(2, 2 * pieces // dp_count)
    slots = dp_count * capacity
    stem_rows, channels = stem.shape
    rows = down.shape[0]
    tap_count = taps.shape[1]
    span = 128 * tm_count
    groups = up.shape[1] // span

    def kernel(
        mel_ref, owner_ref, slot_ref, stem_ref, up_ref, down_ref, taps_ref, one_ref, two_ref,
        sent, pack, *up_parts
    ):
        def iota(shape, dim):
            return lax.broadcasted_iota(jnp.int32, shape, dim)

        def table(flags):
            return jnp.where(flags, 1.0, 0.0).astype(BF16)

        pack[:stem_rows, :channels] = stem_ref[...]
        pack[stem_rows:, :channels] = down_ref[...]
        lane = iota((rows, 128), 1)
        spread = table(lane % rows == iota((rows, 128), 0))
        gain = jnp.broadcast_to(one_ref[...].astype(F32), (stem_rows, rows)).astype(BF16)
        pack[:stem_rows, channels:] = jnp.dot(gain, spread, preferred_element_type=F32).astype(BF16)
        tap_lane = table(iota((tap_count, 128), 1) == iota((tap_count, 128), 0))
        square = iota((rows, rows), 0) == iota((rows, rows), 1)
        diagonal = jnp.where(
            square, jnp.broadcast_to(two_ref[...].astype(F32), (rows, rows)), 0.0
        ).astype(BF16)
        small = jnp.dot(taps_ref[...], tap_lane, preferred_element_type=F32)
        small = small + jnp.dot(diagonal, table(lane == tap_count), preferred_element_type=F32)
        pack[stem_rows:, channels:] = small.astype(BF16)

        place = lax.axis_index("tm")
        at = iota((span, 128), 0)
        to = iota((span, 128), 1)
        for k in range(tm_count):
            want = to // rows * (rows * tm_count) + (place ^ k) * rows + to % rows
            pick = table(at == want)
            for g in range(groups):
                up_parts[k][:, g * 128 : (g + 1) * 128] = jnp.dot(
                    up_ref[:, g * span : (g + 1) * span], pick, preferred_element_type=F32
                ).astype(BF16)

        owners = jnp.broadcast_to(owner_ref[...].astype(F32), (pieces, pieces))
        earlier = iota((pieces, pieces), 0) < iota((pieces, pieces), 1)
        same = jnp.where(owners.T == owners, jnp.where(earlier, 1.0, 0.0), 0.0)
        target = owners[:1] * float(capacity) + jnp.sum(same, axis=0, keepdims=True)
        target = jnp.broadcast_to(target, (slots, pieces)).astype(jnp.int32)
        chosen = target == iota((slots, pieces), 0)
        pick = table(chosen)
        sent[:, :values] = jnp.dot(pick, mel_ref[...], preferred_element_type=F32).astype(BF16)
        labels = jnp.broadcast_to(slot_ref[...].astype(F32) + 1.0, (slots, pieces))
        label = jnp.sum(jnp.where(chosen, labels, 0.0), axis=1, keepdims=True)
        sent[:, values:] = jnp.broadcast_to(label, (slots, 128)).astype(BF16)

    outs = pl.pallas_call(
        kernel,
        out_shape=[
            jax.ShapeDtypeStruct((slots, values + 128), BF16),
            jax.ShapeDtypeStruct((stem_rows + rows, channels + 128), BF16),
        ]
        + [jax.ShapeDtypeStruct((rows, up.shape[1] // tm_count), BF16)] * tm_count,
        compiler_params=kernel_params(),
        cost_estimate=costs(1 << 27, 2 << 20),
    )(
        mel, owner[None, :], slot[None, :], stem, up, down, taps, gain_one[None, :],
        gain_two[None, :],
    )
    return outs[0], outs[1], list(outs[2:])


def place_frames(arrived, pieces, features):
    slots, width = arrived.shape
    steps = (width - 128) // features

    def kernel(arrived_ref, out):
        labels = arrived_ref[:, steps * features :].astype(F32).T[:1]
        want = jnp.broadcast_to(labels, (pieces * steps, slots)).astype(jnp.int32)
        row = lax.broadcasted_iota(jnp.int32, (pieces * steps, slots), 0)
        total = jnp.zeros((pieces * steps, features), F32)
        for q in range(steps):
            put = jnp.where(row == (want - 1) * steps + q, 1.0, 0.0).astype(BF16)
            total = total + jnp.dot(
                put, arrived_ref[:, q * features : (q + 1) * features], preferred_element_type=F32
            )
        out[...] = total.astype(BF16)

    return pl.pallas_call(
        kernel,
        out_shape=jax.ShapeDtypeStruct((pieces * steps, features), BF16),
        compiler_params=kernel_params(),
        cost_estimate=costs(2 * arrived.size * pieces * steps, 4 * arrived.size),
    )(arrived)


def stem_forward(frames, stem_all, count, axis, rows):
    length = frames.shape[0]
    features, width = stem_all.shape
    channels = width - 128
    block = length // count
    stem_rows = features * rows // channels

    def kernel(frames_ref, stem_ref, normed, pre_own, gain_out):
        place = lax.axis_index(axis)
        beside = stem_ref[:, channels:].astype(F32)
        gains = []
        for g in range(channels // 128):
            row = lax.broadcasted_iota(jnp.int32, (features, 128), 0)
            lane = lax.broadcasted_iota(jnp.int32, (features, 128), 1) + g * 128
            gains.append(
                jnp.sum(
                    jnp.where(row == lane // rows * stem_rows, beside, 0.0), axis=0, keepdims=True
                )
            )
        gain_out[...] = jnp.concatenate(gains, axis=1)
        for b in range(count):
            pre = jnp.dot(
                frames_ref[b * block : (b + 1) * block, :],
                stem_ref[:, :channels],
                preferred_element_type=F32,
            )
            hat, _ = standardize((pre * jax.nn.sigmoid(pre)).astype(BF16).astype(F32))
            normed[b * block : (b + 1) * block, :] = (hat * gain_out[...]).astype(BF16)

            @pl.when(place == b)
            def _():
                pre_own[...] = pre

    return pl.pallas_call(
        kernel,
        out_shape=[
            jax.ShapeDtypeStruct((length, channels), BF16),
            jax.ShapeDtypeStruct((block, channels), F32),
            jax.ShapeDtypeStruct((1, channels), F32),
        ],
        compiler_params=kernel_params(),
        cost_estimate=costs(2 * frames.size * channels, 2 * stem_all.size + 4 * frames.size),
    )(frames, stem_all)


PAD = 16


def up_forward(normed, up):
    length = normed.shape[0]
    held = up.shape[1] // 2
    step = min(128, length)

    def kernel(normed_ref, up_ref, linear, gate, gated):
        edge = jnp.zeros((PAD, held), F32)
        gated[:PAD, :] = edge
        gated[PAD + length :, :] = edge
        for b in range(0, length, step):
            proj = jnp.dot(normed_ref[b : b + step, :], up_ref[...], preferred_element_type=F32)
            sigma = jax.nn.sigmoid(proj[:, held:])
            linear[b : b + step, :] = proj[:, :held]
            gate[b : b + step, :] = sigma
            gated[PAD + b : PAD + b + step, :] = (proj[:, :held] * sigma).astype(BF16).astype(F32)

    return pl.pallas_call(
        kernel,
        out_shape=[
            jax.ShapeDtypeStruct((length, held), F32),
            jax.ShapeDtypeStruct((length, held), F32),
            jax.ShapeDtypeStruct((length + 2 * PAD, held), F32),
        ],
        compiler_params=kernel_params(),
        cost_estimate=costs(4 * normed.size * held, 2 * normed.size + 2 * up.size),
    )(normed, up)


def columns_of(first, second):
    rows = first.shape[0]
    lane = lax.broadcasted_iota(jnp.int32, (rows, 128), 1)
    both = jnp.where(lane == 0, first, jnp.where(lane == 1, second, 0.0))
    return both.T[:8]


def rows_of(table):
    rows = table.shape[1]
    turned = jnp.concatenate([table, jnp.zeros((120, rows), F32)], axis=0).T
    return turned[:, :1], turned[:, 1:2]


TILE = 64


def conv_forward(gated, small, segments, taps):
    length, held = gated.shape[0] - 2 * PAD, gated.shape[1]
    margin = (taps - 1) // 2

    def kernel(gated_ref, small_ref, seg_ref, conv, stats, turned, gated_near, seg_near):
        turned[...] = small_ref[...].astype(F32).T

        def tile(t, carry):
            base = pl.multiple_of(t * TILE, TILE)
            gated_near[...] = gated_ref[pl.ds(base, TILE + 2 * PAD), :]
            seg_near[...] = seg_ref[pl.ds(base, TILE + 2 * PAD), :]
            centre = seg_near[PAD : PAD + TILE, :]
            sums = [jnp.zeros((TILE, 128), F32) for _ in range(held // 128)]
            for k in range(taps):
                shift = PAD + k - margin
                inside = seg_near[shift : shift + TILE, :] == centre
                for g in range(held // 128):
                    lanes = slice(g * 128, (g + 1) * 128)
                    value = gated_near[shift : shift + TILE, lanes]
                    sums[g] = sums[g] + jnp.where(inside, value, 0.0) * turned[k : k + 1, lanes]
            conv[pl.ds(base, TILE), :] = jnp.concatenate(sums, axis=1)
            return carry

        lax.fori_loop(0, length // TILE, tile, 0)
        value = conv[...]
        mean = jnp.mean(value, axis=-1, keepdims=True)
        centered = value - mean
        stats[...] = columns_of(mean, jnp.sum(centered * centered, axis=-1, keepdims=True))

    return pl.pallas_call(
        kernel,
        out_shape=[
            jax.ShapeDtypeStruct((length, held), F32),
            jax.ShapeDtypeStruct((8, length), F32),
            jax.ShapeDtypeStruct((128, held), F32),
        ],
        scratch_shapes=[
            pltpu.VMEM((TILE + 2 * PAD, held), F32),
            pltpu.VMEM((TILE + 2 * PAD, 128), jnp.int32),
        ],
        compiler_params=kernel_params(),
        cost_estimate=costs(4 * taps * gated.size, 8 * gated.size),
    )(gated, small, segments)


def activate(conv, stats, turned, grad_act, taps):
    length, held = conv.shape
    count = len(stats)

    def kernel(conv_ref, turned_ref, grad_ref, *refs):
        tables, (active, hat_out, grad_hat_out, inverse_out, sums, gain_term) = (
            refs[:count], refs[count:],
        )
        means = [table[0:1, :] for table in tables]
        mean = sum(means) * (1.0 / count)
        squares = sum(table[1:2, :] for table in tables)
        squares = squares + held * sum((one - mean) * (one - mean) for one in means)
        inverse = lax.rsqrt(squares * (1.0 / (held * count)) + NORM_EPS)
        both = jnp.concatenate([mean, inverse, jnp.zeros((6, length), F32)], axis=0)
        mean, inverse = rows_of(both)
        inverse_out[...] = jnp.broadcast_to(inverse, (length, 128))
        gain = turned_ref[taps : taps + 1, :]
        hat = (conv_ref[...] - mean) * inverse
        scaled = hat * gain
        sigma = jax.nn.sigmoid(scaled)
        active[...] = (scaled * sigma).astype(BF16)
        grad_scaled = grad_ref[...] * (sigma * (1.0 + scaled * (1.0 - sigma)))
        gain_term[...] = jnp.sum(grad_scaled * hat, axis=0, keepdims=True)
        grad_hat = grad_scaled * gain
        hat_out[...] = hat
        grad_hat_out[...] = grad_hat
        sums[...] = columns_of(
            jnp.sum(grad_hat, axis=-1, keepdims=True),
            jnp.sum(grad_hat * hat, axis=-1, keepdims=True),
        )

    return pl.pallas_call(
        kernel,
        out_shape=[
            jax.ShapeDtypeStruct((length, held), BF16),
            jax.ShapeDtypeStruct((length, held), F32),
            jax.ShapeDtypeStruct((length, held), F32),
            jax.ShapeDtypeStruct((length, 128), F32),
            jax.ShapeDtypeStruct((8, length), F32),
            jax.ShapeDtypeStruct((1, held), F32),
        ],
        compiler_params=kernel_params(),
        cost_estimate=costs(40 * conv.size, 20 * conv.size),
    )(conv, turned, grad_act, *stats)


def conv_backward(grad_hat, hat, inverse, sums, gated, segments, linear, gate, turned, taps, gain_term):
    length, held = hat.shape
    count = len(sums)
    margin = (taps - 1) // 2
    groups = held // 128

    def kernel(
        grad_ref, hat_ref, inverse_ref, gated_ref, seg_ref, linear_ref, gate_ref, turned_ref,
        gain_ref, *refs
    ):
        tables, (proj, terms), (grad_conv, partial, grad_near, gated_near, seg_near) = (
            refs[:count], refs[count : count + 2], refs[count + 2 :],
        )
        total = sum(table[...] for table in tables) * (1.0 / (held * count))
        first, second = rows_of(total)
        edge = jnp.zeros((PAD, held), F32)
        grad_conv[:PAD, :] = edge
        grad_conv[PAD + length :, :] = edge
        value = (grad_ref[...] - first - hat_ref[...] * second) * inverse_ref[:, :1]
        grad_conv[PAD : PAD + length, :] = value.astype(BF16).astype(F32)
        partial[...] = jnp.zeros_like(partial)

        def tile(t, carry):
            base = pl.multiple_of(t * TILE, TILE)
            grad_near[...] = grad_conv[pl.ds(base, TILE + 2 * PAD), :]
            gated_near[...] = gated_ref[pl.ds(base, TILE + 2 * PAD), :]
            seg_near[...] = seg_ref[pl.ds(base, TILE + 2 * PAD), :]
            centre = seg_near[PAD : PAD + TILE, :]
            lanes = [slice(g * 128, (g + 1) * 128) for g in range(groups)]
            here = [grad_near[PAD : PAD + TILE, lanes[g]] for g in range(groups)]
            back = [jnp.zeros((TILE, 128), F32) for _ in range(groups)]
            for k in range(taps):
                shift = PAD + k - margin
                inside = seg_near[shift : shift + TILE, :] == centre
                for g in range(groups):
                    near = grad_near[shift : shift + TILE, lanes[g]]
                    weight = turned_ref[taps - 1 - k : taps - k, lanes[g]]
                    back[g] = back[g] + jnp.where(inside, near, 0.0) * weight
                    source = gated_near[shift : shift + TILE, lanes[g]]
                    product = jnp.where(inside, source, 0.0) * here[g]
                    partial[k, :, lanes[g]] += jnp.sum(
                        product.reshape(TILE // 8, 8, 128), axis=0
                    )
            for g in range(groups):
                sigma = gate_ref[pl.ds(base, TILE), lanes[g]]
                part = back[g] * sigma
                proj[pl.ds(base, TILE), lanes[g]] = part.astype(BF16)
                far = slice(held + g * 128, held + (g + 1) * 128)
                proj[pl.ds(base, TILE), far] = (
                    part * linear_ref[pl.ds(base, TILE), lanes[g]] * (1.0 - sigma)
                ).astype(BF16)
            return carry

        lax.fori_loop(0, length // TILE, tile, 0)
        terms[:taps, :] = jnp.sum(partial[...], axis=1)
        terms[taps : taps + 1, :] = gain_ref[...]

    return pl.pallas_call(
        kernel,
        out_shape=[
            jax.ShapeDtypeStruct((length, 2 * held), BF16),
            jax.ShapeDtypeStruct((taps + 1, held), F32),
        ],
        scratch_shapes=[
            pltpu.VMEM((length + 2 * PAD, held), F32),
            pltpu.VMEM((taps, 8, held), F32),
            pltpu.VMEM((TILE + 2 * PAD, held), F32),
            pltpu.VMEM((TILE + 2 * PAD, held), F32),
            pltpu.VMEM((TILE + 2 * PAD, 128), jnp.int32),
        ],
        compiler_params=kernel_params(),
        cost_estimate=costs(8 * taps * hat.size, 24 * hat.size),
    )(grad_hat, hat, inverse, gated, segments, linear, gate, turned, gain_term, *sums)


def one_hot(rows, columns):
    return (rows[:, None] == columns[None, :]).astype(BF16)


def order_pieces(mel_pieces, dest_owner, dest_slot, dp_count):
    pieces, piece_values = mel_pieces.shape
    capacity = max(2, 2 * pieces // dp_count)
    matches = (dest_owner[:, None] == jnp.arange(dp_count, dtype=jnp.int32)[None, :]).astype(jnp.int32)
    earlier = jnp.cumsum(matches, axis=0) - matches
    position = dest_owner * capacity + jnp.sum(earlier * matches, axis=1)
    pick = one_hot(jnp.arange(dp_count * capacity, dtype=jnp.int32), position)
    label = jnp.broadcast_to((dest_slot + 1).astype(BF16)[:, None], (pieces, 128))
    return jnp.dot(
        pick, jnp.concatenate([mel_pieces, label], axis=1), preferred_element_type=F32
    ).astype(BF16)


def per_device(
    mel_pieces,
    dest_owner,
    dest_slot,
    segment_ids,
    out_grad,
    stem_weight,
    up_weight,
    down_weight,
    depth_kernel,
    gain_pre,
    gain_post,
):
    dp_count = lax.axis_size("dp")
    tm_count = lax.axis_size("tm")
    chains = stages_of({"dp": dp_count, "tm": tm_count})
    dp_chains, tm_chains = chains["dp"], chains["tm"]
    column = lax.axis_index("tm")
    taps = depth_kernel.shape[1]
    margin = (taps - 1) // 2
    block = out_grad.shape[1]
    channels = out_grad.shape[2]
    held = channels // tm_count
    rows = down_weight.shape[0]
    stem_rows = stem_weight.shape[0]
    features = stem_rows * dp_count * tm_count
    length = block * tm_count

    span = 128 * tm_count
    lane = jnp.arange(span, dtype=jnp.int32)
    grouped = (lane // rows) % tm_count * 128 + lane // (rows * tm_count) * rows + lane % rows
    if stem_rows % 16 == 0 and rows % 16 == 0:
        sent, pack, up_parts = prepare(
            mel_pieces[0], dest_owner[0], dest_slot[0], stem_weight, up_weight, down_weight,
            depth_kernel, gain_pre, gain_post, dp_count, tm_count,
        )
    else:
        sent = order_pieces(mel_pieces[0], dest_owner[0], dest_slot[0], dp_count)
        up_parts = regroup_columns(up_weight, lane, grouped, "tm", tm_count)
        beside = jnp.broadcast_to(jnp.tile(gain_pre, 128 // rows)[None, :], (stem_rows, 128))
        small = jnp.concatenate(
            [depth_kernel, gain_post[:, None], jnp.zeros((rows, 128 - taps - 1), BF16)], axis=1
        )
        pack = jnp.concatenate(
            [
                jnp.concatenate([stem_weight, beside], axis=1),
                jnp.concatenate([down_weight, small], axis=1),
            ]
        )

    up_parts = [up_parts[0]] + [swap(up_parts[k], "tm", k) for k in range(1, tm_count)]
    up_mine = place_parts(up_parts, "tm", 1, tm_count, 0)
    stem_mine, down_all = split_gather(pack, "dp", dp_chains, stem_rows)
    up_full = gather(up_mine.reshape(tm_count * rows, 2 * held), "dp", dp_chains)
    up_full = up_full.reshape(channels, 2 * held)
    down_full = down_all[:, :channels]
    small_all = down_all[:, channels:]
    stem_all = place_parts(gather_parts(stem_mine, "tm", tm_chains), "tm", 1, tm_count, 1)
    stem_all = stem_all.reshape(features, channels + 128)

    pieces = mel_pieces.shape[1]
    capacity = max(2, 2 * pieces // dp_count)
    arrived = lax.all_to_all(
        sent.reshape(dp_count, capacity, -1), "dp", split_axis=0, concat_axis=0, tiled=True
    ).reshape(dp_count * capacity, -1)
    frames = place_frames(arrived, pieces, features)
    frames = place_parts(gather_parts(frames, "tm", tm_chains), "tm", 1, tm_count, 0)
    frames = frames.reshape(length, features)
    grad_out = out_grad[0]
    grad_out_all = gather_parts(after(grad_out, stem_mine), "tm", tm_chains)
    grad_out_all = place_parts(grad_out_all, "tm", 1, tm_count, 0).reshape(length, channels)
    segments = jnp.pad(segment_ids[0], (PAD, PAD), constant_values=-1)
    segments = jnp.broadcast_to(segments[:, None], (length + 2 * PAD, 128))

    normed, stem_pre, gain_one = stem_forward(frames, stem_all, tm_count, "tm", rows)
    linear, gate_sig, gated = up_forward(normed, up_full)
    conv, stats, turned = conv_forward(gated, small_all, segments, taps)
    grad_act = lax.dot_general(
        grad_out_all, down_full, (((1,), (1,)), ((), ())), preferred_element_type=F32
    )
    activated, conv_hat, grad_hat, inverse, sums, gain_post_term = activate(
        conv, swap_all(stats, "tm"), turned, grad_act, taps
    )
    sums = swap_all(sums, "tm")
    late = after(activated, *sums[:2])
    down_terms = message_terms(late, grad_out_all, dp_count, tm_count)
    y_terms = block_terms(late, down_full, False, "tm", tm_count)
    down_sums = lax.all_to_all(down_terms, ("dp", "tm"), split_axis=0, concat_axis=0, tiled=True)

    grad_hat = after(grad_hat, down_terms, *y_terms)
    grad_proj, kernel_term = conv_backward(
        grad_hat, conv_hat, inverse, sums, gated, segments, linear, gate_sig, turned, taps,
        gain_post_term,
    )
    y_part = block_sum(*y_terms, "tm", tm_chains)

    normed_terms = block_terms(after(grad_proj, y_part), up_full, True, "tm", tm_count)
    grad_normed = block_sum(*normed_terms, "tm", tm_chains)
    up_terms = message_terms(
        after(normed, down_sums, *normed_terms), grad_proj, dp_count, tm_count
    )
    up_sums = lax.all_to_all(up_terms, ("dp", "tm"), split_axis=0, concat_axis=0, tiled=True)
    y_out = (jax.nn.silu(stem_pre).astype(BF16).astype(F32) + after(y_part, up_terms)).astype(BF16)
    grad_down = jnp.sum(
        after(down_sums, up_terms).reshape(dp_count, tm_count * rows, held).astype(F32), axis=0
    )

    extra = 16
    grad_stem_pre = stem_backward(
        grad_normed, stem_pre, grad_out, gain_one, extra
    )
    chosen = jnp.arange(features // tm_count, dtype=jnp.int32)
    chosen = (chosen // stem_rows * tm_count + column) * stem_rows + chosen % stem_rows
    frames_part = jnp.dot(
        frames, one_hot(jnp.arange(features, dtype=jnp.int32), chosen), preferred_element_type=F32
    ).astype(BF16)
    frames_part = frames_part.reshape(tm_count, block, features // tm_count)
    frames_part = jnp.pad(frames_part, ((0, 0), (0, extra), (0, extra)))
    frames_part = frames_part.at[:, block, features // tm_count].set(1)
    grad_stem_parts = gather_parts(grad_stem_pre, "tm", tm_chains)
    stem_sum = 0.0
    for k in range(tm_count):
        frames_k = lax.dynamic_index_in_dim(frames_part, column ^ k, 0, keepdims=False)
        stem_sum = stem_sum + jnp.dot(
            frames_k.T, grad_stem_parts[k], preferred_element_type=F32
        )
    small_term = kernel_term.reshape(taps + 1, dp_count, rows).transpose(1, 0, 2)
    small_term = small_term.reshape(dp_count, 1, (taps + 1) * rows).astype(BF16)
    small_term = jnp.pad(small_term, ((0, 0), (0, 0), (0, channels - (taps + 1) * rows)))
    gain_term = stem_sum[features // tm_count].astype(BF16).reshape(dp_count, 1, tm_count * rows)
    gain_term = jnp.pad(gain_term, ((0, 0), (0, 0), (0, channels - tm_count * rows)))
    stem_terms = stem_sum[: features // tm_count].astype(BF16)
    stem_terms = stem_terms.reshape(dp_count, stem_rows, channels)
    stem_terms = jnp.concatenate([stem_terms, small_term, gain_term], axis=1)
    stem_terms = after(stem_terms, up_sums)
    stem_sums = lax.all_to_all(stem_terms, "dp", split_axis=0, concat_axis=0, tiled=True)
    up_sums = up_sums.reshape(dp_count, tm_count, tm_count * rows, 128)
    spread = one_hot(lane, grouped).reshape(tm_count, 128, span)
    grad_up = jnp.einsum("ijab,jbc->ac", up_sums, spread, preferred_element_type=F32)
    stem_sums = jnp.sum(stem_sums.astype(F32), axis=0)
    grad_stem = stem_sums[:stem_rows]
    small_sum = stem_sums[stem_rows, : (taps + 1) * rows].reshape(taps + 1, rows)
    grad_kernel, grad_gain_post = small_sum[:taps].T, small_sum[taps]
    grad_gain_pre = lax.dynamic_slice_in_dim(stem_sums[stem_rows + 1], column * rows, rows, 0)
    return (y_out[None], grad_stem, grad_up, grad_down, grad_kernel, grad_gain_pre, grad_gain_post)


def solution(mesh):
    return jax.shard_map(
        per_device,
        mesh=mesh,
        in_specs=(
            P("dp", "tm", None),
            P("dp", "tm"),
            P("dp", "tm"),
            P("dp", None),
            P("dp", "tm", None),
            P(("dp", "tm"), None),
            P(("dp", "tm"), None),
            P(("dp", "tm"), None),
            P(("dp", "tm"), None),
            P(("dp", "tm")),
            P(("dp", "tm")),
        ),
        out_specs=(
            P("dp", "tm", None),
            P(("dp", "tm"), None),
            P("dp", "tm"),
            P("dp", "tm"),
            P(("dp", "tm"), None),
            P(("dp", "tm")),
            P(("dp", "tm")),
        ),
        check_vma=False,
    )
```

```python
import jax
import jax.numpy as jnp
from jax import lax
from jax.experimental import pallas as pl
from jax.experimental.pallas import tpu as pltpu
from jax.sharding import PartitionSpec as P

NORM_EPS = 1e-05
BF16 = jnp.bfloat16
F32 = jnp.float32


def stages_of(sizes):
    if sizes["dp"] == 8 and sizes["tm"] == 4:
        return {"dp": ((2, 4), (1, 2)), "tm": ((2, 2), (1, 2))}
    if sizes["dp"] == 64 and sizes["tm"] == 4:
        return {"dp": ((8, 8), (2, 4), (1, 2)), "tm": ((1, 4),)}
    return {axis: ((1, size),) for axis, size in sizes.items()}


def swap(value, axis, mask):
    size = lax.axis_size(axis)
    return lax.ppermute(value, axis, [(i, i ^ mask) for i in range(size)])


VMEM_LIMIT = 16 << 20


def kernel_params():
    return pltpu.CompilerParams(vmem_limit_bytes=VMEM_LIMIT)


def costs(flops, moved):
    return pl.CostEstimate(flops=flops, bytes_accessed=moved, transcendentals=0)


def after(value, *others):
    return lax.optimization_barrier((value,) + others)[0]


def place_parts(parts, axis, stride, size, dim):
    shape = parts[0].shape
    out_shape = shape[:dim] + (size,) + shape[dim:]

    def kernel(*refs):
        place = (lax.axis_index(axis) // stride) % size
        for k in range(size):
            refs[size][(slice(None),) * dim + (place ^ k,)] = refs[k][...]

    return pl.pallas_call(
        kernel,
        out_shape=jax.ShapeDtypeStruct(out_shape, parts[0].dtype),
        compiler_params=kernel_params(),
        cost_estimate=pl.CostEstimate(
            flops=0, bytes_accessed=2 * size * parts[0].size * 2, transcendentals=0
        ),
    )(*parts)


def gather_stage(value, axis, stride, size, dim):
    parts = [value] + [swap(value, axis, k * stride) for k in range(1, size)]
    return place_parts(parts, axis, stride, size, dim)


def gather_rest(value, axis, chains):
    shape = value.shape[1:]
    for dim, (stride, size) in enumerate(chains[1:], 1):
        value = gather_stage(value, axis, stride, size, dim)
    return value.reshape((-1,) + shape)


def block_terms(left, right, transposed, axis, count):
    block = left.shape[0] // count
    width = right.shape[0] if transposed else right.shape[1]
    dims = (((1,), (1 if transposed else 0,)), ((), ()))

    def kernel(left_ref, right_ref, own, *others):
        place = lax.axis_index(axis)
        for k in range(count):
            start = pl.multiple_of((place ^ k) * block, block)
            term = lax.dot_general(
                left_ref[pl.ds(start, block), :], right_ref[...], dims, preferred_element_type=F32
            )
            if k == 0:
                own[...] = term
            else:
                others[k - 1][...] = term.astype(BF16)

    return pl.pallas_call(
        kernel,
        out_shape=[jax.ShapeDtypeStruct((block, width), F32)]
        + [jax.ShapeDtypeStruct((block, width), BF16)] * (count - 1),
        compiler_params=kernel_params(),
        cost_estimate=pl.CostEstimate(
            flops=2 * left.size * width,
            bytes_accessed=2 * (left.size + right.size) + 10 * block * width,
            transcendentals=0,
        ),
    )(left, right)


def block_sum(others, axis, chains, first=None):
    if list(chains) == [(2, 2), (1, 2)]:
        near, passed = swap(others[0], axis, 1), swap(others[2], axis, 1)
        passed = add_pair(others[1], passed)
        if first is not None:
            passed = after(passed, first)
        return swap(passed, axis, 2), [near], passed
    parts = [swap(other, axis, k) for k, other in enumerate(others, 1)]
    return parts[-1], parts[:-1], others[-1]


def add_pair(one, other):
    def kernel(one_ref, other_ref, out):
        out[...] = (one_ref[...].astype(F32) + other_ref[...].astype(F32)).astype(BF16)

    return pl.pallas_call(
        kernel,
        out_shape=jax.ShapeDtypeStruct(one.shape, BF16),
        compiler_params=kernel_params(),
        cost_estimate=costs(one.size, 6 * one.size),
    )(one, other)


def finish_rows(stem_pre, own, parts):
    def kernel(pre_ref, own_ref, *refs):
        total = own_ref[...]
        for part in refs[:-1]:
            total = total + part[...].astype(F32)
        pre = pre_ref[...]
        stem_out = (pre * jax.nn.sigmoid(pre)).astype(BF16).astype(F32)
        refs[-1][...] = (stem_out + total).astype(BF16)

    return pl.pallas_call(
        kernel,
        out_shape=jax.ShapeDtypeStruct(own.shape, BF16),
        compiler_params=kernel_params(),
        cost_estimate=costs(8 * own.size, 14 * own.size),
    )(stem_pre, own, *parts)


def part_terms(left, right, axis, chains):
    total = lax.axis_size(axis)
    stride, size = chains[-1]
    rows, columns = left.shape[1] // total, right.shape[1]
    step = max(1, 128 // rows)

    def kernel(left_ref, right_ref, *outs):
        place = (lax.axis_index(axis) // stride) % size
        for i in range(0, total, step):
            term = lax.dot_general(
                left_ref[:, i * rows : (i + step) * rows],
                right_ref[...],
                (((0,), (0,)), ((), ())),
                preferred_element_type=F32,
            ).astype(BF16)
            for n in range(step):
                for k in range(size):

                    @pl.when((i + n) % size ^ place == k)
                    def _():
                        outs[k][(i + n) // size] = term[n * rows : (n + 1) * rows]

    return pl.pallas_call(
        kernel,
        out_shape=[jax.ShapeDtypeStruct((total // size, rows, columns), BF16)] * size,
        compiler_params=kernel_params(),
        cost_estimate=costs(
            2 * left.size * columns, 2 * (left.size + right.size + left.shape[1] * columns)
        ),
    )(left, right)


def add_parts(parts, axis, chain):
    stride, size = chain
    shape = (parts[0].shape[0] // size,) + parts[0].shape[1:]

    def kernel(*refs):
        place = (lax.axis_index(axis) // stride) % size
        for a in range(shape[0]):
            for k in range(size):
                at = a * size + (place ^ k)
                total = sum(part[at].astype(F32) for part in refs[: len(parts)])
                refs[len(parts) + k][a] = total.astype(BF16)

    return pl.pallas_call(
        kernel,
        out_shape=[jax.ShapeDtypeStruct(shape, BF16)] * size,
        compiler_params=kernel_params(),
        cost_estimate=costs(len(parts) * parts[0].size, 4 * len(parts) * parts[0].size),
    )(*parts)


def swap_parts(parts, axis, chain):
    stride, _ = chain
    return [parts[0]] + [swap(part, axis, k * stride) for k, part in enumerate(parts[1:], 1)]


def reduce_parts(parts, axis, chains):
    parts = swap_parts(parts, axis, chains[-1])
    for chain in reversed(chains[:-1]):
        parts = swap_parts(add_parts(parts, axis, chain), axis, chain)
    return parts


def cut_columns(parts, axis):
    count = lax.axis_size(axis)
    rows, columns = parts[0].shape[1:]
    share = columns // count

    def kernel(*refs):
        place = lax.axis_index(axis)
        total = sum(part[0].astype(F32) for part in refs[: len(parts)]).astype(BF16)
        for j in range(count):
            for k in range(count):

                @pl.when(place ^ j == k)
                def _():
                    refs[len(parts) + k][...] = total[:, j * share : (j + 1) * share]

    return pl.pallas_call(
        kernel,
        out_shape=[jax.ShapeDtypeStruct((rows, share), BF16)] * count,
        compiler_params=kernel_params(),
        cost_estimate=costs(len(parts) * parts[0].size, 4 * len(parts) * parts[0].size),
    )(*parts)


def stack_rows(parts, axis):
    count = len(parts)
    rows, columns = parts[0].shape

    def kernel(*refs):
        place = lax.axis_index(axis)
        for k in range(count):
            start = pl.multiple_of((place ^ k) * rows, rows)
            refs[count][pl.ds(start, rows), :] = refs[k][...].astype(F32)

    return pl.pallas_call(
        kernel,
        out_shape=jax.ShapeDtypeStruct((count * rows, columns), F32),
        compiler_params=kernel_params(),
        cost_estimate=costs(0, 6 * count * parts[0].size),
    )(*parts)


def mix_columns(parts, axis, small):
    count = len(parts)
    rows = parts[0].shape[0]
    span = 128 * count

    def kernel(*refs):
        place = lax.axis_index(axis)
        at = lax.broadcasted_iota(jnp.int32, (128, span), 0)
        to = lax.broadcasted_iota(jnp.int32, (128, span), 1)
        total = jnp.zeros((rows, span), F32)
        for k in range(count):
            want = at // small * (small * count) + (place ^ k) * small + at % small
            spread = jnp.where(to == want, 1.0, 0.0).astype(BF16)
            total = total + jnp.dot(refs[k][...], spread, preferred_element_type=F32)
        refs[count][...] = total

    return pl.pallas_call(
        kernel,
        out_shape=jax.ShapeDtypeStruct((rows, span), F32),
        compiler_params=kernel_params(),
        cost_estimate=costs(2 * rows * span * span, 8 * rows * span),
    )(*parts)


def message_terms(left, right, parts, sides):
    rows, columns = left.shape[1] // parts, right.shape[1] // sides
    if rows % 16:
        terms = jnp.dot(left.T, right, preferred_element_type=F32).astype(BF16)
        terms = terms.reshape(parts, rows, sides, columns).transpose(0, 2, 1, 3)
        return terms.reshape(parts * sides, rows, columns)
    step = max(1, 128 // rows)

    def kernel(left_ref, right_ref, out):
        for i in range(0, parts, step):
            term = lax.dot_general(
                left_ref[:, i * rows : (i + step) * rows],
                right_ref[...],
                (((0,), (0,)), ((), ())),
                preferred_element_type=F32,
            ).astype(BF16)
            for k in range(step):
                for j in range(sides):
                    out[(i + k) * sides + j] = term[
                        k * rows : (k + 1) * rows, j * columns : (j + 1) * columns
                    ]

    return pl.pallas_call(
        kernel,
        out_shape=jax.ShapeDtypeStruct((parts * sides, rows, columns), BF16),
        compiler_params=kernel_params(),
        cost_estimate=pl.CostEstimate(
            flops=2 * left.size * right.shape[1],
            bytes_accessed=2 * (left.size + right.size + left.shape[1] * right.shape[1]),
            transcendentals=0,
        ),
    )(left, right)


def regroup_columns(weight, lane, grouped, axis, count):
    rows, columns = weight.shape
    span = lane.shape[0]
    groups = columns // span
    if rows % 16:
        parts = jnp.dot(
            weight.reshape(rows * groups, span), one_hot(grouped, lane), preferred_element_type=F32
        ).astype(BF16)
        parts = parts.reshape(rows, groups, count, 128).transpose(2, 0, 1, 3)
        parts = parts.reshape(count, rows, groups * 128)
        return [
            lax.dynamic_index_in_dim(parts, lax.axis_index(axis) ^ k, 0, keepdims=False)
            for k in range(count)
        ]
    small = rows

    def kernel(weight_ref, *outs):
        place = lax.axis_index(axis)
        at = lax.broadcasted_iota(jnp.int32, (span, 128), 0)
        to = lax.broadcasted_iota(jnp.int32, (span, 128), 1)
        for k in range(count):
            want = to // small * (small * count) + (place ^ k) * small + to % small
            pick = jnp.where(at == want, 1.0, 0.0).astype(BF16)
            for g in range(groups):
                outs[k][:, g * 128 : (g + 1) * 128] = jnp.dot(
                    weight_ref[:, g * span : (g + 1) * span], pick, preferred_element_type=F32
                ).astype(BF16)

    return pl.pallas_call(
        kernel,
        out_shape=[jax.ShapeDtypeStruct((rows, columns // count), BF16)] * count,
        cost_estimate=pl.CostEstimate(
            flops=2 * weight.size * span, bytes_accessed=4 * weight.size, transcendentals=0
        ),
    )(weight)


def stem_backward(own, parts, stem_pre, grad_out, gain, extra):
    block, channels = own.shape

    def kernel(own_ref, pre_ref, out_grad_ref, gain_ref, *refs):
        out = refs[-1]
        pre = pre_ref[...]
        sigma = jax.nn.sigmoid(pre)
        hat, inverse = standardize((pre * sigma).astype(BF16).astype(F32))
        grad = own_ref[...]
        for part in refs[:-1]:
            grad = grad + part[...].astype(F32)
        out[block:, :] = jnp.concatenate(
            [jnp.sum(grad * hat, axis=0, keepdims=True), jnp.zeros((extra - 1, channels), F32)]
        ).astype(BF16)
        back = grad * gain_ref[...]
        first = jnp.mean(back, axis=-1, keepdims=True)
        second = jnp.mean(back * hat, axis=-1, keepdims=True)
        stem_out = out_grad_ref[...].astype(F32) + (back - first - hat * second) * inverse
        out[:block, :] = (stem_out * (sigma * (1.0 + pre * (1.0 - sigma)))).astype(BF16)

    return pl.pallas_call(
        kernel,
        out_shape=jax.ShapeDtypeStruct((block + extra, channels), BF16),
        compiler_params=kernel_params(),
        cost_estimate=pl.CostEstimate(
            flops=30 * own.size, bytes_accessed=14 * own.size, transcendentals=0
        ),
    )(own, stem_pre, grad_out, gain, *parts)


def standardize(values):
    centered = values - jnp.mean(values, axis=-1, keepdims=True)
    inverse = lax.rsqrt(jnp.mean(centered * centered, axis=-1, keepdims=True) + NORM_EPS)
    return (centered * inverse, inverse)


def gather_parts(value, axis, chains):
    if list(chains) == [(2, 2), (1, 2)]:
        far = swap(value, axis, 2)
        return [value, swap(value, axis, 1), far, swap(far, axis, 1)]
    return [value] + [swap(value, axis, k) for k in range(1, lax.axis_size(axis))]


def swap_all(value, axis):
    return [value] + [swap(value, axis, k) for k in range(1, lax.axis_size(axis))]


def split_parts(parts, axis, stride, size, dim, cut):
    shape = parts[0].shape
    lead = shape[:dim] + (size,) + shape[dim:-2]
    rows, width = shape[-2:]
    chunks = (width - cut) // 128

    def kernel(*refs):
        place = (lax.axis_index(axis) // stride) % size
        for k in range(size):
            target = (slice(None),) * dim + (place ^ k,)
            refs[size][target] = refs[k][..., :cut]
            for q in range(chunks):
                inner = (slice(None),) * (len(lead) - dim - 1) + (q,)
                lanes = slice(cut + q * 128, cut + (q + 1) * 128)
                refs[size + 1][target + inner] = refs[k][..., lanes]

    return pl.pallas_call(
        kernel,
        out_shape=[
            jax.ShapeDtypeStruct(lead + (rows, cut), parts[0].dtype),
            jax.ShapeDtypeStruct(lead + (chunks, rows, 128), parts[0].dtype),
        ],
        compiler_params=kernel_params(),
        cost_estimate=costs(0, 4 * size * parts[0].size),
    )(*parts)


def split_gather(value, axis, chains, cut):
    for dim, (stride, size) in enumerate(chains):
        parts = [value] + [swap(value, axis, k * stride) for k in range(1, size)]
        if dim == len(chains) - 1:
            left, beyond = split_parts(parts, axis, stride, size, dim, cut)
        else:
            value = place_parts(parts, axis, stride, size, dim)
    return left.reshape((-1,) + left.shape[-2:]), beyond.reshape(-1, 128)


def prepare(mel, owner, slot, stem, up, taps, gain_one, gain_two, dp_count, tm_count):
    pieces, values = mel.shape
    capacity = max(2, 2 * pieces // dp_count)
    slots = dp_count * capacity
    stem_rows, channels = stem.shape
    rows, tap_count = taps.shape
    chunks = rows // stem_rows
    span = 128 * tm_count
    groups = up.shape[1] // span
    inputs = (
        up, stem, taps, gain_one[None, :], gain_two[None, :], owner[None, :], slot[None, :], mel
    )
    count = len(inputs)

    def kernel(*refs):
        sent, pack, *up_parts = refs[count : count + 2 + tm_count]
        held = refs[count + 2 + tm_count : -1]
        copies = [
            pltpu.make_async_copy(refs[k], held[k], refs[-1].at[k]) for k in range(count)
        ]
        for copy in copies:
            copy.start()
        up_ref, stem_ref, taps_ref, one_ref, two_ref, owner_ref, slot_ref, mel_ref = held

        def iota(shape, dim):
            return lax.broadcasted_iota(jnp.int32, shape, dim)

        def table(flags):
            return jnp.where(flags, 1.0, 0.0).astype(BF16)

        for copy in copies:
            copy.wait()
        pack[:, :channels] = stem_ref[...]
        lane = iota((rows, 128), 1)
        spread = table(lane % rows == iota((rows, 128), 0))
        gain = jnp.broadcast_to(one_ref[...].astype(F32), (stem_rows, rows)).astype(BF16)
        pack[:, channels : channels + 128] = jnp.dot(
            gain, spread, preferred_element_type=F32
        ).astype(BF16)
        tap_lane = table(iota((tap_count, 128), 1) == iota((tap_count, 128), 0))
        square = iota((rows, rows), 0) == iota((rows, rows), 1)
        diagonal = jnp.where(
            square, jnp.broadcast_to(two_ref[...].astype(F32), (rows, rows)), 0.0
        ).astype(BF16)
        small = jnp.dot(taps_ref[...], tap_lane, preferred_element_type=F32)
        small = small + jnp.dot(diagonal, table(lane == tap_count), preferred_element_type=F32)
        for q in range(chunks):
            lanes = slice(channels + 128 * (q + 1), channels + 128 * (q + 2))
            pack[:, lanes] = small[q * stem_rows : (q + 1) * stem_rows].astype(BF16)

        place = lax.axis_index("tm")
        at = iota((span, 128), 0)
        to = iota((span, 128), 1)
        for k in range(tm_count):
            want = to // rows * (rows * tm_count) + (place ^ k) * rows + to % rows
            pick = table(at == want)
            for g in range(groups):
                up_parts[k][:, g * 128 : (g + 1) * 128] = jnp.dot(
                    up_ref[:, g * span : (g + 1) * span], pick, preferred_element_type=F32
                ).astype(BF16)

        owners = jnp.broadcast_to(owner_ref[...].astype(F32), (pieces, pieces))
        earlier = iota((pieces, pieces), 0) < iota((pieces, pieces), 1)
        same = jnp.where(owners.T == owners, jnp.where(earlier, 1.0, 0.0), 0.0)
        target = owners[:1] * float(capacity) + jnp.sum(same, axis=0, keepdims=True)
        target = jnp.broadcast_to(target, (slots, pieces)).astype(jnp.int32)
        chosen = target == iota((slots, pieces), 0)
        pick = table(chosen)
        sent[:, :values] = jnp.dot(pick, mel_ref[...], preferred_element_type=F32).astype(BF16)
        labels = jnp.broadcast_to(slot_ref[...].astype(F32) + 1.0, (slots, pieces))
        label = jnp.sum(jnp.where(chosen, labels, 0.0), axis=1, keepdims=True)
        sent[:, values:] = jnp.broadcast_to(label, (slots, 128)).astype(BF16)

    outs = pl.pallas_call(
        kernel,
        out_shape=[
            jax.ShapeDtypeStruct((slots, values + 128), BF16),
            jax.ShapeDtypeStruct((stem_rows, channels + 128 * (chunks + 1)), BF16),
        ]
        + [jax.ShapeDtypeStruct((rows, up.shape[1] // tm_count), BF16)] * tm_count,
        in_specs=[pl.BlockSpec(memory_space=pl.ANY)] * count,
        scratch_shapes=[pltpu.VMEM(value.shape, value.dtype) for value in inputs]
        + [pltpu.SemaphoreType.DMA((count,))],
        cost_estimate=costs(1 << 27, 2 << 20),
    )(*inputs)
    return outs[0], outs[1], list(outs[2:])


def place_frames(arrived, pieces, features):
    slots, width = arrived.shape
    steps = (width - 128) // features

    def kernel(arrived_ref, out):
        labels = arrived_ref[:, steps * features :].astype(F32).T[:1]
        want = jnp.broadcast_to(labels, (pieces * steps, slots)).astype(jnp.int32)
        row = lax.broadcasted_iota(jnp.int32, (pieces * steps, slots), 0)
        total = jnp.zeros((pieces * steps, features), F32)
        for q in range(steps):
            put = jnp.where(row == (want - 1) * steps + q, 1.0, 0.0).astype(BF16)
            total = total + jnp.dot(
                put, arrived_ref[:, q * features : (q + 1) * features], preferred_element_type=F32
            )
        out[...] = total.astype(BF16)

    return pl.pallas_call(
        kernel,
        out_shape=jax.ShapeDtypeStruct((pieces * steps, features), BF16),
        compiler_params=kernel_params(),
        cost_estimate=costs(2 * arrived.size * pieces * steps, 4 * arrived.size),
    )(arrived)


def stem_forward(frames, stem_all, count, axis, rows, extra):
    length = frames.shape[0]
    features, width = stem_all.shape
    channels = width - 128
    block = length // count
    stem_rows = features * rows // channels
    share = features // count

    def kernel(frames_ref, stem_ref, normed, pre_own, gain_out, turned):
        place = lax.axis_index(axis)
        feature = lax.broadcasted_iota(jnp.int32, (features, share), 0)
        chosen = lax.broadcasted_iota(jnp.int32, (features, share), 1)
        chosen = (chosen // stem_rows * count + place) * stem_rows + chosen % stem_rows
        pick = jnp.where(feature == chosen, 1.0, 0.0).astype(BF16)
        corner = lax.broadcasted_iota(jnp.int32, (extra, extra), 0)
        corner = corner + lax.broadcasted_iota(jnp.int32, (extra, extra), 1)
        corner = jnp.where(corner == 0, 1.0, 0.0).astype(BF16)
        for k in range(count):
            start = pl.multiple_of((place ^ k) * block, block)
            turned[k, :share, :block] = lax.dot_general(
                pick,
                frames_ref[pl.ds(start, block), :],
                (((0,), (1,)), ((), ())),
                preferred_element_type=F32,
            ).astype(BF16)
            turned[k, share:, :block] = jnp.zeros((extra, block), BF16)
            turned[k, :share, block:] = jnp.zeros((share, extra), BF16)
            turned[k, share:, block:] = corner
        beside = stem_ref[:, channels:].astype(F32)
        gains = []
        for g in range(channels // 128):
            row = lax.broadcasted_iota(jnp.int32, (features, 128), 0)
            lane = lax.broadcasted_iota(jnp.int32, (features, 128), 1) + g * 128
            gains.append(
                jnp.sum(
                    jnp.where(row == lane // rows * stem_rows, beside, 0.0), axis=0, keepdims=True
                )
            )
        gain_out[...] = jnp.concatenate(gains, axis=1)
        for b in range(count):
            pre = jnp.dot(
                frames_ref[b * block : (b + 1) * block, :],
                stem_ref[:, :channels],
                preferred_element_type=F32,
            )
            hat, _ = standardize((pre * jax.nn.sigmoid(pre)).astype(BF16).astype(F32))
            normed[b * block : (b + 1) * block, :] = (hat * gain_out[...]).astype(BF16)

            @pl.when(place == b)
            def _():
                pre_own[...] = pre

    return pl.pallas_call(
        kernel,
        out_shape=[
            jax.ShapeDtypeStruct((length, channels), BF16),
            jax.ShapeDtypeStruct((block, channels), F32),
            jax.ShapeDtypeStruct((1, channels), F32),
            jax.ShapeDtypeStruct((count, share + extra, block + extra), BF16),
        ],
        compiler_params=kernel_params(),
        cost_estimate=costs(2 * frames.size * channels, 2 * stem_all.size + 4 * frames.size),
    )(frames, stem_all)


PAD = 16


def up_forward(normed, up):
    length = normed.shape[0]
    held = up.shape[1] // 2
    step = min(128, length)

    def kernel(normed_ref, up_ref, linear, gate, gated):
        edge = jnp.zeros((PAD, held), F32)
        gated[:PAD, :] = edge
        gated[PAD + length :, :] = edge
        for b in range(0, length, step):
            proj = jnp.dot(normed_ref[b : b + step, :], up_ref[...], preferred_element_type=F32)
            sigma = jax.nn.sigmoid(proj[:, held:])
            linear[b : b + step, :] = proj[:, :held]
            gate[b : b + step, :] = sigma
            gated[PAD + b : PAD + b + step, :] = (proj[:, :held] * sigma).astype(BF16).astype(F32)

    return pl.pallas_call(
        kernel,
        out_shape=[
            jax.ShapeDtypeStruct((length, held), F32),
            jax.ShapeDtypeStruct((length, held), F32),
            jax.ShapeDtypeStruct((length + 2 * PAD, held), F32),
        ],
        compiler_params=kernel_params(),
        cost_estimate=costs(4 * normed.size * held, 2 * normed.size + 2 * up.size),
    )(normed, up)


def columns_of(first, second):
    rows = first.shape[0]
    lane = lax.broadcasted_iota(jnp.int32, (rows, 128), 1)
    both = jnp.where(lane == 0, first, jnp.where(lane == 1, second, 0.0))
    return both.T[:8]


def rows_of(table):
    rows = table.shape[1]
    turned = jnp.concatenate([table, jnp.zeros((120, rows), F32)], axis=0).T
    return turned[:, :1], turned[:, 1:2]


TILE = 64


def conv_forward(gated, small, segments, taps):
    length, held = gated.shape[0] - 2 * PAD, gated.shape[1]
    margin = (taps - 1) // 2

    def kernel(gated_ref, small_ref, seg_ref, conv, stats, turned, gated_near, seg_near):
        turned[...] = small_ref[...].astype(F32).T

        def tile(t, carry):
            base = pl.multiple_of(t * TILE, TILE)
            gated_near[...] = gated_ref[pl.ds(base, TILE + 2 * PAD), :]
            seg_near[...] = seg_ref[pl.ds(base, TILE + 2 * PAD), :]
            centre = seg_near[PAD : PAD + TILE, :]
            sums = [jnp.zeros((TILE, 128), F32) for _ in range(held // 128)]
            for k in range(taps):
                shift = PAD + k - margin
                inside = seg_near[shift : shift + TILE, :] == centre
                for g in range(held // 128):
                    lanes = slice(g * 128, (g + 1) * 128)
                    value = gated_near[shift : shift + TILE, lanes]
                    sums[g] = sums[g] + jnp.where(inside, value, 0.0) * turned[k : k + 1, lanes]
            conv[pl.ds(base, TILE), :] = jnp.concatenate(sums, axis=1)
            return carry

        lax.fori_loop(0, length // TILE, tile, 0)
        value = conv[...]
        mean = jnp.mean(value, axis=-1, keepdims=True)
        centered = value - mean
        stats[...] = columns_of(mean, jnp.sum(centered * centered, axis=-1, keepdims=True))

    return pl.pallas_call(
        kernel,
        out_shape=[
            jax.ShapeDtypeStruct((length, held), F32),
            jax.ShapeDtypeStruct((8, length), F32),
            jax.ShapeDtypeStruct((128, held), F32),
        ],
        scratch_shapes=[
            pltpu.VMEM((TILE + 2 * PAD, held), F32),
            pltpu.VMEM((TILE + 2 * PAD, 128), jnp.int32),
        ],
        compiler_params=kernel_params(),
        cost_estimate=costs(4 * taps * gated.size, 8 * gated.size),
    )(gated, small, segments)


def activate(conv, stats, turned, grad_act, taps):
    length, held = conv.shape
    count = len(stats)

    def kernel(conv_ref, turned_ref, grad_ref, *refs):
        tables, (active, hat_out, grad_hat_out, inverse_out, sums, gain_term) = (
            refs[:count], refs[count:],
        )
        means = [table[0:1, :] for table in tables]
        mean = sum(means) * (1.0 / count)
        squares = sum(table[1:2, :] for table in tables)
        squares = squares + held * sum((one - mean) * (one - mean) for one in means)
        inverse = lax.rsqrt(squares * (1.0 / (held * count)) + NORM_EPS)
        both = jnp.concatenate([mean, inverse, jnp.zeros((6, length), F32)], axis=0)
        mean, inverse = rows_of(both)
        inverse_out[...] = jnp.broadcast_to(inverse, (length, 128))
        gain = turned_ref[taps : taps + 1, :]
        hat = (conv_ref[...] - mean) * inverse
        scaled = hat * gain
        sigma = jax.nn.sigmoid(scaled)
        active[...] = (scaled * sigma).astype(BF16)
        grad_scaled = grad_ref[...] * (sigma * (1.0 + scaled * (1.0 - sigma)))
        gain_term[...] = jnp.sum(grad_scaled * hat, axis=0, keepdims=True)
        grad_hat = grad_scaled * gain
        hat_out[...] = hat
        grad_hat_out[...] = grad_hat
        sums[...] = columns_of(
            jnp.sum(grad_hat, axis=-1, keepdims=True),
            jnp.sum(grad_hat * hat, axis=-1, keepdims=True),
        )

    return pl.pallas_call(
        kernel,
        out_shape=[
            jax.ShapeDtypeStruct((length, held), BF16),
            jax.ShapeDtypeStruct((length, held), F32),
            jax.ShapeDtypeStruct((length, held), F32),
            jax.ShapeDtypeStruct((length, 128), F32),
            jax.ShapeDtypeStruct((8, length), F32),
            jax.ShapeDtypeStruct((1, held), F32),
        ],
        compiler_params=kernel_params(),
        cost_estimate=costs(40 * conv.size, 20 * conv.size),
    )(conv, turned, grad_act, *stats)


def conv_backward(grad_hat, hat, inverse, sums, gated, segments, linear, gate, turned, taps, gain_term):
    length, held = hat.shape
    count = len(sums)
    margin = (taps - 1) // 2
    groups = held // 128

    def kernel(
        grad_ref, hat_ref, inverse_ref, gated_ref, seg_ref, linear_ref, gate_ref, turned_ref,
        gain_ref, *refs
    ):
        tables, (proj, terms), (grad_conv, partial, grad_near, gated_near, seg_near) = (
            refs[:count], refs[count : count + 2], refs[count + 2 :],
        )
        total = sum(table[...] for table in tables) * (1.0 / (held * count))
        first, second = rows_of(total)
        edge = jnp.zeros((PAD, held), F32)
        grad_conv[:PAD, :] = edge
        grad_conv[PAD + length :, :] = edge
        value = (grad_ref[...] - first - hat_ref[...] * second) * inverse_ref[:, :1]
        grad_conv[PAD : PAD + length, :] = value.astype(BF16).astype(F32)
        partial[...] = jnp.zeros_like(partial)

        def tile(t, carry):
            base = pl.multiple_of(t * TILE, TILE)
            grad_near[...] = grad_conv[pl.ds(base, TILE + 2 * PAD), :]
            gated_near[...] = gated_ref[pl.ds(base, TILE + 2 * PAD), :]
            seg_near[...] = seg_ref[pl.ds(base, TILE + 2 * PAD), :]
            centre = seg_near[PAD : PAD + TILE, :]
            lanes = [slice(g * 128, (g + 1) * 128) for g in range(groups)]
            here = [grad_near[PAD : PAD + TILE, lanes[g]] for g in range(groups)]
            back = [jnp.zeros((TILE, 128), F32) for _ in range(groups)]
            for k in range(taps):
                shift = PAD + k - margin
                inside = seg_near[shift : shift + TILE, :] == centre
                for g in range(groups):
                    near = grad_near[shift : shift + TILE, lanes[g]]
                    weight = turned_ref[taps - 1 - k : taps - k, lanes[g]]
                    back[g] = back[g] + jnp.where(inside, near, 0.0) * weight
                    source = gated_near[shift : shift + TILE, lanes[g]]
                    product = jnp.where(inside, source, 0.0) * here[g]
                    partial[k, :, lanes[g]] += jnp.sum(
                        product.reshape(TILE // 8, 8, 128), axis=0
                    )
            for g in range(groups):
                sigma = gate_ref[pl.ds(base, TILE), lanes[g]]
                part = back[g] * sigma
                proj[pl.ds(base, TILE), lanes[g]] = part.astype(BF16)
                far = slice(held + g * 128, held + (g + 1) * 128)
                proj[pl.ds(base, TILE), far] = (
                    part * linear_ref[pl.ds(base, TILE), lanes[g]] * (1.0 - sigma)
                ).astype(BF16)
            return carry

        lax.fori_loop(0, length // TILE, tile, 0)
        terms[:taps, :] = jnp.sum(partial[...], axis=1)
        terms[taps : taps + 1, :] = gain_ref[...]

    return pl.pallas_call(
        kernel,
        out_shape=[
            jax.ShapeDtypeStruct((length, 2 * held), BF16),
            jax.ShapeDtypeStruct((taps + 1, held), F32),
        ],
        scratch_shapes=[
            pltpu.VMEM((length + 2 * PAD, held), F32),
            pltpu.VMEM((taps, 8, held), F32),
            pltpu.VMEM((TILE + 2 * PAD, held), F32),
            pltpu.VMEM((TILE + 2 * PAD, held), F32),
            pltpu.VMEM((TILE + 2 * PAD, 128), jnp.int32),
        ],
        compiler_params=kernel_params(),
        cost_estimate=costs(8 * taps * hat.size, 24 * hat.size),
    )(grad_hat, hat, inverse, gated, segments, linear, gate, turned, gain_term, *sums)


def stem_message(turned, parts, small, axis, chains, stem_rows):
    dp_count = lax.axis_size(axis)
    stride, size = chains[-1]
    count, share, width = turned.shape
    channels = parts[0].shape[1]
    rows = dp_count * stem_rows
    own = channels // dp_count
    height = stem_rows + 8

    def kernel(turned_ref, small_ref, *refs):
        outs = refs[count:]
        place = (lax.axis_index(axis) // stride) % size
        total = jnp.zeros((share, channels), F32)
        for k in range(count):
            total = total + jnp.dot(turned_ref[k], refs[k][...], preferred_element_type=F32)
        for i in range(dp_count):
            gain = jnp.concatenate(
                [total[rows : rows + 1, i * own : (i + 1) * own], jnp.zeros((1, channels - own), F32)],
                axis=1,
            )
            block = jnp.concatenate(
                [
                    total[i * stem_rows : (i + 1) * stem_rows],
                    small_ref[i : i + 1, :],
                    gain,
                    jnp.zeros((6, channels), F32),
                ],
                axis=0,
            ).astype(BF16)
            for k in range(size):

                @pl.when(i % size ^ place == k)
                def _():
                    outs[k][i // size] = block

    return pl.pallas_call(
        kernel,
        out_shape=[jax.ShapeDtypeStruct((dp_count // size, height, channels), BF16)] * size,
        compiler_params=kernel_params(),
        cost_estimate=costs(2 * turned.size * channels, 4 * count * width * channels),
    )(turned, small, *parts)


def stem_finish(parts, stem_rows, rows, taps, axis):
    channels = parts[0].shape[2]
    count = len(parts)

    def kernel(*refs):
        stem, kernel_out, post, pre = refs[count:]
        total = sum(jnp.sum(part[...].astype(F32), axis=0) for part in refs[:count])
        stem[...] = total[:stem_rows]
        lane = lax.broadcasted_iota(jnp.int32, (taps + 1, channels), 1)
        tap = lax.broadcasted_iota(jnp.int32, (taps + 1, channels), 0)
        spread = jnp.where(lane // rows == tap, total[stem_rows : stem_rows + 1], 0.0)
        at = lax.broadcasted_iota(jnp.int32, (channels, rows), 0)
        to = lax.broadcasted_iota(jnp.int32, (channels, rows), 1)
        fold = jnp.where(at % rows == to, 1.0, 0.0)
        table = jnp.dot(
            spread, fold, preferred_element_type=F32, precision=lax.Precision.HIGHEST
        )
        kernel_out[...] = table.T[:, :taps]
        post[...] = table[taps : taps + 1]
        mine = lax.axis_index(axis) * rows
        own = jnp.where(at == to + mine, 1.0, 0.0)
        line = jnp.broadcast_to(total[stem_rows + 1 : stem_rows + 2], (8, channels))
        pre[...] = jnp.dot(
            line, own, preferred_element_type=F32, precision=lax.Precision.HIGHEST
        )[:1]

    return pl.pallas_call(
        kernel,
        out_shape=[
            jax.ShapeDtypeStruct((stem_rows, channels), F32),
            jax.ShapeDtypeStruct((rows, taps), F32),
            jax.ShapeDtypeStruct((1, rows), F32),
            jax.ShapeDtypeStruct((1, rows), F32),
        ],
        compiler_params=kernel_params(),
        cost_estimate=costs(1 << 24, 2 * count * parts[0].size),
    )(*parts)


def one_hot(rows, columns):
    return (rows[:, None] == columns[None, :]).astype(BF16)


def order_pieces(mel_pieces, dest_owner, dest_slot, dp_count):
    pieces, piece_values = mel_pieces.shape
    capacity = max(2, 2 * pieces // dp_count)
    matches = (dest_owner[:, None] == jnp.arange(dp_count, dtype=jnp.int32)[None, :]).astype(jnp.int32)
    earlier = jnp.cumsum(matches, axis=0) - matches
    position = dest_owner * capacity + jnp.sum(earlier * matches, axis=1)
    pick = one_hot(jnp.arange(dp_count * capacity, dtype=jnp.int32), position)
    label = jnp.broadcast_to((dest_slot + 1).astype(BF16)[:, None], (pieces, 128))
    return jnp.dot(
        pick, jnp.concatenate([mel_pieces, label], axis=1), preferred_element_type=F32
    ).astype(BF16)


def per_device(
    mel_pieces,
    dest_owner,
    dest_slot,
    segment_ids,
    out_grad,
    stem_weight,
    up_weight,
    down_weight,
    depth_kernel,
    gain_pre,
    gain_post,
):
    dp_count = lax.axis_size("dp")
    tm_count = lax.axis_size("tm")
    chains = stages_of({"dp": dp_count, "tm": tm_count})
    dp_chains, tm_chains = chains["dp"], chains["tm"]
    column = lax.axis_index("tm")
    taps = depth_kernel.shape[1]
    margin = (taps - 1) // 2
    block = out_grad.shape[1]
    channels = out_grad.shape[2]
    held = channels // tm_count
    rows = down_weight.shape[0]
    stem_rows = stem_weight.shape[0]
    features = stem_rows * dp_count * tm_count
    length = block * tm_count

    span = 128 * tm_count
    lane = jnp.arange(span, dtype=jnp.int32)
    grouped = (lane // rows) % tm_count * 128 + lane // (rows * tm_count) * rows + lane % rows
    if stem_rows % 16 == 0 and rows % 16 == 0:
        sent, pack, up_parts = prepare(
            mel_pieces[0], dest_owner[0], dest_slot[0], stem_weight, up_weight, depth_kernel,
            gain_pre, gain_post, dp_count, tm_count,
        )
    else:
        sent = order_pieces(mel_pieces[0], dest_owner[0], dest_slot[0], dp_count)
        up_parts = regroup_columns(up_weight, lane, grouped, "tm", tm_count)
        beside = jnp.broadcast_to(jnp.tile(gain_pre, 128 // rows)[None, :], (stem_rows, 128))
        small = jnp.concatenate(
            [depth_kernel, gain_post[:, None], jnp.zeros((rows, 128 - taps - 1), BF16)], axis=1
        )
        small = [small[q : q + stem_rows] for q in range(0, rows, stem_rows)]
        pack = jnp.concatenate([stem_weight, beside] + small, axis=1)

    stem_mine, small_all = split_gather(pack, "dp", dp_chains, channels + 128)
    up_parts = [up_parts[0]] + [swap(up_parts[k], "tm", k) for k in range(1, tm_count)]
    up_mine = place_parts(up_parts, "tm", 1, tm_count, 0).reshape(tm_count * rows, 2 * held)
    up_near = gather_stage(up_mine, "dp", *dp_chains[0], 0)
    up_full = gather_rest(up_near, "dp", dp_chains).reshape(channels, 2 * held)
    down_near = gather_stage(after(down_weight, up_near), "dp", *dp_chains[0], 0)
    down_full = gather_rest(down_near, "dp", dp_chains).reshape(held, channels)
    stem_parts = gather_parts(stem_mine, "tm", tm_chains)
    stem_all = place_parts(stem_parts, "tm", 1, tm_count, 1)
    stem_all = stem_all.reshape(features, channels + 128)

    pieces = mel_pieces.shape[1]
    capacity = max(2, 2 * pieces // dp_count)
    arrived = lax.all_to_all(
        after(sent, up_mine, stem_mine).reshape(dp_count, capacity, -1), "dp", split_axis=0, concat_axis=0, tiled=True
    ).reshape(dp_count * capacity, -1)
    frames = place_frames(arrived, pieces, features)
    frames = place_parts(gather_parts(frames, "tm", tm_chains), "tm", 1, tm_count, 0)
    frames = frames.reshape(length, features)
    grad_out = out_grad[0]
    grad_out_all = gather_parts(after(grad_out, stem_parts[2]), "tm", tm_chains)
    grad_out_all = place_parts(grad_out_all, "tm", 1, tm_count, 0).reshape(length, channels)
    segments = jnp.pad(segment_ids[0], (PAD, PAD), constant_values=-1)
    segments = jnp.broadcast_to(segments[:, None], (length + 2 * PAD, 128))

    extra = 16
    normed, stem_pre, gain_one, frames_turned = stem_forward(
        frames, stem_all, tm_count, "tm", rows, extra
    )
    linear, gate_sig, gated = up_forward(normed, up_full)
    conv, stats, turned = conv_forward(gated, small_all, segments, taps)
    grad_act = lax.dot_general(
        grad_out_all, down_full, (((1,), (1,)), ((), ())), preferred_element_type=F32
    )
    activated, conv_hat, grad_hat, inverse, sums, gain_post_term = activate(
        conv, swap_all(stats, "tm"), turned, grad_act, taps
    )
    sums = swap_all(sums, "tm")
    by_parts = stem_rows % 16 == 0 and rows % 16 == 0
    if by_parts:
        down_terms = part_terms(activated, grad_out_all, "dp", dp_chains)
    else:
        down_terms = [message_terms(activated, grad_out_all, dp_count, tm_count)]
    y_own, *y_others = block_terms(activated, down_full, False, "tm", tm_count)
    down_terms, y_others = lax.optimization_barrier((down_terms, y_others, *sums))[:2]
    y_far, y_parts, y_passed = block_sum(y_others, "tm", tm_chains)
    if by_parts:
        down_parts = swap_parts(down_terms, "dp", dp_chains[-1])

    grad_hat = after(grad_hat, *down_terms, y_passed)
    grad_proj, kernel_term = conv_backward(
        grad_hat, conv_hat, inverse, sums, gated, segments, linear, gate_sig, turned, taps,
        gain_post_term,
    )

    own_terms, *other_terms = block_terms(
        after(grad_proj, y_far), up_full, True, "tm", tm_count
    )
    small_term = kernel_term.reshape(taps + 1, dp_count, rows).transpose(1, 0, 2)
    small_term = small_term.reshape(dp_count, (taps + 1) * rows)
    small_term = jnp.pad(small_term, ((0, 0), (0, channels - (taps + 1) * rows)))
    if by_parts:
        up_terms = part_terms(after(normed, *other_terms), grad_proj, "dp", dp_chains)
    else:
        up_terms = [message_terms(normed, grad_proj, dp_count, tm_count)]
    grad_far, grad_parts, grad_passed = block_sum(other_terms, "tm", tm_chains, up_terms[-1])
    if by_parts:
        down_parts = add_parts(
            [after(down_parts[0], grad_passed)] + down_parts[1:], "dp", dp_chains[0]
        )
        down_parts = swap_parts(down_parts, "dp", dp_chains[0])
        up_parts = reduce_parts(up_terms, "dp", dp_chains)
    grad_stem_pre = stem_backward(
        own_terms, grad_parts + [grad_far], stem_pre, grad_out, gain_one, extra
    )
    grad_stem_parts = gather_parts(grad_stem_pre, "tm", tm_chains)
    y_out = finish_rows(after(stem_pre, grad_stem_pre), y_own, y_parts + [y_far])
    if by_parts:
        stem_terms = stem_message(
            frames_turned, grad_stem_parts, small_term, "dp", dp_chains, stem_rows
        )
        stem_sums = reduce_parts(stem_terms, "dp", dp_chains)
        down_parts = cut_columns([after(down_parts[0], grad_stem_pre)] + down_parts[1:], "tm")
        down_parts = [down_parts[0]] + [
            swap(part, "tm", k) for k, part in enumerate(down_parts[1:], 1)
        ]
        grad_down = stack_rows(down_parts, "tm")
        up_parts = cut_columns(up_parts, "tm")
        up_parts = [up_parts[0]] + [
            swap(part, "tm", k) for k, part in enumerate(up_parts[1:], 1)
        ]
        grad_up = mix_columns(up_parts, "tm", rows)
    else:
        down_sums = lax.all_to_all(
            down_terms[0], ("dp", "tm"), split_axis=0, concat_axis=0, tiled=True
        )
        grad_down = jnp.sum(
            down_sums.reshape(dp_count, tm_count * rows, held).astype(F32), axis=0
        )
        up_sums = lax.all_to_all(
            up_terms[0], ("dp", "tm"), split_axis=0, concat_axis=0, tiled=True
        )
        up_sums = up_sums.reshape(dp_count, tm_count, tm_count * rows, 128)
        spread = one_hot(lane, grouped).reshape(tm_count, 128, span)
        grad_up = jnp.einsum("ijab,jbc->ac", up_sums, spread, preferred_element_type=F32)
        stem_sum = sum(
            jnp.dot(frames_turned[k], grad_stem_parts[k], preferred_element_type=F32)
            for k in range(tm_count)
        )
        share = features // tm_count
        gain_term = stem_sum[share].reshape(dp_count, 1, tm_count * rows)
        gain_term = jnp.pad(gain_term, ((0, 0), (0, 0), (0, channels - tm_count * rows)))
        stem_terms = stem_sum[:share].reshape(dp_count, stem_rows, channels)
        stem_terms = jnp.concatenate([stem_terms, small_term[:, None, :], gain_term], axis=1)
        stem_terms = jnp.pad(stem_terms.astype(BF16), ((0, 0), (0, 6), (0, 0)))
        stem_sums = [
            lax.all_to_all(stem_terms, "dp", split_axis=0, concat_axis=0, tiled=True)
        ]
    grad_stem, grad_kernel, grad_gain_post, grad_gain_pre = stem_finish(
        stem_sums, stem_rows, rows, taps, "tm"
    )
    grad_gain_post, grad_gain_pre = grad_gain_post[0], grad_gain_pre[0]
    return (y_out[None], grad_stem, grad_up, grad_down, grad_kernel, grad_gain_pre, grad_gain_post)


def solution(mesh):
    return jax.shard_map(
        per_device,
        mesh=mesh,
        in_specs=(
            P("dp", "tm", None),
            P("dp", "tm"),
            P("dp", "tm"),
            P("dp", None),
            P("dp", "tm", None),
            P(("dp", "tm"), None),
            P(("dp", "tm"), None),
            P(("dp", "tm"), None),
            P(("dp", "tm"), None),
            P(("dp", "tm")),
            P(("dp", "tm")),
        ),
        out_specs=(
            P("dp", "tm", None),
            P(("dp", "tm"), None),
            P("dp", "tm"),
            P("dp", "tm"),
            P(("dp", "tm"), None),
            P(("dp", "tm")),
            P(("dp", "tm")),
        ),
        check_vma=False,
    )
```

```python
import jax
import jax.numpy as jnp
from jax import lax
from jax.experimental import pallas as pl
from jax.experimental.pallas import tpu as pltpu
from jax.sharding import PartitionSpec as P

NORM_EPS = 1e-05
BF16 = jnp.bfloat16
F32 = jnp.float32


def stages_of(sizes):
    if sizes["dp"] == 8 and sizes["tm"] == 4:
        return {"dp": ((2, 4), (1, 2)), "tm": ((2, 2), (1, 2))}
    if sizes["dp"] == 64 and sizes["tm"] == 4:
        return {"dp": ((8, 8), (2, 4), (1, 2)), "tm": ((1, 4),)}
    return {axis: ((1, size),) for axis, size in sizes.items()}


def swap(value, axis, mask):
    size = lax.axis_size(axis)
    return lax.ppermute(value, axis, [(i, i ^ mask) for i in range(size)])


VMEM_LIMIT = 16 << 20


def kernel_params():
    return pltpu.CompilerParams(vmem_limit_bytes=VMEM_LIMIT)


def costs(microseconds):
    return pl.CostEstimate(
        flops=int(microseconds * 2e10), bytes_accessed=1 << 16, transcendentals=0
    )


def after(value, *others):
    return lax.optimization_barrier((value,) + others)[0]


def place_parts(parts, axis, stride, size, dim):
    shape = parts[0].shape
    out_shape = shape[:dim] + (size,) + shape[dim:]

    def kernel(*refs):
        place = (lax.axis_index(axis) // stride) % size
        for k in range(size):
            refs[size][(slice(None),) * dim + (place ^ k,)] = refs[k][...]

    return pl.pallas_call(
        kernel,
        out_shape=jax.ShapeDtypeStruct(out_shape, parts[0].dtype),
        compiler_params=kernel_params(),
        cost_estimate=costs(0.8),
    )(*parts)


def gather_stage(value, axis, stride, size, dim):
    parts = [value] + [swap(value, axis, k * stride) for k in range(1, size)]
    return place_parts(parts, axis, stride, size, dim)


def gather_rest(value, axis, chains):
    shape = value.shape[1:]
    for dim, (stride, size) in enumerate(chains[1:], 1):
        value = gather_stage(value, axis, stride, size, dim)
    return value.reshape((-1,) + shape)


def block_terms(left, right, transposed, axis, count):
    block = left.shape[0] // count
    width = right.shape[0] if transposed else right.shape[1]
    dims = (((1,), (1 if transposed else 0,)), ((), ()))

    def kernel(left_ref, right_ref, own, *refs):
        others, terms = refs[:-1], refs[-1]
        place = lax.axis_index(axis)
        terms[...] = lax.dot_general(
            left_ref[...], right_ref[...], dims, preferred_element_type=F32
        )
        for k in range(count):
            start = pl.multiple_of((place ^ k) * block, block)
            if k == 0:
                own[...] = terms[pl.ds(start, block), :]
            else:
                others[k - 1][...] = terms[pl.ds(start, block), :].astype(BF16)

    return pl.pallas_call(
        kernel,
        out_shape=[jax.ShapeDtypeStruct((block, width), F32)]
        + [jax.ShapeDtypeStruct((block, width), BF16)] * (count - 1),
        scratch_shapes=[pltpu.VMEM((count * block, width), F32)],
        compiler_params=kernel_params(),
        cost_estimate=costs(1.2),
    )(left, right)


def block_sum(others, axis, chains, first=None):
    if list(chains) == [(2, 2), (1, 2)]:
        near, passed = swap(others[0], axis, 1), swap(others[2], axis, 1)
        passed = add_pair(others[1], passed)
        if first is not None:
            passed = after(passed, first)
        return swap(passed, axis, 2), [near], passed
    parts = [swap(other, axis, k) for k, other in enumerate(others, 1)]
    return parts[-1], parts[:-1], others[-1]


def add_pair(one, other):
    def kernel(one_ref, other_ref, out):
        out[...] = (one_ref[...].astype(F32) + other_ref[...].astype(F32)).astype(BF16)

    return pl.pallas_call(
        kernel,
        out_shape=jax.ShapeDtypeStruct(one.shape, BF16),
        compiler_params=kernel_params(),
        cost_estimate=costs(0.5),
    )(one, other)


def finish_rows(stem_pre, own, parts):
    def kernel(pre_ref, own_ref, *refs):
        total = own_ref[...]
        for part in refs[:-1]:
            total = total + part[...].astype(F32)
        pre = pre_ref[...]
        stem_out = (pre * jax.nn.sigmoid(pre)).astype(BF16).astype(F32)
        refs[-1][...] = (stem_out + total).astype(BF16)

    return pl.pallas_call(
        kernel,
        out_shape=jax.ShapeDtypeStruct(own.shape, BF16),
        compiler_params=kernel_params(),
        cost_estimate=costs(0.6),
    )(stem_pre, own, *parts)


def turn(value):
    rows, columns = value.shape

    def kernel(source, out):
        for c in range(0, columns, 128):
            out[c : c + 128, :] = source[:, c : c + 128].astype(F32).T.astype(BF16)

    return pl.pallas_call(
        kernel,
        out_shape=jax.ShapeDtypeStruct((columns, rows), value.dtype),
        compiler_params=kernel_params(),
        cost_estimate=costs(1.0),
    )(value)


def part_terms(left, right, turned, axis, chains):
    total = lax.axis_size(axis)
    stride, size = chains[-1]
    rows, columns = left.shape[0 if turned else 1] // total, right.shape[1]
    step = max(1, 512 // rows) if turned else max(1, 128 // rows)

    def kernel(left_ref, right_ref, *outs):
        place = (lax.axis_index(axis) // stride) % size
        for i in range(0, total, step):
            block = slice(i * rows, (i + step) * rows)
            if turned:
                term = jnp.dot(left_ref[block, :], right_ref[...], preferred_element_type=F32)
            else:
                term = lax.dot_general(
                    left_ref[:, block],
                    right_ref[...],
                    (((0,), (0,)), ((), ())),
                    preferred_element_type=F32,
                )
            term = term.astype(BF16)
            for n in range(step):
                for k in range(size):

                    @pl.when((i + n) % size ^ place == k)
                    def _():
                        outs[k][(i + n) // size] = term[n * rows : (n + 1) * rows]

    return pl.pallas_call(
        kernel,
        out_shape=[jax.ShapeDtypeStruct((total // size, rows, columns), BF16)] * size,
        compiler_params=kernel_params(),
        cost_estimate=costs(1.5),
    )(left, right)


def join_parts(first, second, axis, chain):
    stride, size = chain
    count = len(first)
    lead, rows, columns = first[0].shape
    _, below, wide = second[0].shape
    folds = wide // columns

    def kernel(*refs):
        place = (lax.axis_index(axis) // stride) % size
        outs = refs[2 * count :]
        for a in range(lead // size):
            for k in range(size):
                at = a * size + (place ^ k)
                total = sum(part[at].astype(F32) for part in refs[:count])
                outs[k][a, :rows, :] = total.astype(BF16)
                total = sum(part[at].astype(F32) for part in refs[count : 2 * count]).astype(BF16)
                for f in range(folds):
                    outs[k][a, rows + f * below : rows + (f + 1) * below, :] = total[
                        :, f * columns : (f + 1) * columns
                    ]

    shape = (lead // size, rows + folds * below, columns)
    return pl.pallas_call(
        kernel,
        out_shape=[jax.ShapeDtypeStruct(shape, BF16)] * size,
        compiler_params=kernel_params(),
        cost_estimate=costs(0.8),
    )(*first, *second)


def swap_all_parts(parts, axis):
    return [parts[0]] + [swap(part, axis, k) for k, part in enumerate(parts[1:], 1)]


def swap_parts(parts, axis, chain):
    stride, _ = chain
    return [parts[0]] + [swap(part, axis, k * stride) for k, part in enumerate(parts[1:], 1)]


def add_parts(parts, axis, chain):
    stride, size = chain
    shape = (parts[0].shape[0] // size,) + parts[0].shape[1:]

    def kernel(*refs):
        place = (lax.axis_index(axis) // stride) % size
        for a in range(shape[0]):
            for k in range(size):
                at = a * size + (place ^ k)
                total = sum(part[at].astype(F32) for part in refs[: len(parts)])
                refs[len(parts) + k][a] = total.astype(BF16)

    return pl.pallas_call(
        kernel,
        out_shape=[jax.ShapeDtypeStruct(shape, BF16)] * size,
        compiler_params=kernel_params(),
        cost_estimate=costs(0.6),
    )(*parts)


def reduce_rest(parts, axis, chains):
    parts = swap_parts(parts, axis, chains[-1])
    for chain in reversed(chains[:-1]):
        parts = swap_parts(add_parts(parts, axis, chain), axis, chain)
    return parts


def cut_columns(parts, axis, rows, below):
    count = lax.axis_size(axis)
    _, height, columns = parts[0].shape
    share = columns // count
    folds = (height - rows) // below
    wide = folds * columns // count

    def kernel(*refs):
        place = lax.axis_index(axis)
        total = sum(part[0].astype(F32) for part in refs[: len(parts)]).astype(BF16)
        for j in range(count):
            fold, start = divmod(wide * j, columns)
            for k in range(count):

                @pl.when(place ^ j == k)
                def _():
                    out = refs[len(parts) + k]
                    out[:rows, :] = total[:rows, j * share : (j + 1) * share]
                    for f in range(folds):
                        lanes = slice(start + f * share, start + (f + 1) * share)
                        out[rows + f * below : rows + (f + 1) * below, :] = total[
                            rows + fold * below : rows + (fold + 1) * below, lanes
                        ]

    return pl.pallas_call(
        kernel,
        out_shape=[jax.ShapeDtypeStruct((height, share), BF16)] * count,
        compiler_params=kernel_params(),
        cost_estimate=costs(0.6),
    )(*parts)


def mix_columns(parts, axis, rows, small):
    count = len(parts)
    height, share = parts[0].shape
    span = share * count
    folds = (height - rows) // small

    def kernel(*refs):
        place = lax.axis_index(axis)
        upper, lower = refs[count:]
        at, to = iota((share, span), 0), iota((share, span), 1)
        total = jnp.zeros((rows, span), F32)
        for k in range(count):
            want = at // small * (small * count) + (place ^ k) * small + at % small
            spread = table(to == want)
            total = total + jnp.dot(refs[k][:rows, :], spread, preferred_element_type=F32)
            start = pl.multiple_of((place ^ k) * small, small)
            for f in range(folds):
                lower[pl.ds(start, small), f * share : (f + 1) * share] = refs[k][
                    rows + f * small : rows + (f + 1) * small, :
                ].astype(F32)
        upper[...] = total

    return pl.pallas_call(
        kernel,
        out_shape=[
            jax.ShapeDtypeStruct((rows, span), F32),
            jax.ShapeDtypeStruct((count * small, folds * share), F32),
        ],
        compiler_params=kernel_params(),
        cost_estimate=costs(0.8),
    )(*parts)


def message_terms(left, right, parts, sides):
    rows, columns = left.shape[1] // parts, right.shape[1] // sides
    terms = jnp.dot(left.T, right, preferred_element_type=F32).astype(BF16)
    terms = terms.reshape(parts, rows, sides, columns).transpose(0, 2, 1, 3)
    return terms.reshape(parts * sides, rows, columns)


def regroup_columns(weight, lane, grouped, axis, count):
    rows, columns = weight.shape
    span = lane.shape[0]
    groups = columns // span
    parts = jnp.dot(
        weight.reshape(rows * groups, span), one_hot(grouped, lane), preferred_element_type=F32
    ).astype(BF16)
    parts = parts.reshape(rows, groups, count, 128).transpose(2, 0, 1, 3)
    parts = parts.reshape(count, rows, groups * 128)
    return [
        lax.dynamic_index_in_dim(parts, lax.axis_index(axis) ^ k, 0, keepdims=False)
        for k in range(count)
    ]


def stem_backward(own, parts, stem_pre, grad_out, gain, extra):
    block, channels = own.shape

    def kernel(own_ref, pre_ref, out_grad_ref, gain_ref, *refs):
        out = refs[-1]
        pre = pre_ref[...]
        sigma = jax.nn.sigmoid(pre)
        hat, inverse = standardize((pre * sigma).astype(BF16).astype(F32))
        grad = own_ref[...]
        for part in refs[:-1]:
            grad = grad + part[...].astype(F32)
        out[block:, :] = jnp.concatenate(
            [jnp.sum(grad * hat, axis=0, keepdims=True), jnp.zeros((extra - 1, channels), F32)]
        ).astype(BF16)
        back = grad * gain_ref[...]
        first = jnp.mean(back, axis=-1, keepdims=True)
        second = jnp.mean(back * hat, axis=-1, keepdims=True)
        stem_out = out_grad_ref[...].astype(F32) + (back - first - hat * second) * inverse
        out[:block, :] = (stem_out * (sigma * (1.0 + pre * (1.0 - sigma)))).astype(BF16)

    return pl.pallas_call(
        kernel,
        out_shape=jax.ShapeDtypeStruct((block + extra, channels), BF16),
        compiler_params=kernel_params(),
        cost_estimate=costs(0.7),
    )(own, stem_pre, grad_out, gain, *parts)


def standardize(values):
    centered = values - jnp.mean(values, axis=-1, keepdims=True)
    inverse = lax.rsqrt(jnp.mean(centered * centered, axis=-1, keepdims=True) + NORM_EPS)
    return (centered * inverse, inverse)


def gather_parts(value, axis, chains, first=None):
    if list(chains) == [(2, 2), (1, 2)]:
        far = swap(value, axis, 2)
        if first is not None:
            far = after(far, first)
        return [value, swap(value, axis, 1), far, swap(far, axis, 1)]
    return [value] + [swap(value, axis, k) for k in range(1, lax.axis_size(axis))]


def swap_all(value, axis):
    return [value] + [swap(value, axis, k) for k in range(1, lax.axis_size(axis))]


def split_parts(parts, axis, stride, size, dim, cuts):
    shape = parts[0].shape
    lead = shape[:dim] + (size,) + shape[dim:-2]
    rows = shape[-2]

    def kernel(*refs):
        place = (lax.axis_index(axis) // stride) % size
        inner = (slice(None),) * (len(lead) - dim - 1)
        for k in range(size):
            target = (slice(None),) * dim + (place ^ k,) + inner
            start = 0
            for n, (width, pieces) in enumerate(cuts):
                for q in range(pieces):
                    refs[size + n][target + (q,)] = refs[k][..., start : start + width]
                    start += width

    return pl.pallas_call(
        kernel,
        out_shape=[
            jax.ShapeDtypeStruct(lead + (pieces, rows, width), parts[0].dtype)
            for width, pieces in cuts
        ],
        compiler_params=kernel_params(),
        cost_estimate=costs(1.0),
    )(*parts)


def split_rest(value, axis, chains, cuts):
    for dim, (stride, size) in enumerate(chains[1:], 1):
        parts = [value] + [swap(value, axis, k * stride) for k in range(1, size)]
        if dim == len(chains) - 1:
            return split_parts(parts, axis, stride, size, dim, cuts)
        value = place_parts(parts, axis, stride, size, dim)


def iota(shape, dim):
    return lax.broadcasted_iota(jnp.int32, shape, dim)


def table(flags):
    return jnp.where(flags, 1.0, 0.0).astype(BF16)


def fetch(sources, held, sems):
    copies = [
        pltpu.make_async_copy(source, target, sems.at[k])
        for k, (source, target) in enumerate(zip(sources, held))
    ]
    for copy in copies:
        copy.start()
    for copy in copies:
        copy.wait()


def fetching_call(kernel, inputs, out_shape, cost):
    return pl.pallas_call(
        kernel,
        out_shape=out_shape,
        in_specs=[pl.BlockSpec(memory_space=pl.ANY)] * len(inputs),
        scratch_shapes=[pltpu.VMEM(value.shape, value.dtype) for value in inputs]
        + [pltpu.SemaphoreType.DMA((len(inputs),))],
        cost_estimate=cost,
    )(*inputs)


def up_columns(up, rows, tm_count):
    span = 128 * tm_count
    groups = up.shape[1] // span

    def kernel(source, *refs):
        up_parts, (up_ref, sems) = refs[:tm_count], refs[tm_count:]
        fetch([source], [up_ref], sems)
        place = lax.axis_index("tm")
        at, to = iota((span, 128), 0), iota((span, 128), 1)
        for k in range(tm_count):
            want = to // rows * (rows * tm_count) + (place ^ k) * rows + to % rows
            pick = table(at == want)
            for g in range(groups):
                up_parts[k][:, g * 128 : (g + 1) * 128] = jnp.dot(
                    up_ref[:, g * span : (g + 1) * span], pick, preferred_element_type=F32
                ).astype(BF16)

    return fetching_call(
        kernel,
        (up,),
        [jax.ShapeDtypeStruct((rows, up.shape[1] // tm_count), BF16)] * tm_count,
        costs(1.5),
    )


def prepare(mel, owner, slot, stem, down, taps, gain_one, gain_two, dp_count):
    pieces, values = mel.shape
    capacity = max(2, 2 * pieces // dp_count)
    slots = dp_count * capacity
    stem_rows, channels = stem.shape
    rows, tap_count = taps.shape
    chunks = rows // stem_rows
    beyond = channels + 128 * (chunks + 1)
    inputs = (
        stem, taps, gain_one[None, :], gain_two[None, :], owner[None, :], slot[None, :], mel, down
    )
    count = len(inputs)

    def kernel(*refs):
        sent, pack = refs[count : count + 2]
        held = refs[count + 2 : -1]
        fetch(refs[:count], held, refs[-1])
        stem_ref, taps_ref, one_ref, two_ref, owner_ref, slot_ref, mel_ref, down_ref = held
        pack[:, :channels] = stem_ref[...]
        lane = iota((rows, 128), 1)
        spread = table(lane % rows == iota((rows, 128), 0))
        gain = jnp.broadcast_to(one_ref[...].astype(F32), (stem_rows, rows)).astype(BF16)
        pack[:, channels : channels + 128] = jnp.dot(
            gain, spread, preferred_element_type=F32
        ).astype(BF16)
        tap_lane = table(iota((tap_count, 128), 1) == iota((tap_count, 128), 0))
        square = iota((rows, rows), 0) == iota((rows, rows), 1)
        diagonal = jnp.where(
            square, jnp.broadcast_to(two_ref[...].astype(F32), (rows, rows)), 0.0
        ).astype(BF16)
        small = jnp.dot(taps_ref[...], tap_lane, preferred_element_type=F32)
        small = small + jnp.dot(diagonal, table(lane == tap_count), preferred_element_type=F32)
        for q in range(chunks):
            lanes = slice(channels + 128 * (q + 1), channels + 128 * (q + 2))
            pack[:, lanes] = small[q * stem_rows : (q + 1) * stem_rows].astype(BF16)
            lanes = slice(beyond + channels * q, beyond + channels * (q + 1))
            pack[:, lanes] = down_ref[q * stem_rows : (q + 1) * stem_rows, :]

        owners = jnp.broadcast_to(owner_ref[...].astype(F32), (pieces, pieces))
        earlier = iota((pieces, pieces), 0) < iota((pieces, pieces), 1)
        same = jnp.where(owners.T == owners, jnp.where(earlier, 1.0, 0.0), 0.0)
        target = owners[:1] * float(capacity) + jnp.sum(same, axis=0, keepdims=True)
        target = jnp.broadcast_to(target, (slots, pieces)).astype(jnp.int32)
        chosen = target == iota((slots, pieces), 0)
        pick = table(chosen)
        sent[:, :values] = jnp.dot(pick, mel_ref[...], preferred_element_type=F32).astype(BF16)
        labels = jnp.broadcast_to(slot_ref[...].astype(F32) + 1.0, (slots, pieces))
        label = jnp.sum(jnp.where(chosen, labels, 0.0), axis=1, keepdims=True)
        sent[:, values:] = jnp.broadcast_to(label, (slots, 128)).astype(BF16)

    return fetching_call(
        kernel,
        inputs,
        [
            jax.ShapeDtypeStruct((slots, values + 128), BF16),
            jax.ShapeDtypeStruct((stem_rows, beyond + channels * chunks), BF16),
        ],
        costs(2.0),
    )


def place_frames(arrived, pieces, features):
    slots, width = arrived.shape
    steps = (width - 128) // features

    def kernel(arrived_ref, out):
        labels = arrived_ref[:, steps * features :].astype(F32).T[:1]
        want = jnp.broadcast_to(labels, (pieces * steps, slots)).astype(jnp.int32)
        row = lax.broadcasted_iota(jnp.int32, (pieces * steps, slots), 0)
        total = jnp.zeros((pieces * steps, features), F32)
        for q in range(steps):
            put = jnp.where(row == (want - 1) * steps + q, 1.0, 0.0).astype(BF16)
            total = total + jnp.dot(
                put, arrived_ref[:, q * features : (q + 1) * features], preferred_element_type=F32
            )
        out[...] = total.astype(BF16)

    return pl.pallas_call(
        kernel,
        out_shape=jax.ShapeDtypeStruct((pieces * steps, features), BF16),
        compiler_params=kernel_params(),
        cost_estimate=costs(0.6),
    )(arrived)


def stem_forward(frames, stem_all, count, axis, rows, extra):
    length = frames.shape[0]
    features, width = stem_all.shape
    channels = width - 128
    block = length // count
    stem_rows = features * rows // channels
    share = features // count

    def kernel(frames_ref, stem_ref, normed, pre_own, gain_out, turned):
        place = lax.axis_index(axis)
        feature = lax.broadcasted_iota(jnp.int32, (features, share), 0)
        chosen = lax.broadcasted_iota(jnp.int32, (features, share), 1)
        chosen = (chosen // stem_rows * count + place) * stem_rows + chosen % stem_rows
        pick = jnp.where(feature == chosen, 1.0, 0.0).astype(BF16)
        corner = lax.broadcasted_iota(jnp.int32, (extra, extra), 0)
        corner = corner + lax.broadcasted_iota(jnp.int32, (extra, extra), 1)
        corner = jnp.where(corner == 0, 1.0, 0.0).astype(BF16)
        for k in range(count):
            start = pl.multiple_of((place ^ k) * block, block)
            turned[k, :share, :block] = lax.dot_general(
                pick,
                frames_ref[pl.ds(start, block), :],
                (((0,), (1,)), ((), ())),
                preferred_element_type=F32,
            ).astype(BF16)
            turned[k, share:, :block] = jnp.zeros((extra, block), BF16)
            turned[k, :share, block:] = jnp.zeros((share, extra), BF16)
            turned[k, share:, block:] = corner
        beside = stem_ref[:, channels:].astype(F32)
        gains = []
        for g in range(channels // 128):
            row = lax.broadcasted_iota(jnp.int32, (features, 128), 0)
            lane = lax.broadcasted_iota(jnp.int32, (features, 128), 1) + g * 128
            gains.append(
                jnp.sum(
                    jnp.where(row == lane // rows * stem_rows, beside, 0.0), axis=0, keepdims=True
                )
            )
        gain_out[...] = jnp.concatenate(gains, axis=1)
        for b in range(count):
            pre = jnp.dot(
                frames_ref[b * block : (b + 1) * block, :],
                stem_ref[:, :channels],
                preferred_element_type=F32,
            )
            hat, _ = standardize((pre * jax.nn.sigmoid(pre)).astype(BF16).astype(F32))
            normed[b * block : (b + 1) * block, :] = (hat * gain_out[...]).astype(BF16)

            @pl.when(place == b)
            def _():
                pre_own[...] = pre

    return pl.pallas_call(
        kernel,
        out_shape=[
            jax.ShapeDtypeStruct((length, channels), BF16),
            jax.ShapeDtypeStruct((block, channels), F32),
            jax.ShapeDtypeStruct((1, channels), F32),
            jax.ShapeDtypeStruct((count, share + extra, block + extra), BF16),
        ],
        compiler_params=kernel_params(),
        cost_estimate=costs(2.8),
    )(frames, stem_all)


PAD = 16


def up_forward(normed, up):
    length = normed.shape[0]
    held = up.shape[1] // 2
    step = min(128, length)

    def kernel(normed_ref, up_ref, linear, gate, gated):
        edge = jnp.zeros((PAD, held), F32)
        gated[:PAD, :] = edge
        gated[PAD + length :, :] = edge
        for b in range(0, length, step):
            proj = jnp.dot(normed_ref[b : b + step, :], up_ref[...], preferred_element_type=F32)
            sigma = jax.nn.sigmoid(proj[:, held:])
            linear[b : b + step, :] = proj[:, :held]
            gate[b : b + step, :] = sigma
            gated[PAD + b : PAD + b + step, :] = (proj[:, :held] * sigma).astype(BF16).astype(F32)

    return pl.pallas_call(
        kernel,
        out_shape=[
            jax.ShapeDtypeStruct((length, held), F32),
            jax.ShapeDtypeStruct((length, held), F32),
            jax.ShapeDtypeStruct((length + 2 * PAD, held), F32),
        ],
        compiler_params=kernel_params(),
        cost_estimate=costs(0.7),
    )(normed, up)


def columns_of(first, second):
    rows = first.shape[0]
    lane = lax.broadcasted_iota(jnp.int32, (rows, 128), 1)
    both = jnp.where(lane == 0, first, jnp.where(lane == 1, second, 0.0))
    return both.T[:8]


def rows_of(table):
    rows = table.shape[1]
    turned = jnp.concatenate([table, jnp.zeros((120, rows), F32)], axis=0).T
    return turned[:, :1], turned[:, 1:2]


TILE = 64


def conv_forward(gated, small, segments, taps):
    length, held = gated.shape[0] - 2 * PAD, gated.shape[1]
    margin = (taps - 1) // 2

    def kernel(gated_ref, small_ref, seg_ref, conv, stats, turned, gated_near, seg_near):
        turned[...] = small_ref[...].astype(F32).T

        def tile(t, carry):
            base = pl.multiple_of(t * TILE, TILE)
            gated_near[...] = gated_ref[pl.ds(base, TILE + 2 * PAD), :]
            seg_near[...] = seg_ref[pl.ds(base, TILE + 2 * PAD), :]
            centre = seg_near[PAD : PAD + TILE, :]
            sums = [jnp.zeros((TILE, 128), F32) for _ in range(held // 128)]
            for k in range(taps):
                shift = PAD + k - margin
                inside = seg_near[shift : shift + TILE, :] == centre
                for g in range(held // 128):
                    lanes = slice(g * 128, (g + 1) * 128)
                    value = gated_near[shift : shift + TILE, lanes]
                    sums[g] = sums[g] + jnp.where(inside, value, 0.0) * turned[k : k + 1, lanes]
            conv[pl.ds(base, TILE), :] = jnp.concatenate(sums, axis=1)
            return carry

        lax.fori_loop(0, length // TILE, tile, 0)
        value = conv[...]
        mean = jnp.mean(value, axis=-1, keepdims=True)
        centered = value - mean
        stats[...] = columns_of(mean, jnp.sum(centered * centered, axis=-1, keepdims=True))

    return pl.pallas_call(
        kernel,
        out_shape=[
            jax.ShapeDtypeStruct((length, held), F32),
            jax.ShapeDtypeStruct((8, length), F32),
            jax.ShapeDtypeStruct((128, held), F32),
        ],
        scratch_shapes=[
            pltpu.VMEM((TILE + 2 * PAD, held), F32),
            pltpu.VMEM((TILE + 2 * PAD, 128), jnp.int32),
        ],
        compiler_params=kernel_params(),
        cost_estimate=costs(3.0),
    )(gated, small, segments)


def activate(conv, stats, turned, grad_act, taps):
    length, held = conv.shape
    count = len(stats)

    def kernel(conv_ref, turned_ref, grad_ref, *refs):
        tables, (active, hat_out, grad_hat_out, inverse_out, sums, gain_term) = (
            refs[:count], refs[count:],
        )
        means = [table[0:1, :] for table in tables]
        mean = sum(means) * (1.0 / count)
        squares = sum(table[1:2, :] for table in tables)
        squares = squares + held * sum((one - mean) * (one - mean) for one in means)
        inverse = lax.rsqrt(squares * (1.0 / (held * count)) + NORM_EPS)
        both = jnp.concatenate([mean, inverse, jnp.zeros((6, length), F32)], axis=0)
        mean, inverse = rows_of(both)
        inverse_out[...] = jnp.broadcast_to(inverse, (length, 128))
        gain = turned_ref[taps : taps + 1, :]
        hat = (conv_ref[...] - mean) * inverse
        scaled = hat * gain
        sigma = jax.nn.sigmoid(scaled)
        active[...] = (scaled * sigma).astype(BF16)
        grad_scaled = grad_ref[...] * (sigma * (1.0 + scaled * (1.0 - sigma)))
        gain_term[...] = jnp.sum(grad_scaled * hat, axis=0, keepdims=True)
        grad_hat = grad_scaled * gain
        hat_out[...] = hat
        grad_hat_out[...] = grad_hat
        sums[...] = columns_of(
            jnp.sum(grad_hat, axis=-1, keepdims=True),
            jnp.sum(grad_hat * hat, axis=-1, keepdims=True),
        )

    return pl.pallas_call(
        kernel,
        out_shape=[
            jax.ShapeDtypeStruct((length, held), BF16),
            jax.ShapeDtypeStruct((length, held), F32),
            jax.ShapeDtypeStruct((length, held), F32),
            jax.ShapeDtypeStruct((length, 128), F32),
            jax.ShapeDtypeStruct((8, length), F32),
            jax.ShapeDtypeStruct((1, held), F32),
        ],
        compiler_params=kernel_params(),
        cost_estimate=costs(0.7),
    )(conv, turned, grad_act, *stats)


def conv_backward(grad_hat, hat, inverse, sums, gated, segments, linear, gate, turned, taps, gain_term):
    length, held = hat.shape
    count = len(sums)
    margin = (taps - 1) // 2
    groups = held // 128

    def kernel(
        grad_ref, hat_ref, inverse_ref, gated_ref, seg_ref, linear_ref, gate_ref, turned_ref,
        gain_ref, *refs
    ):
        tables, (proj, terms), (grad_conv, partial, grad_near, gated_near, seg_near) = (
            refs[:count], refs[count : count + 2], refs[count + 2 :],
        )
        total = sum(table[...] for table in tables) * (1.0 / (held * count))
        first, second = rows_of(total)
        edge = jnp.zeros((PAD, held), F32)
        grad_conv[:PAD, :] = edge
        grad_conv[PAD + length :, :] = edge
        value = (grad_ref[...] - first - hat_ref[...] * second) * inverse_ref[:, :1]
        grad_conv[PAD : PAD + length, :] = value.astype(BF16).astype(F32)
        partial[...] = jnp.zeros_like(partial)

        def tile(t, carry):
            base = pl.multiple_of(t * TILE, TILE)
            grad_near[...] = grad_conv[pl.ds(base, TILE + 2 * PAD), :]
            gated_near[...] = gated_ref[pl.ds(base, TILE + 2 * PAD), :]
            seg_near[...] = seg_ref[pl.ds(base, TILE + 2 * PAD), :]
            centre = seg_near[PAD : PAD + TILE, :]
            lanes = [slice(g * 128, (g + 1) * 128) for g in range(groups)]
            here = [grad_near[PAD : PAD + TILE, lanes[g]] for g in range(groups)]
            back = [jnp.zeros((TILE, 128), F32) for _ in range(groups)]
            for k in range(taps):
                shift = PAD + k - margin
                inside = seg_near[shift : shift + TILE, :] == centre
                for g in range(groups):
                    near = grad_near[shift : shift + TILE, lanes[g]]
                    weight = turned_ref[taps - 1 - k : taps - k, lanes[g]]
                    back[g] = back[g] + jnp.where(inside, near, 0.0) * weight
                    source = gated_near[shift : shift + TILE, lanes[g]]
                    product = jnp.where(inside, source, 0.0) * here[g]
                    partial[k, :, lanes[g]] += jnp.sum(
                        product.reshape(TILE // 8, 8, 128), axis=0
                    )
            for g in range(groups):
                sigma = gate_ref[pl.ds(base, TILE), lanes[g]]
                part = back[g] * sigma
                proj[pl.ds(base, TILE), lanes[g]] = part.astype(BF16)
                far = slice(held + g * 128, held + (g + 1) * 128)
                proj[pl.ds(base, TILE), far] = (
                    part * linear_ref[pl.ds(base, TILE), lanes[g]] * (1.0 - sigma)
                ).astype(BF16)
            return carry

        lax.fori_loop(0, length // TILE, tile, 0)
        terms[:taps, :] = jnp.sum(partial[...], axis=1)
        terms[taps : taps + 1, :] = gain_ref[...]

    return pl.pallas_call(
        kernel,
        out_shape=[
            jax.ShapeDtypeStruct((length, 2 * held), BF16),
            jax.ShapeDtypeStruct((taps + 1, held), F32),
        ],
        scratch_shapes=[
            pltpu.VMEM((length + 2 * PAD, held), F32),
            pltpu.VMEM((taps, 8, held), F32),
            pltpu.VMEM((TILE + 2 * PAD, held), F32),
            pltpu.VMEM((TILE + 2 * PAD, held), F32),
            pltpu.VMEM((TILE + 2 * PAD, 128), jnp.int32),
        ],
        compiler_params=kernel_params(),
        cost_estimate=costs(6.2),
    )(grad_hat, hat, inverse, gated, segments, linear, gate, turned, gain_term, *sums)


def stem_message(turned, parts, small, axis, chains, stem_rows):
    dp_count = lax.axis_size(axis)
    stride, size = chains[-1]
    count, share, width = turned.shape
    channels = parts[0].shape[1]
    rows = dp_count * stem_rows
    own = channels // dp_count
    height = stem_rows + 8

    def kernel(turned_ref, small_ref, *refs):
        outs = refs[count:]
        place = (lax.axis_index(axis) // stride) % size
        total = jnp.zeros((share, channels), F32)
        for k in range(count):
            total = total + jnp.dot(turned_ref[k], refs[k][...], preferred_element_type=F32)
        for i in range(dp_count):
            gain = jnp.concatenate(
                [total[rows : rows + 1, i * own : (i + 1) * own], jnp.zeros((1, channels - own), F32)],
                axis=1,
            )
            block = jnp.concatenate(
                [
                    total[i * stem_rows : (i + 1) * stem_rows],
                    small_ref[i : i + 1, :],
                    gain,
                    jnp.zeros((6, channels), F32),
                ],
                axis=0,
            ).astype(BF16)
            for k in range(size):

                @pl.when(i % size ^ place == k)
                def _():
                    outs[k][i // size] = block

    return pl.pallas_call(
        kernel,
        out_shape=[jax.ShapeDtypeStruct((dp_count // size, height, channels), BF16)] * size,
        compiler_params=kernel_params(),
        cost_estimate=costs(1.2),
    )(turned, small, *parts)


def stem_finish(parts, stem_rows, rows, taps, axis):
    channels = parts[0].shape[2]
    count = len(parts)

    def kernel(*refs):
        stem, kernel_out, post, pre = refs[count:]
        total = sum(jnp.sum(part[...].astype(F32), axis=0) for part in refs[:count])
        stem[...] = total[:stem_rows]
        lane = lax.broadcasted_iota(jnp.int32, (taps + 1, channels), 1)
        tap = lax.broadcasted_iota(jnp.int32, (taps + 1, channels), 0)
        spread = jnp.where(lane // rows == tap, total[stem_rows : stem_rows + 1], 0.0)
        at = lax.broadcasted_iota(jnp.int32, (channels, rows), 0)
        to = lax.broadcasted_iota(jnp.int32, (channels, rows), 1)
        fold = jnp.where(at % rows == to, 1.0, 0.0)
        table = jnp.dot(
            spread, fold, preferred_element_type=F32, precision=lax.Precision.HIGHEST
        )
        kernel_out[...] = table.T[:, :taps]
        post[...] = table[taps : taps + 1]
        mine = lax.axis_index(axis) * rows
        own = jnp.where(at == to + mine, 1.0, 0.0)
        line = jnp.broadcast_to(total[stem_rows + 1 : stem_rows + 2], (8, channels))
        pre[...] = jnp.dot(
            line, own, preferred_element_type=F32, precision=lax.Precision.HIGHEST
        )[:1]

    return pl.pallas_call(
        kernel,
        out_shape=[
            jax.ShapeDtypeStruct((stem_rows, channels), F32),
            jax.ShapeDtypeStruct((rows, taps), F32),
            jax.ShapeDtypeStruct((1, rows), F32),
            jax.ShapeDtypeStruct((1, rows), F32),
        ],
        compiler_params=kernel_params(),
        cost_estimate=costs(1.2),
    )(*parts)


def one_hot(rows, columns):
    return (rows[:, None] == columns[None, :]).astype(BF16)


def order_pieces(mel_pieces, dest_owner, dest_slot, dp_count):
    pieces, piece_values = mel_pieces.shape
    capacity = max(2, 2 * pieces // dp_count)
    matches = (dest_owner[:, None] == jnp.arange(dp_count, dtype=jnp.int32)[None, :]).astype(jnp.int32)
    earlier = jnp.cumsum(matches, axis=0) - matches
    position = dest_owner * capacity + jnp.sum(earlier * matches, axis=1)
    pick = one_hot(jnp.arange(dp_count * capacity, dtype=jnp.int32), position)
    label = jnp.broadcast_to((dest_slot + 1).astype(BF16)[:, None], (pieces, 128))
    return jnp.dot(
        pick, jnp.concatenate([mel_pieces, label], axis=1), preferred_element_type=F32
    ).astype(BF16)


def per_device(
    mel_pieces,
    dest_owner,
    dest_slot,
    segment_ids,
    out_grad,
    stem_weight,
    up_weight,
    down_weight,
    depth_kernel,
    gain_pre,
    gain_post,
):
    dp_count = lax.axis_size("dp")
    tm_count = lax.axis_size("tm")
    chains = stages_of({"dp": dp_count, "tm": tm_count})
    dp_chains, tm_chains = chains["dp"], chains["tm"]
    column = lax.axis_index("tm")
    taps = depth_kernel.shape[1]
    margin = (taps - 1) // 2
    block = out_grad.shape[1]
    channels = out_grad.shape[2]
    held = channels // tm_count
    rows = down_weight.shape[0]
    stem_rows = stem_weight.shape[0]
    features = stem_rows * dp_count * tm_count
    length = block * tm_count

    sums_chains = ((4, 2), (2, 2), (1, 2))

    by_parts = stem_rows % 16 == 0 and rows % 16 == 0 and dp_chains == ((2, 4), (1, 2))
    span = 128 * tm_count
    lane = jnp.arange(span, dtype=jnp.int32)
    grouped = (lane // rows) % tm_count * 128 + lane // (rows * tm_count) * rows + lane % rows
    chunks = rows // stem_rows
    if by_parts:
        up_parts = up_columns(up_weight, rows, tm_count)
        sent, pack = prepare(
            mel_pieces[0], dest_owner[0], dest_slot[0], after(stem_weight, up_parts[0]),
            down_weight, depth_kernel, gain_pre, gain_post, dp_count,
        )
    else:
        sent = order_pieces(mel_pieces[0], dest_owner[0], dest_slot[0], dp_count)
        up_parts = regroup_columns(up_weight, lane, grouped, "tm", tm_count)
        beside = jnp.broadcast_to(jnp.tile(gain_pre, 128 // rows)[None, :], (stem_rows, 128))
        small = jnp.concatenate(
            [depth_kernel, gain_post[:, None], jnp.zeros((rows, 128 - taps - 1), BF16)], axis=1
        )
        folded = [
            value[q : q + stem_rows]
            for value in (small, down_weight)
            for q in range(0, rows, stem_rows)
        ]
        pack = jnp.concatenate([stem_weight, beside] + folded, axis=1)

    up_parts = [up_parts[0]] + [swap(up_parts[k], "tm", k) for k in range(1, tm_count)]
    up_mine = place_parts(up_parts, "tm", 1, tm_count, 0).reshape(tm_count * rows, 2 * held)
    pack_near = gather_stage(pack, "dp", *dp_chains[0], 0)
    up_sides = swap_parts([up_mine] * dp_chains[0][1], "dp", dp_chains[0])
    stem_mine, small_all, down_full = split_rest(
        pack_near, "dp", dp_chains, ((channels + 128, 1), (128, chunks), (channels, chunks))
    )
    stem_mine = stem_mine.reshape(dp_count, stem_rows, channels + 128)
    small_all = small_all.reshape(held, 128)
    down_full = down_full.reshape(held, channels)

    pieces = mel_pieces.shape[1]
    capacity = max(2, 2 * pieces // dp_count)
    arrived = lax.all_to_all(
        after(sent, pack_near, up_sides[1]).reshape(dp_count, capacity, -1),
        "dp",
        split_axis=0,
        concat_axis=0,
        tiled=True,
    ).reshape(dp_count * capacity, -1)
    up_near = place_parts(up_sides, "dp", *dp_chains[0], 0)
    frames = place_frames(after(arrived, up_near), pieces, features)
    frame_parts = gather_parts(frames, "tm", tm_chains)
    stem_parts = gather_parts(stem_mine, "tm", tm_chains, frames)
    frames = place_parts(frame_parts, "tm", 1, tm_count, 0).reshape(length, features)
    stem_all = place_parts(stem_parts, "tm", 1, tm_count, 1)
    stem_all = stem_all.reshape(features, channels + 128)

    grad_out = out_grad[0]
    grad_first = after(grad_out, stem_parts[2])
    hierarchical = list(tm_chains) == [(2, 2), (1, 2)]
    if hierarchical:
        grad_parts = [grad_first, swap(grad_first, "tm", 1), swap(grad_first, "tm", 2)]
    else:
        grad_parts = gather_parts(grad_first, "tm", tm_chains)

    segments = jnp.pad(segment_ids[0], (PAD, PAD), constant_values=-1)
    segments = jnp.broadcast_to(segments[:, None], (length + 2 * PAD, 128))

    extra = 16
    normed, stem_pre, gain_one, frames_turned = stem_forward(
        frames, stem_all, tm_count, "tm", rows, extra
    )
    up_full = gather_rest(up_near, "dp", dp_chains).reshape(channels, 2 * held)
    grad_parts = lax.optimization_barrier((grad_parts, normed))[0]
    if hierarchical:
        grad_parts = grad_parts + [swap(grad_parts[2], "tm", 1)]
    linear, gate_sig, gated = up_forward(normed, up_full)
    conv, stats, turned = conv_forward(gated, small_all, segments, taps)
    stats = swap_all(stats, "tm")
    grad_parts = lax.optimization_barrier((grad_parts, conv))[0]
    grad_out_all = place_parts(grad_parts, "tm", 1, tm_count, 0).reshape(length, channels)
    grad_act = lax.dot_general(
        grad_out_all, down_full, (((1,), (1,)), ((), ())), preferred_element_type=F32
    )
    activated, conv_hat, grad_hat, inverse, sums, gain_post_term = activate(
        conv, stats, turned, grad_act, taps
    )
    sums = swap_all(sums, "tm")
    if by_parts:
        down_terms = part_terms(activated, grad_out_all, False, "dp", sums_chains)
        normed_turned = turn(normed)
        grad_hat = after(grad_hat, normed_turned)
    else:
        down_terms = [message_terms(activated, grad_out_all, dp_count, tm_count)]
    down_terms = lax.optimization_barrier((down_terms, *sums))[0]
    if by_parts:
        down_parts = swap_parts(down_terms, "dp", sums_chains[-1])

    grad_hat = after(grad_hat, *down_terms)
    grad_proj, kernel_term = conv_backward(
        grad_hat, conv_hat, inverse, sums, gated, segments, linear, gate_sig, turned, taps,
        gain_post_term,
    )

    own_terms, *other_terms = block_terms(
        after(grad_proj, *down_parts[1:]) if by_parts else grad_proj, up_full, True, "tm", tm_count
    )
    if by_parts:
        up_terms = part_terms(
            after(normed_turned, *other_terms), grad_proj, True, "dp", sums_chains
        )
        up_parts = swap_parts(up_terms, "dp", sums_chains[-1])
    else:
        up_terms = [message_terms(normed, grad_proj, dp_count, tm_count)]
    grad_far, grad_parts, grad_passed = block_sum(other_terms, "tm", tm_chains, up_terms[-1])
    small_term = after(kernel_term, grad_passed)
    small_term = small_term.reshape(taps + 1, dp_count, rows).transpose(1, 0, 2)
    small_term = small_term.reshape(dp_count, (taps + 1) * rows)
    small_term = jnp.pad(small_term, ((0, 0), (0, channels - (taps + 1) * rows)))
    y_own, *y_others = block_terms(
        after(activated, grad_passed), down_full, False, "tm", tm_count
    )
    grad_stem_pre = stem_backward(
        own_terms, grad_parts + [grad_far], stem_pre, grad_out, gain_one, extra
    )
    if by_parts:
        up_parts = join_parts(
            [after(up_parts[0], grad_stem_pre)] + up_parts[1:], down_parts, "dp", sums_chains[1]
        )
        grad_stem_parts = gather_parts(grad_stem_pre, "tm", tm_chains, up_parts[-1])
        up_parts = reduce_rest(up_parts, "dp", sums_chains[:2])
    else:
        grad_stem_parts = gather_parts(grad_stem_pre, "tm", tm_chains)
    y_far, y_parts, _ = block_sum(y_others, "tm", tm_chains, grad_stem_parts[2])
    if by_parts:
        stem_terms = stem_message(
            frames_turned, grad_stem_parts, small_term, "dp", sums_chains, stem_rows
        )
        stem_sums = reduce_rest(stem_terms, "dp", sums_chains)
    else:
        stem_sum = sum(
            jnp.dot(frames_turned[k], grad_stem_parts[k], preferred_element_type=F32)
            for k in range(tm_count)
        )
        share = features // tm_count
        gain_term = stem_sum[share].reshape(dp_count, 1, tm_count * rows)
        gain_term = jnp.pad(gain_term, ((0, 0), (0, 0), (0, channels - tm_count * rows)))
        stem_terms = stem_sum[:share].reshape(dp_count, stem_rows, channels)
        stem_terms = jnp.concatenate([stem_terms, small_term[:, None, :], gain_term], axis=1)
        stem_terms = jnp.pad(stem_terms.astype(BF16), ((0, 0), (0, 6), (0, 0)))
        stem_sums = [
            lax.all_to_all(stem_terms, "dp", split_axis=0, concat_axis=0, tiled=True)
        ]
    if by_parts:
        up_parts = cut_columns([after(up_parts[0], *stem_terms)] + up_parts[1:], "tm", tm_count * rows, rows)
        up_parts = swap_all_parts(up_parts, "tm")
        grad_up, grad_down = mix_columns(up_parts, "tm", tm_count * rows, rows)
    else:
        down_sums = lax.all_to_all(
            down_terms[0], ("dp", "tm"), split_axis=0, concat_axis=0, tiled=True
        )
        grad_down = jnp.sum(
            down_sums.reshape(dp_count, tm_count * rows, held).astype(F32), axis=0
        )
        up_sums = lax.all_to_all(
            up_terms[0], ("dp", "tm"), split_axis=0, concat_axis=0, tiled=True
        )
        up_sums = up_sums.reshape(dp_count, tm_count, tm_count * rows, 128)
        spread = one_hot(lane, grouped).reshape(tm_count, 128, span)
        grad_up = jnp.einsum("ijab,jbc->ac", up_sums, spread, preferred_element_type=F32)
    y_out = finish_rows(stem_pre, y_own, y_parts + [y_far])
    grad_stem, grad_kernel, grad_gain_post, grad_gain_pre = stem_finish(
        stem_sums, stem_rows, rows, taps, "tm"
    )
    grad_gain_post, grad_gain_pre = grad_gain_post[0], grad_gain_pre[0]
    return (y_out[None], grad_stem, grad_up, grad_down, grad_kernel, grad_gain_pre, grad_gain_post)


def solution(mesh):
    return jax.shard_map(
        per_device,
        mesh=mesh,
        in_specs=(
            P("dp", "tm", None),
            P("dp", "tm"),
            P("dp", "tm"),
            P("dp", None),
            P("dp", "tm", None),
            P(("dp", "tm"), None),
            P(("dp", "tm"), None),
            P(("dp", "tm"), None),
            P(("dp", "tm"), None),
            P(("dp", "tm")),
            P(("dp", "tm")),
        ),
        out_specs=(
            P("dp", "tm", None),
            P(("dp", "tm"), None),
            P("dp", "tm"),
            P("dp", "tm"),
            P(("dp", "tm"), None),
            P(("dp", "tm")),
            P(("dp", "tm")),
        ),
        check_vma=False,
    )
```

```python
import jax
import jax.numpy as jnp
from jax import lax
from jax.experimental import pallas as pl
from jax.experimental.pallas import tpu as pltpu
from jax.sharding import PartitionSpec as P

NORM_EPS = 1e-05
BF16 = jnp.bfloat16
F32 = jnp.float32


def stages_of(sizes):
    if sizes["dp"] == 8 and sizes["tm"] == 4:
        return {"dp": ((2, 4), (1, 2)), "tm": ((2, 2), (1, 2))}
    if sizes["dp"] == 64 and sizes["tm"] == 4:
        return {"dp": ((8, 8), (2, 4), (1, 2)), "tm": ((1, 4),)}
    return {axis: ((1, size),) for axis, size in sizes.items()}


def swap(value, axis, mask):
    size = lax.axis_size(axis)
    return lax.ppermute(value, axis, [(i, i ^ mask) for i in range(size)])


VMEM_LIMIT = 16 << 20


def kernel_params():
    return pltpu.CompilerParams(vmem_limit_bytes=VMEM_LIMIT)


def costs(microseconds):
    return pl.CostEstimate(
        flops=int(microseconds * 2e10), bytes_accessed=1 << 16, transcendentals=0
    )


def after(value, *others):
    return lax.optimization_barrier((value,) + others)[0]


def place_parts(parts, axis, stride, size, dim):
    shape = parts[0].shape
    out_shape = shape[:dim] + (size,) + shape[dim:]

    def kernel(*refs):
        place = (lax.axis_index(axis) // stride) % size
        for k in range(size):
            refs[size][(slice(None),) * dim + (place ^ k,)] = refs[k][...]

    return pl.pallas_call(
        kernel,
        out_shape=jax.ShapeDtypeStruct(out_shape, parts[0].dtype),
        compiler_params=kernel_params(),
        cost_estimate=costs(0.8),
    )(*parts)


def gather_stage(value, axis, stride, size, dim):
    parts = [value] + [swap(value, axis, k * stride) for k in range(1, size)]
    return place_parts(parts, axis, stride, size, dim)


def gather_rest(value, axis, chains):
    shape = value.shape[1:]
    for dim, (stride, size) in enumerate(chains[1:], 1):
        value = gather_stage(value, axis, stride, size, dim)
    return value.reshape((-1,) + shape)


def block_terms(left, right, transposed, axis, count):
    block = left.shape[0] // count
    width = right.shape[0] if transposed else right.shape[1]
    dims = (((1,), (1 if transposed else 0,)), ((), ()))

    def kernel(left_ref, right_ref, own, *refs):
        others, terms = refs[:-1], refs[-1]
        place = lax.axis_index(axis)
        terms[...] = lax.dot_general(
            left_ref[...], right_ref[...], dims, preferred_element_type=F32
        )
        for k in range(count):
            start = pl.multiple_of((place ^ k) * block, block)
            if k == 0:
                own[...] = terms[pl.ds(start, block), :]
            else:
                others[k - 1][...] = terms[pl.ds(start, block), :].astype(BF16)

    return pl.pallas_call(
        kernel,
        out_shape=[jax.ShapeDtypeStruct((block, width), F32)]
        + [jax.ShapeDtypeStruct((block, width), BF16)] * (count - 1),
        scratch_shapes=[pltpu.VMEM((count * block, width), F32)],
        compiler_params=kernel_params(),
        cost_estimate=costs(1.2),
    )(left, right)


def block_sum(others, axis, chains, first=None):
    if list(chains) == [(2, 2), (1, 2)]:
        near, passed = swap(others[0], axis, 1), swap(others[2], axis, 1)
        passed = add_pair(others[1], passed)
        if first is not None:
            passed = after(passed, first)
        return swap(passed, axis, 2), [near], passed
    parts = [swap(other, axis, k) for k, other in enumerate(others, 1)]
    return parts[-1], parts[:-1], others[-1]


def add_pair(one, other):
    def kernel(one_ref, other_ref, out):
        out[...] = (one_ref[...].astype(F32) + other_ref[...].astype(F32)).astype(BF16)

    return pl.pallas_call(
        kernel,
        out_shape=jax.ShapeDtypeStruct(one.shape, BF16),
        compiler_params=kernel_params(),
        cost_estimate=costs(0.5),
    )(one, other)


def finish_rows(stem_pre, own, parts):
    def kernel(pre_ref, own_ref, *refs):
        total = own_ref[...]
        for part in refs[:-1]:
            total = total + part[...].astype(F32)
        pre = pre_ref[...]
        stem_out = (pre * jax.nn.sigmoid(pre)).astype(BF16).astype(F32)
        refs[-1][...] = (stem_out + total).astype(BF16)

    return pl.pallas_call(
        kernel,
        out_shape=jax.ShapeDtypeStruct(own.shape, BF16),
        compiler_params=kernel_params(),
        cost_estimate=costs(0.6),
    )(stem_pre, own, *parts)


def turn(value):
    rows, columns = value.shape

    def kernel(source, out):
        for c in range(0, columns, 128):
            out[c : c + 128, :] = source[:, c : c + 128].astype(F32).T.astype(BF16)

    return pl.pallas_call(
        kernel,
        out_shape=jax.ShapeDtypeStruct((columns, rows), value.dtype),
        compiler_params=kernel_params(),
        cost_estimate=costs(1.0),
    )(value)


def part_terms(left, right, turned, axis, chains):
    total = lax.axis_size(axis)
    stride, size = chains[-1]
    rows, columns = left.shape[0 if turned else 1] // total, right.shape[1]
    step = max(1, 512 // rows) if turned else max(1, 128 // rows)

    def kernel(left_ref, right_ref, *outs):
        place = (lax.axis_index(axis) // stride) % size
        for i in range(0, total, step):
            block = slice(i * rows, (i + step) * rows)
            if turned:
                term = jnp.dot(left_ref[block, :], right_ref[...], preferred_element_type=F32)
            else:
                term = lax.dot_general(
                    left_ref[:, block],
                    right_ref[...],
                    (((0,), (0,)), ((), ())),
                    preferred_element_type=F32,
                )
            term = term.astype(BF16)
            for n in range(step):
                for k in range(size):

                    @pl.when((i + n) % size ^ place == k)
                    def _():
                        outs[k][(i + n) // size] = term[n * rows : (n + 1) * rows]

    return pl.pallas_call(
        kernel,
        out_shape=[jax.ShapeDtypeStruct((total // size, rows, columns), BF16)] * size,
        compiler_params=kernel_params(),
        cost_estimate=costs(1.5),
    )(left, right)


def swap_all_parts(parts, axis):
    return [parts[0]] + [swap(part, axis, k) for k, part in enumerate(parts[1:], 1)]


def swap_parts(parts, axis, chain):
    stride, _ = chain
    return [parts[0]] + [swap(part, axis, k * stride) for k, part in enumerate(parts[1:], 1)]


def add_parts(parts, axis, chain):
    stride, size = chain
    shape = (parts[0].shape[0] // size,) + parts[0].shape[1:]

    def kernel(*refs):
        place = (lax.axis_index(axis) // stride) % size
        for a in range(shape[0]):
            for k in range(size):
                at = a * size + (place ^ k)
                total = sum(part[at].astype(F32) for part in refs[: len(parts)])
                refs[len(parts) + k][a] = total.astype(BF16)

    return pl.pallas_call(
        kernel,
        out_shape=[jax.ShapeDtypeStruct(shape, BF16)] * size,
        compiler_params=kernel_params(),
        cost_estimate=costs(0.6),
    )(*parts)


def reduce_rest(parts, axis, chains):
    parts = swap_parts(parts, axis, chains[-1])
    for chain in reversed(chains[:-1]):
        parts = swap_parts(add_parts(parts, axis, chain), axis, chain)
    return parts


def cut_columns(first, second, axis):
    count = lax.axis_size(axis)
    terms = len(first)
    _, rows, columns = first[0].shape
    _, below, wide = second[0].shape
    share = columns // count
    folds = wide // columns

    def kernel(*refs):
        place = lax.axis_index(axis)
        upper = sum(part[0].astype(F32) for part in refs[:terms]).astype(BF16)
        lower = sum(part[0].astype(F32) for part in refs[terms : 2 * terms]).astype(BF16)
        for j in range(count):
            for k in range(count):

                @pl.when(place ^ j == k)
                def _():
                    out = refs[2 * terms + k]
                    out[:rows, :] = upper[:, j * share : (j + 1) * share]
                    for f in range(folds):
                        start = (j * folds + f) * share
                        out[rows + f * below : rows + (f + 1) * below, :] = lower[
                            :, start : start + share
                        ]

    return pl.pallas_call(
        kernel,
        out_shape=[jax.ShapeDtypeStruct((rows + folds * below, share), BF16)] * count,
        compiler_params=kernel_params(),
        cost_estimate=costs(0.6),
    )(*first, *second)


def mix_columns(parts, axis, rows, small):
    count = len(parts)
    height, share = parts[0].shape
    span = share * count
    folds = (height - rows) // small

    def kernel(*refs):
        place = lax.axis_index(axis)
        upper, lower = refs[count:]
        at, to = iota((share, span), 0), iota((share, span), 1)
        total = jnp.zeros((rows, span), F32)
        for k in range(count):
            want = at // small * (small * count) + (place ^ k) * small + at % small
            spread = table(to == want)
            total = total + jnp.dot(refs[k][:rows, :], spread, preferred_element_type=F32)
            start = pl.multiple_of((place ^ k) * small, small)
            for f in range(folds):
                lower[pl.ds(start, small), f * share : (f + 1) * share] = refs[k][
                    rows + f * small : rows + (f + 1) * small, :
                ].astype(F32)
        upper[...] = total

    return pl.pallas_call(
        kernel,
        out_shape=[
            jax.ShapeDtypeStruct((rows, span), F32),
            jax.ShapeDtypeStruct((count * small, folds * share), F32),
        ],
        compiler_params=kernel_params(),
        cost_estimate=costs(0.8),
    )(*parts)


def message_terms(left, right, parts, sides):
    rows, columns = left.shape[1] // parts, right.shape[1] // sides
    terms = jnp.dot(left.T, right, preferred_element_type=F32).astype(BF16)
    terms = terms.reshape(parts, rows, sides, columns).transpose(0, 2, 1, 3)
    return terms.reshape(parts * sides, rows, columns)


def regroup_columns(weight, lane, grouped, axis, count):
    rows, columns = weight.shape
    span = lane.shape[0]
    groups = columns // span
    parts = jnp.dot(
        weight.reshape(rows * groups, span), one_hot(grouped, lane), preferred_element_type=F32
    ).astype(BF16)
    parts = parts.reshape(rows, groups, count, 128).transpose(2, 0, 1, 3)
    parts = parts.reshape(count, rows, groups * 128)
    return [
        lax.dynamic_index_in_dim(parts, lax.axis_index(axis) ^ k, 0, keepdims=False)
        for k in range(count)
    ]


def stem_backward(own, parts, stem_pre, grad_out, gain, extra):
    block, channels = own.shape

    def kernel(own_ref, pre_ref, out_grad_ref, gain_ref, *refs):
        out = refs[-1]
        pre = pre_ref[...]
        sigma = jax.nn.sigmoid(pre)
        hat, inverse = standardize((pre * sigma).astype(BF16).astype(F32))
        grad = own_ref[...]
        for part in refs[:-1]:
            grad = grad + part[...].astype(F32)
        out[block:, :] = jnp.concatenate(
            [jnp.sum(grad * hat, axis=0, keepdims=True), jnp.zeros((extra - 1, channels), F32)]
        ).astype(BF16)
        back = grad * gain_ref[...]
        first = jnp.mean(back, axis=-1, keepdims=True)
        second = jnp.mean(back * hat, axis=-1, keepdims=True)
        stem_out = out_grad_ref[...].astype(F32) + (back - first - hat * second) * inverse
        out[:block, :] = (stem_out * (sigma * (1.0 + pre * (1.0 - sigma)))).astype(BF16)

    return pl.pallas_call(
        kernel,
        out_shape=jax.ShapeDtypeStruct((block + extra, channels), BF16),
        compiler_params=kernel_params(),
        cost_estimate=costs(0.7),
    )(own, stem_pre, grad_out, gain, *parts)


def standardize(values):
    centered = values - jnp.mean(values, axis=-1, keepdims=True)
    inverse = lax.rsqrt(jnp.mean(centered * centered, axis=-1, keepdims=True) + NORM_EPS)
    return (centered * inverse, inverse)


def gather_parts(value, axis, chains, first=None):
    if list(chains) == [(2, 2), (1, 2)]:
        far = swap(value, axis, 2)
        if first is not None:
            far = after(far, first)
        return [value, swap(value, axis, 1), far, swap(far, axis, 1)]
    return [value] + [swap(value, axis, k) for k in range(1, lax.axis_size(axis))]


def swap_all(value, axis):
    return [value] + [swap(value, axis, k) for k in range(1, lax.axis_size(axis))]


def split_parts(parts, axis, stride, size, dim, cuts):
    shape = parts[0].shape
    lead = shape[:dim] + (size,) + shape[dim:-2]
    rows = shape[-2]

    def kernel(*refs):
        place = (lax.axis_index(axis) // stride) % size
        inner = (slice(None),) * (len(lead) - dim - 1)
        for k in range(size):
            target = (slice(None),) * dim + (place ^ k,) + inner
            start = 0
            for n, (width, pieces) in enumerate(cuts):
                for q in range(pieces):
                    refs[size + n][target + (q,)] = refs[k][..., start : start + width]
                    start += width

    return pl.pallas_call(
        kernel,
        out_shape=[
            jax.ShapeDtypeStruct(lead + (pieces, rows, width), parts[0].dtype)
            for width, pieces in cuts
        ],
        compiler_params=kernel_params(),
        cost_estimate=costs(1.0),
    )(*parts)


def split_rest(value, axis, chains, cuts):
    for dim, (stride, size) in enumerate(chains[1:], 1):
        parts = [value] + [swap(value, axis, k * stride) for k in range(1, size)]
        if dim == len(chains) - 1:
            return split_parts(parts, axis, stride, size, dim, cuts)
        value = place_parts(parts, axis, stride, size, dim)


def iota(shape, dim):
    return lax.broadcasted_iota(jnp.int32, shape, dim)


def table(flags):
    return jnp.where(flags, 1.0, 0.0).astype(BF16)


def fetch(sources, held, sems):
    copies = [
        pltpu.make_async_copy(source, target, sems.at[k])
        for k, (source, target) in enumerate(zip(sources, held))
    ]
    for copy in copies:
        copy.start()
    for copy in copies:
        copy.wait()


def fetching_call(kernel, inputs, out_shape, cost):
    return pl.pallas_call(
        kernel,
        out_shape=out_shape,
        in_specs=[pl.BlockSpec(memory_space=pl.ANY)] * len(inputs),
        scratch_shapes=[pltpu.VMEM(value.shape, value.dtype) for value in inputs]
        + [pltpu.SemaphoreType.DMA((len(inputs),))],
        cost_estimate=cost,
    )(*inputs)


def up_columns(up, rows, tm_count):
    span = 128 * tm_count
    groups = up.shape[1] // span

    def kernel(source, *refs):
        up_parts, (up_ref, sems) = refs[:tm_count], refs[tm_count:]
        fetch([source], [up_ref], sems)
        place = lax.axis_index("tm")
        at, to = iota((span, 128), 0), iota((span, 128), 1)
        for k in range(tm_count):
            want = to // rows * (rows * tm_count) + (place ^ k) * rows + to % rows
            pick = table(at == want)
            for g in range(groups):
                up_parts[k][:, g * 128 : (g + 1) * 128] = jnp.dot(
                    up_ref[:, g * span : (g + 1) * span], pick, preferred_element_type=F32
                ).astype(BF16)

    return fetching_call(
        kernel,
        (up,),
        [jax.ShapeDtypeStruct((rows, up.shape[1] // tm_count), BF16)] * tm_count,
        costs(1.5),
    )


def prepare(mel, owner, slot, stem, down, taps, gain_one, gain_two, dp_count):
    pieces, values = mel.shape
    capacity = max(2, 2 * pieces // dp_count)
    slots = dp_count * capacity
    stem_rows, channels = stem.shape
    rows, tap_count = taps.shape
    chunks = rows // stem_rows
    beyond = channels + 128 * (chunks + 1)
    inputs = (
        stem, taps, gain_one[None, :], gain_two[None, :], owner[None, :], slot[None, :], mel, down
    )
    count = len(inputs)

    def kernel(*refs):
        sent, pack = refs[count : count + 2]
        held = refs[count + 2 : -1]
        fetch(refs[:count], held, refs[-1])
        stem_ref, taps_ref, one_ref, two_ref, owner_ref, slot_ref, mel_ref, down_ref = held
        pack[:, :channels] = stem_ref[...]
        lane = iota((rows, 128), 1)
        spread = table(lane % rows == iota((rows, 128), 0))
        gain = jnp.broadcast_to(one_ref[...].astype(F32), (stem_rows, rows)).astype(BF16)
        pack[:, channels : channels + 128] = jnp.dot(
            gain, spread, preferred_element_type=F32
        ).astype(BF16)
        tap_lane = table(iota((tap_count, 128), 1) == iota((tap_count, 128), 0))
        square = iota((rows, rows), 0) == iota((rows, rows), 1)
        diagonal = jnp.where(
            square, jnp.broadcast_to(two_ref[...].astype(F32), (rows, rows)), 0.0
        ).astype(BF16)
        small = jnp.dot(taps_ref[...], tap_lane, preferred_element_type=F32)
        small = small + jnp.dot(diagonal, table(lane == tap_count), preferred_element_type=F32)
        for q in range(chunks):
            lanes = slice(channels + 128 * (q + 1), channels + 128 * (q + 2))
            pack[:, lanes] = small[q * stem_rows : (q + 1) * stem_rows].astype(BF16)
            lanes = slice(beyond + channels * q, beyond + channels * (q + 1))
            pack[:, lanes] = down_ref[q * stem_rows : (q + 1) * stem_rows, :]

        owners = jnp.broadcast_to(owner_ref[...].astype(F32), (pieces, pieces))
        earlier = iota((pieces, pieces), 0) < iota((pieces, pieces), 1)
        same = jnp.where(owners.T == owners, jnp.where(earlier, 1.0, 0.0), 0.0)
        target = owners[:1] * float(capacity) + jnp.sum(same, axis=0, keepdims=True)
        target = jnp.broadcast_to(target, (slots, pieces)).astype(jnp.int32)
        chosen = target == iota((slots, pieces), 0)
        pick = table(chosen)
        sent[:, :values] = jnp.dot(pick, mel_ref[...], preferred_element_type=F32).astype(BF16)
        labels = jnp.broadcast_to(slot_ref[...].astype(F32) + 1.0, (slots, pieces))
        label = jnp.sum(jnp.where(chosen, labels, 0.0), axis=1, keepdims=True)
        sent[:, values:] = jnp.broadcast_to(label, (slots, 128)).astype(BF16)

    return fetching_call(
        kernel,
        inputs,
        [
            jax.ShapeDtypeStruct((slots, values + 128), BF16),
            jax.ShapeDtypeStruct((stem_rows, beyond + channels * chunks), BF16),
        ],
        costs(2.0),
    )


def place_frames(arrived, pieces, features):
    slots, width = arrived.shape
    steps = (width - 128) // features

    def kernel(arrived_ref, out):
        labels = arrived_ref[:, steps * features :].astype(F32).T[:1]
        want = jnp.broadcast_to(labels, (pieces * steps, slots)).astype(jnp.int32)
        row = lax.broadcasted_iota(jnp.int32, (pieces * steps, slots), 0)
        total = jnp.zeros((pieces * steps, features), F32)
        for q in range(steps):
            put = jnp.where(row == (want - 1) * steps + q, 1.0, 0.0).astype(BF16)
            total = total + jnp.dot(
                put, arrived_ref[:, q * features : (q + 1) * features], preferred_element_type=F32
            )
        out[...] = total.astype(BF16)

    return pl.pallas_call(
        kernel,
        out_shape=jax.ShapeDtypeStruct((pieces * steps, features), BF16),
        compiler_params=kernel_params(),
        cost_estimate=costs(0.6),
    )(arrived)


def stem_forward(frames, stem_all, count, axis, rows, extra):
    length = frames.shape[0]
    features, width = stem_all.shape
    channels = width - 128
    block = length // count
    stem_rows = features * rows // channels
    share = features // count

    def kernel(frames_ref, stem_ref, normed, pre_own, gain_out, turned):
        place = lax.axis_index(axis)
        feature = lax.broadcasted_iota(jnp.int32, (features, share), 0)
        chosen = lax.broadcasted_iota(jnp.int32, (features, share), 1)
        chosen = (chosen // stem_rows * count + place) * stem_rows + chosen % stem_rows
        pick = jnp.where(feature == chosen, 1.0, 0.0).astype(BF16)
        corner = lax.broadcasted_iota(jnp.int32, (extra, extra), 0)
        corner = corner + lax.broadcasted_iota(jnp.int32, (extra, extra), 1)
        corner = jnp.where(corner == 0, 1.0, 0.0).astype(BF16)
        for k in range(count):
            start = pl.multiple_of((place ^ k) * block, block)
            turned[k, :share, :block] = lax.dot_general(
                pick,
                frames_ref[pl.ds(start, block), :],
                (((0,), (1,)), ((), ())),
                preferred_element_type=F32,
            ).astype(BF16)
            turned[k, share:, :block] = jnp.zeros((extra, block), BF16)
            turned[k, :share, block:] = jnp.zeros((share, extra), BF16)
            turned[k, share:, block:] = corner
        beside = stem_ref[:, channels:].astype(F32)
        gains = []
        for g in range(channels // 128):
            row = lax.broadcasted_iota(jnp.int32, (features, 128), 0)
            lane = lax.broadcasted_iota(jnp.int32, (features, 128), 1) + g * 128
            gains.append(
                jnp.sum(
                    jnp.where(row == lane // rows * stem_rows, beside, 0.0), axis=0, keepdims=True
                )
            )
        gain_out[...] = jnp.concatenate(gains, axis=1)
        for b in range(count):
            pre = jnp.dot(
                frames_ref[b * block : (b + 1) * block, :],
                stem_ref[:, :channels],
                preferred_element_type=F32,
            )
            hat, _ = standardize((pre * jax.nn.sigmoid(pre)).astype(BF16).astype(F32))
            normed[b * block : (b + 1) * block, :] = (hat * gain_out[...]).astype(BF16)

            @pl.when(place == b)
            def _():
                pre_own[...] = pre

    return pl.pallas_call(
        kernel,
        out_shape=[
            jax.ShapeDtypeStruct((length, channels), BF16),
            jax.ShapeDtypeStruct((block, channels), F32),
            jax.ShapeDtypeStruct((1, channels), F32),
            jax.ShapeDtypeStruct((count, share + extra, block + extra), BF16),
        ],
        compiler_params=kernel_params(),
        cost_estimate=costs(2.8),
    )(frames, stem_all)


PAD = 16


def up_forward(normed, up):
    length = normed.shape[0]
    held = up.shape[1] // 2
    step = min(128, length)

    def kernel(normed_ref, up_ref, linear, gate, gated):
        edge = jnp.zeros((PAD, held), F32)
        gated[:PAD, :] = edge
        gated[PAD + length :, :] = edge
        for b in range(0, length, step):
            proj = jnp.dot(normed_ref[b : b + step, :], up_ref[...], preferred_element_type=F32)
            sigma = jax.nn.sigmoid(proj[:, held:])
            linear[b : b + step, :] = proj[:, :held]
            gate[b : b + step, :] = sigma
            gated[PAD + b : PAD + b + step, :] = (proj[:, :held] * sigma).astype(BF16).astype(F32)

    return pl.pallas_call(
        kernel,
        out_shape=[
            jax.ShapeDtypeStruct((length, held), F32),
            jax.ShapeDtypeStruct((length, held), F32),
            jax.ShapeDtypeStruct((length + 2 * PAD, held), F32),
        ],
        compiler_params=kernel_params(),
        cost_estimate=costs(0.7),
    )(normed, up)


def columns_of(first, second):
    rows = first.shape[0]
    lane = lax.broadcasted_iota(jnp.int32, (rows, 128), 1)
    both = jnp.where(lane == 0, first, jnp.where(lane == 1, second, 0.0))
    return both.T[:8]


def rows_of(table):
    rows = table.shape[1]
    turned = jnp.concatenate([table, jnp.zeros((120, rows), F32)], axis=0).T
    return turned[:, :1], turned[:, 1:2]


def spread_segments(segments):
    length = segments.shape[1]

    def kernel(source, out):
        edge = jnp.full((PAD, 128), -1.0, F32)
        out[:PAD, :] = edge
        out[PAD + length :, :] = edge
        out[PAD : PAD + length, :] = jnp.broadcast_to(
            source[...].astype(F32), (128, length)
        ).T

    return pl.pallas_call(
        kernel,
        out_shape=jax.ShapeDtypeStruct((length + 2 * PAD, 128), F32),
        compiler_params=kernel_params(),
        cost_estimate=costs(0.5),
    )(segments)


def multiply_turned(left, right):
    def kernel(left_ref, right_ref, out):
        out[...] = lax.dot_general(
            left_ref[...], right_ref[...], (((1,), (1,)), ((), ())), preferred_element_type=F32
        )

    return pl.pallas_call(
        kernel,
        out_shape=jax.ShapeDtypeStruct((left.shape[0], right.shape[0]), F32),
        compiler_params=kernel_params(),
        cost_estimate=costs(0.6),
    )(left, right)


TILE = 64


def conv_forward(gated, small, segments, taps):
    length, held = gated.shape[0] - 2 * PAD, gated.shape[1]
    margin = (taps - 1) // 2

    def kernel(gated_ref, small_ref, seg_ref, conv, stats, turned, gated_near, seg_near):
        turned[...] = small_ref[...].astype(F32).T

        def tile(t, carry):
            base = pl.multiple_of(t * TILE, TILE)
            gated_near[...] = gated_ref[pl.ds(base, TILE + 2 * PAD), :]
            seg_near[...] = seg_ref[pl.ds(base, TILE + 2 * PAD), :]
            centre = seg_near[PAD : PAD + TILE, :]
            sums = [jnp.zeros((TILE, 128), F32) for _ in range(held // 128)]
            for k in range(taps):
                shift = PAD + k - margin
                inside = seg_near[shift : shift + TILE, :] == centre
                for g in range(held // 128):
                    lanes = slice(g * 128, (g + 1) * 128)
                    value = gated_near[shift : shift + TILE, lanes]
                    sums[g] = sums[g] + jnp.where(inside, value, 0.0) * turned[k : k + 1, lanes]
            conv[pl.ds(base, TILE), :] = jnp.concatenate(sums, axis=1)
            return carry

        lax.fori_loop(0, length // TILE, tile, 0)
        value = conv[...]
        mean = jnp.mean(value, axis=-1, keepdims=True)
        centered = value - mean
        stats[...] = columns_of(mean, jnp.sum(centered * centered, axis=-1, keepdims=True))

    return pl.pallas_call(
        kernel,
        out_shape=[
            jax.ShapeDtypeStruct((length, held), F32),
            jax.ShapeDtypeStruct((8, length), F32),
            jax.ShapeDtypeStruct((128, held), F32),
        ],
        scratch_shapes=[
            pltpu.VMEM((TILE + 2 * PAD, held), F32),
            pltpu.VMEM((TILE + 2 * PAD, 128), F32),
        ],
        compiler_params=kernel_params(),
        cost_estimate=costs(3.0),
    )(gated, small, segments)


def activate(conv, stats, turned, grad_act, taps):
    length, held = conv.shape
    count = len(stats)

    def kernel(conv_ref, turned_ref, grad_ref, *refs):
        tables, (active, hat_out, grad_hat_out, inverse_out, sums, gain_term) = (
            refs[:count], refs[count:],
        )
        means = [table[0:1, :] for table in tables]
        mean = sum(means) * (1.0 / count)
        squares = sum(table[1:2, :] for table in tables)
        squares = squares + held * sum((one - mean) * (one - mean) for one in means)
        inverse = lax.rsqrt(squares * (1.0 / (held * count)) + NORM_EPS)
        both = jnp.concatenate([mean, inverse, jnp.zeros((6, length), F32)], axis=0)
        mean, inverse = rows_of(both)
        inverse_out[...] = jnp.broadcast_to(inverse, (length, 128))
        gain = turned_ref[taps : taps + 1, :]
        hat = (conv_ref[...] - mean) * inverse
        scaled = hat * gain
        sigma = jax.nn.sigmoid(scaled)
        active[...] = (scaled * sigma).astype(BF16)
        grad_scaled = grad_ref[...] * (sigma * (1.0 + scaled * (1.0 - sigma)))
        gain_term[...] = jnp.sum(grad_scaled * hat, axis=0, keepdims=True)
        grad_hat = grad_scaled * gain
        hat_out[...] = hat
        grad_hat_out[...] = grad_hat
        sums[...] = columns_of(
            jnp.sum(grad_hat, axis=-1, keepdims=True),
            jnp.sum(grad_hat * hat, axis=-1, keepdims=True),
        )

    return pl.pallas_call(
        kernel,
        out_shape=[
            jax.ShapeDtypeStruct((length, held), BF16),
            jax.ShapeDtypeStruct((length, held), F32),
            jax.ShapeDtypeStruct((length, held), F32),
            jax.ShapeDtypeStruct((length, 128), F32),
            jax.ShapeDtypeStruct((8, length), F32),
            jax.ShapeDtypeStruct((1, held), F32),
        ],
        compiler_params=kernel_params(),
        cost_estimate=costs(0.7),
    )(conv, turned, grad_act, *stats)


def conv_backward(grad_hat, hat, inverse, sums, gated, segments, linear, gate, turned, taps, gain_term):
    length, held = hat.shape
    count = len(sums)
    margin = (taps - 1) // 2
    groups = held // 128

    def kernel(
        grad_ref, hat_ref, inverse_ref, gated_ref, seg_ref, linear_ref, gate_ref, turned_ref,
        gain_ref, *refs
    ):
        tables, (proj, terms), (grad_conv, partial, grad_near, gated_near, seg_near) = (
            refs[:count], refs[count : count + 2], refs[count + 2 :],
        )
        total = sum(table[...] for table in tables) * (1.0 / (held * count))
        first, second = rows_of(total)
        edge = jnp.zeros((PAD, held), F32)
        grad_conv[:PAD, :] = edge
        grad_conv[PAD + length :, :] = edge
        value = (grad_ref[...] - first - hat_ref[...] * second) * inverse_ref[:, :1]
        grad_conv[PAD : PAD + length, :] = value.astype(BF16).astype(F32)
        partial[...] = jnp.zeros_like(partial)

        def tile(t, carry):
            base = pl.multiple_of(t * TILE, TILE)
            grad_near[...] = grad_conv[pl.ds(base, TILE + 2 * PAD), :]
            gated_near[...] = gated_ref[pl.ds(base, TILE + 2 * PAD), :]
            seg_near[...] = seg_ref[pl.ds(base, TILE + 2 * PAD), :]
            centre = seg_near[PAD : PAD + TILE, :]
            lanes = [slice(g * 128, (g + 1) * 128) for g in range(groups)]
            here = [grad_near[PAD : PAD + TILE, lanes[g]] for g in range(groups)]
            back = [jnp.zeros((TILE, 128), F32) for _ in range(groups)]
            for k in range(taps):
                shift = PAD + k - margin
                inside = seg_near[shift : shift + TILE, :] == centre
                for g in range(groups):
                    near = grad_near[shift : shift + TILE, lanes[g]]
                    weight = turned_ref[taps - 1 - k : taps - k, lanes[g]]
                    back[g] = back[g] + jnp.where(inside, near, 0.0) * weight
                    source = gated_near[shift : shift + TILE, lanes[g]]
                    product = jnp.where(inside, source, 0.0) * here[g]
                    partial[k, :, lanes[g]] += jnp.sum(
                        product.reshape(TILE // 8, 8, 128), axis=0
                    )
            for g in range(groups):
                sigma = gate_ref[pl.ds(base, TILE), lanes[g]]
                part = back[g] * sigma
                proj[pl.ds(base, TILE), lanes[g]] = part.astype(BF16)
                far = slice(held + g * 128, held + (g + 1) * 128)
                proj[pl.ds(base, TILE), far] = (
                    part * linear_ref[pl.ds(base, TILE), lanes[g]] * (1.0 - sigma)
                ).astype(BF16)
            return carry

        lax.fori_loop(0, length // TILE, tile, 0)
        terms[:taps, :] = jnp.sum(partial[...], axis=1)
        terms[taps : taps + 1, :] = gain_ref[...]

    return pl.pallas_call(
        kernel,
        out_shape=[
            jax.ShapeDtypeStruct((length, 2 * held), BF16),
            jax.ShapeDtypeStruct((taps + 1, held), F32),
        ],
        scratch_shapes=[
            pltpu.VMEM((length + 2 * PAD, held), F32),
            pltpu.VMEM((taps, 8, held), F32),
            pltpu.VMEM((TILE + 2 * PAD, held), F32),
            pltpu.VMEM((TILE + 2 * PAD, held), F32),
            pltpu.VMEM((TILE + 2 * PAD, 128), F32),
        ],
        compiler_params=kernel_params(),
        cost_estimate=costs(6.2),
    )(grad_hat, hat, inverse, gated, segments, linear, gate, turned, gain_term, *sums)


def stem_message(turned, parts, small, axis, chains, stem_rows):
    dp_count = lax.axis_size(axis)
    stride, size = chains[-1]
    count, share, width = turned.shape
    channels = parts[0].shape[1]
    rows = dp_count * stem_rows
    own = channels // dp_count
    height = stem_rows + 16

    folds = channels // small.shape[1]
    below = small.shape[0] // folds

    def kernel(turned_ref, small_ref, *refs):
        outs = refs[count:]
        place = (lax.axis_index(axis) // stride) % size
        total = jnp.zeros((share, channels), F32)
        for k in range(count):
            total = total + jnp.dot(turned_ref[k], refs[k][...], preferred_element_type=F32)
        lower = jnp.concatenate(
            [small_ref[q * below : (q + 1) * below, :] for q in range(folds)], axis=1
        )
        for i in range(dp_count):
            gain = jnp.concatenate(
                [total[rows : rows + 1, i * own : (i + 1) * own], jnp.zeros((1, channels - own), F32)],
                axis=1,
            )
            block = jnp.concatenate(
                [
                    total[i * stem_rows : (i + 1) * stem_rows],
                    lower,
                    gain,
                    jnp.zeros((7, channels), F32),
                ],
                axis=0,
            ).astype(BF16)
            for k in range(size):

                @pl.when(i % size ^ place == k)
                def _():
                    outs[k][i // size] = block

    return pl.pallas_call(
        kernel,
        out_shape=[jax.ShapeDtypeStruct((dp_count // size, height, channels), BF16)] * size,
        compiler_params=kernel_params(),
        cost_estimate=costs(1.2),
    )(turned, small, *parts)


def stem_finish(parts, stem_rows, rows, taps, axis):
    channels = parts[0].shape[2]
    count = len(parts)

    def kernel(*refs):
        stem, kernel_out, post, pre = refs[count:]
        total = sum(jnp.sum(part[...].astype(F32), axis=0) for part in refs[:count])
        stem[...] = total[:stem_rows]
        held = channels // lax.axis_size(axis)
        below = (taps + 1) * held // channels
        pick = iota((held, rows), 0) == iota((held, rows), 1) + lax.axis_index("dp") * rows
        pick = jnp.where(pick, 1.0, 0.0)
        lower = total[stem_rows : stem_rows + below]
        rest = jnp.concatenate(
            [
                jnp.dot(
                    lower[:, q * held : (q + 1) * held],
                    pick,
                    preferred_element_type=F32,
                    precision=lax.Precision.HIGHEST,
                )
                for q in range(channels // held)
            ],
            axis=0,
        )
        kernel_out[...] = rest.T[:, :taps]
        post[...] = rest[taps : taps + 1]
        at, to = iota((channels, rows), 0), iota((channels, rows), 1)
        mine = lax.axis_index(axis) * rows
        own = jnp.where(at == to + mine, 1.0, 0.0)
        line = jnp.broadcast_to(total[stem_rows + below : stem_rows + below + 1], (8, channels))
        pre[...] = jnp.dot(
            line, own, preferred_element_type=F32, precision=lax.Precision.HIGHEST
        )[:1]

    return pl.pallas_call(
        kernel,
        out_shape=[
            jax.ShapeDtypeStruct((stem_rows, channels), F32),
            jax.ShapeDtypeStruct((rows, taps), F32),
            jax.ShapeDtypeStruct((1, rows), F32),
            jax.ShapeDtypeStruct((1, rows), F32),
        ],
        compiler_params=kernel_params(),
        cost_estimate=costs(1.2),
    )(*parts)


def one_hot(rows, columns):
    return (rows[:, None] == columns[None, :]).astype(BF16)


def order_pieces(mel_pieces, dest_owner, dest_slot, dp_count):
    pieces, piece_values = mel_pieces.shape
    capacity = max(2, 2 * pieces // dp_count)
    matches = (dest_owner[:, None] == jnp.arange(dp_count, dtype=jnp.int32)[None, :]).astype(jnp.int32)
    earlier = jnp.cumsum(matches, axis=0) - matches
    position = dest_owner * capacity + jnp.sum(earlier * matches, axis=1)
    pick = one_hot(jnp.arange(dp_count * capacity, dtype=jnp.int32), position)
    label = jnp.broadcast_to((dest_slot + 1).astype(BF16)[:, None], (pieces, 128))
    return jnp.dot(
        pick, jnp.concatenate([mel_pieces, label], axis=1), preferred_element_type=F32
    ).astype(BF16)


def per_device(
    mel_pieces,
    dest_owner,
    dest_slot,
    segment_ids,
    out_grad,
    stem_weight,
    up_weight,
    down_weight,
    depth_kernel,
    gain_pre,
    gain_post,
):
    dp_count = lax.axis_size("dp")
    tm_count = lax.axis_size("tm")
    chains = stages_of({"dp": dp_count, "tm": tm_count})
    dp_chains, tm_chains = chains["dp"], chains["tm"]
    column = lax.axis_index("tm")
    taps = depth_kernel.shape[1]
    margin = (taps - 1) // 2
    block = out_grad.shape[1]
    channels = out_grad.shape[2]
    held = channels // tm_count
    rows = down_weight.shape[0]
    stem_rows = stem_weight.shape[0]
    features = stem_rows * dp_count * tm_count
    length = block * tm_count

    sums_chains = ((4, 2), (2, 2), (1, 2))

    by_parts = stem_rows % 16 == 0 and rows % 16 == 0 and dp_chains == ((2, 4), (1, 2))
    span = 128 * tm_count
    lane = jnp.arange(span, dtype=jnp.int32)
    grouped = (lane // rows) % tm_count * 128 + lane // (rows * tm_count) * rows + lane % rows
    chunks = rows // stem_rows
    if by_parts:
        up_parts = up_columns(up_weight, rows, tm_count)
        sent, pack = prepare(
            mel_pieces[0], dest_owner[0], dest_slot[0], after(stem_weight, up_parts[0]),
            down_weight, depth_kernel, gain_pre, gain_post, dp_count,
        )
    else:
        sent = order_pieces(mel_pieces[0], dest_owner[0], dest_slot[0], dp_count)
        up_parts = regroup_columns(up_weight, lane, grouped, "tm", tm_count)
        beside = jnp.broadcast_to(jnp.tile(gain_pre, 128 // rows)[None, :], (stem_rows, 128))
        small = jnp.concatenate(
            [depth_kernel, gain_post[:, None], jnp.zeros((rows, 128 - taps - 1), BF16)], axis=1
        )
        folded = [
            value[q : q + stem_rows]
            for value in (small, down_weight)
            for q in range(0, rows, stem_rows)
        ]
        pack = jnp.concatenate([stem_weight, beside] + folded, axis=1)

    up_parts = [up_parts[0]] + [swap(up_parts[k], "tm", k) for k in range(1, tm_count)]
    up_mine = place_parts(up_parts, "tm", 1, tm_count, 0).reshape(tm_count * rows, 2 * held)
    pack_near = gather_stage(pack, "dp", *dp_chains[0], 0)
    up_sides = swap_parts([up_mine] * dp_chains[0][1], "dp", dp_chains[0])
    stem_mine, small_all, down_full = split_rest(
        pack_near, "dp", dp_chains, ((channels + 128, 1), (128, chunks), (channels, chunks))
    )
    stem_mine = stem_mine.reshape(dp_count, stem_rows, channels + 128)
    small_all = small_all.reshape(held, 128)
    down_full = down_full.reshape(held, channels)

    pieces = mel_pieces.shape[1]
    capacity = max(2, 2 * pieces // dp_count)
    arrived = lax.all_to_all(
        after(sent, pack_near).reshape(dp_count, capacity, -1),
        "dp",
        split_axis=0,
        concat_axis=0,
        tiled=True,
    ).reshape(dp_count * capacity, -1)
    up_near = place_parts(up_sides, "dp", *dp_chains[0], 0)
    frames = place_frames(after(arrived, up_near), pieces, features)
    frame_parts = gather_parts(frames, "tm", tm_chains)
    stem_parts = gather_parts(stem_mine, "tm", tm_chains, frames)
    frames = place_parts(frame_parts, "tm", 1, tm_count, 0).reshape(length, features)
    stem_all = place_parts(stem_parts, "tm", 1, tm_count, 1)
    stem_all = stem_all.reshape(features, channels + 128)

    grad_out = out_grad[0]
    grad_first = after(grad_out, up_near)
    hierarchical = list(tm_chains) == [(2, 2), (1, 2)]
    if hierarchical:
        grad_parts = [grad_first, swap(grad_first, "tm", 1), swap(grad_first, "tm", 2)]
    else:
        grad_parts = gather_parts(grad_first, "tm", tm_chains)

    segments = spread_segments(segment_ids)

    extra = 16
    normed, stem_pre, gain_one, frames_turned = stem_forward(
        frames, stem_all, tm_count, "tm", rows, extra
    )
    up_full = gather_rest(up_near, "dp", dp_chains).reshape(channels, 2 * held)
    grad_parts = lax.optimization_barrier((grad_parts, normed))[0]
    if hierarchical:
        grad_parts = grad_parts + [swap(grad_parts[2], "tm", 1)]
    linear, gate_sig, gated = up_forward(normed, up_full)
    conv, stats, turned = conv_forward(gated, small_all, segments, taps)
    stats = swap_all(stats, "tm")
    grad_parts = lax.optimization_barrier((grad_parts, conv))[0]
    grad_out_all = place_parts(grad_parts, "tm", 1, tm_count, 0).reshape(length, channels)
    grad_act = multiply_turned(grad_out_all, down_full)
    activated, conv_hat, grad_hat, inverse, sums, gain_post_term = activate(
        conv, stats, turned, grad_act, taps
    )
    sums = swap_all(sums, "tm")
    if by_parts:
        down_terms = part_terms(activated, grad_out_all, False, "dp", sums_chains)
        normed_turned = turn(normed)
        grad_hat = after(grad_hat, normed_turned)
    else:
        down_terms = [message_terms(activated, grad_out_all, dp_count, tm_count)]
    down_terms = lax.optimization_barrier((down_terms, *sums))[0]
    if by_parts:
        down_parts = swap_parts(down_terms, "dp", sums_chains[-1])

    grad_hat = after(grad_hat, *down_terms)
    grad_proj, kernel_term = conv_backward(
        grad_hat, conv_hat, inverse, sums, gated, segments, linear, gate_sig, turned, taps,
        gain_post_term,
    )

    own_terms, *other_terms = block_terms(
        after(grad_proj, *down_parts[1:]) if by_parts else grad_proj, up_full, True, "tm", tm_count
    )
    if by_parts:
        up_terms = part_terms(
            after(normed_turned, *other_terms), grad_proj, True, "dp", sums_chains
        )
        up_parts = swap_parts(up_terms, "dp", sums_chains[-1])
    else:
        up_terms = [message_terms(normed, grad_proj, dp_count, tm_count)]
    grad_far, grad_parts, grad_passed = block_sum(other_terms, "tm", tm_chains, up_terms[-1])
    if by_parts:
        down_parts[0] = after(down_parts[0], grad_passed)
        down_parts = add_parts(down_parts, "dp", sums_chains[1])
        down_parts = swap_parts(down_parts, "dp", sums_chains[1])
        own_terms = after(own_terms, *down_parts[1:])
    y_own, *y_others = block_terms(
        after(activated, grad_passed), down_full, False, "tm", tm_count
    )
    grad_stem_pre = stem_backward(
        own_terms, grad_parts + [grad_far], stem_pre, grad_out, gain_one, extra
    )
    if by_parts:
        up_parts[0] = after(up_parts[0], grad_stem_pre)
        up_parts = add_parts(up_parts, "dp", sums_chains[1])
        down_parts[0] = after(down_parts[0], up_parts[-1])
        down_parts = add_parts(down_parts, "dp", sums_chains[0])
        down_parts = swap_parts(down_parts, "dp", sums_chains[0])
        grad_stem_parts = gather_parts(grad_stem_pre, "tm", tm_chains, down_parts[0])
        up_parts = reduce_rest(up_parts, "dp", sums_chains[:2])
    else:
        grad_stem_parts = gather_parts(grad_stem_pre, "tm", tm_chains)
    y_far, y_parts, _ = block_sum(y_others, "tm", tm_chains, grad_stem_parts[2])
    if by_parts:
        stem_terms = stem_message(
            frames_turned, grad_stem_parts, kernel_term, "dp", sums_chains, stem_rows
        )
        stem_sums = reduce_rest(stem_terms, "dp", sums_chains)
    else:
        stem_sum = sum(
            jnp.dot(frames_turned[k], grad_stem_parts[k], preferred_element_type=F32)
            for k in range(tm_count)
        )
        share = features // tm_count
        gain_term = stem_sum[share].reshape(dp_count, 1, tm_count * rows)
        gain_term = jnp.pad(gain_term, ((0, 0), (0, 0), (0, channels - tm_count * rows)))
        stem_terms = stem_sum[:share].reshape(dp_count, stem_rows, channels)
        folds = channels // held
        small_term = kernel_term.reshape(folds, -1, held).transpose(1, 0, 2).reshape(-1, channels)
        small_term = jnp.broadcast_to(small_term[None], (dp_count,) + small_term.shape)
        stem_terms = jnp.concatenate([stem_terms, small_term, gain_term], axis=1)
        stem_terms = jnp.pad(stem_terms.astype(BF16), ((0, 0), (0, 7), (0, 0)))
        stem_sums = [
            lax.all_to_all(stem_terms, "dp", split_axis=0, concat_axis=0, tiled=True)
        ]
    if by_parts:
        up_parts[0] = after(up_parts[0], *stem_terms)
        up_parts = cut_columns(up_parts, down_parts, "tm")
        up_parts = swap_all_parts(up_parts, "tm")
        grad_up, grad_down = mix_columns(up_parts, "tm", tm_count * rows, rows)
    else:
        down_sums = lax.all_to_all(
            down_terms[0], ("dp", "tm"), split_axis=0, concat_axis=0, tiled=True
        )
        grad_down = jnp.sum(
            down_sums.reshape(dp_count, tm_count * rows, held).astype(F32), axis=0
        )
        up_sums = lax.all_to_all(
            up_terms[0], ("dp", "tm"), split_axis=0, concat_axis=0, tiled=True
        )
        up_sums = up_sums.reshape(dp_count, tm_count, tm_count * rows, 128)
        spread = one_hot(lane, grouped).reshape(tm_count, 128, span)
        grad_up = jnp.einsum("ijab,jbc->ac", up_sums, spread, preferred_element_type=F32)
    y_out = finish_rows(stem_pre, y_own, y_parts + [y_far])
    grad_stem, grad_kernel, grad_gain_post, grad_gain_pre = stem_finish(
        stem_sums, stem_rows, rows, taps, "tm"
    )
    grad_gain_post, grad_gain_pre = grad_gain_post[0], grad_gain_pre[0]
    return (y_out[None], grad_stem, grad_up, grad_down, grad_kernel, grad_gain_pre, grad_gain_post)


def solution(mesh):
    return jax.shard_map(
        per_device,
        mesh=mesh,
        in_specs=(
            P("dp", "tm", None),
            P("dp", "tm"),
            P("dp", "tm"),
            P("dp", None),
            P("dp", "tm", None),
            P(("dp", "tm"), None),
            P(("dp", "tm"), None),
            P(("dp", "tm"), None),
            P(("dp", "tm"), None),
            P(("dp", "tm")),
            P(("dp", "tm")),
        ),
        out_specs=(
            P("dp", "tm", None),
            P(("dp", "tm"), None),
            P("dp", "tm"),
            P("dp", "tm"),
            P(("dp", "tm"), None),
            P(("dp", "tm")),
            P(("dp", "tm")),
        ),
        check_vma=False,
    )
```

```python
import jax
import jax.numpy as jnp
from jax import lax
from jax.experimental import pallas as pl
from jax.experimental.pallas import tpu as pltpu
from jax.sharding import PartitionSpec as P

NORM_EPS = 1e-05
BF16 = jnp.bfloat16
F32 = jnp.float32


def stages_of(sizes):
    if sizes["dp"] == 8 and sizes["tm"] == 4:
        return {"dp": ((2, 4), (1, 2)), "tm": ((2, 2), (1, 2))}
    if sizes["dp"] == 64 and sizes["tm"] == 4:
        return {"dp": ((8, 8), (2, 4), (1, 2)), "tm": ((1, 4),)}
    return {axis: ((1, size),) for axis, size in sizes.items()}


def swap(value, axis, mask):
    size = lax.axis_size(axis)
    return lax.ppermute(value, axis, [(i, i ^ mask) for i in range(size)])


VMEM_LIMIT = 16 << 20


def kernel_params():
    return pltpu.CompilerParams(vmem_limit_bytes=VMEM_LIMIT)


def costs(microseconds):
    return pl.CostEstimate(
        flops=int(microseconds * 2e10), bytes_accessed=1 << 16, transcendentals=0
    )


def after(value, *others):
    return lax.optimization_barrier((value,) + others)[0]


def place_parts(parts, axis, stride, size, dim):
    shape = parts[0].shape
    out_shape = shape[:dim] + (size,) + shape[dim:]

    def kernel(*refs):
        place = (lax.axis_index(axis) // stride) % size
        for k in range(size):
            refs[size][(slice(None),) * dim + (place ^ k,)] = refs[k][...]

    return pl.pallas_call(
        kernel,
        out_shape=jax.ShapeDtypeStruct(out_shape, parts[0].dtype),
        compiler_params=kernel_params(),
        cost_estimate=costs(2.74),
    )(*parts)


def gather_stage(value, axis, stride, size, dim):
    parts = [value] + [swap(value, axis, k * stride) for k in range(1, size)]
    return place_parts(parts, axis, stride, size, dim)


def gather_rest(value, axis, chains):
    shape = value.shape[1:]
    for dim, (stride, size) in enumerate(chains[1:], 1):
        value = gather_stage(value, axis, stride, size, dim)
    return value.reshape((-1,) + shape)


def block_terms(left, right, transposed, axis, count):
    block = left.shape[0] // count
    width = right.shape[0] if transposed else right.shape[1]
    dims = (((1,), (1 if transposed else 0,)), ((), ()))

    def kernel(left_ref, right_ref, own, *refs):
        others, terms = refs[:-1], refs[-1]
        place = lax.axis_index(axis)
        terms[...] = lax.dot_general(
            left_ref[...], right_ref[...], dims, preferred_element_type=F32
        )
        for k in range(count):
            start = pl.multiple_of((place ^ k) * block, block)
            if k == 0:
                own[...] = terms[pl.ds(start, block), :]
            else:
                others[k - 1][...] = terms[pl.ds(start, block), :].astype(BF16)

    return pl.pallas_call(
        kernel,
        out_shape=[jax.ShapeDtypeStruct((block, width), F32)]
        + [jax.ShapeDtypeStruct((block, width), BF16)] * (count - 1),
        scratch_shapes=[pltpu.VMEM((count * block, width), F32)],
        compiler_params=kernel_params(),
        cost_estimate=costs(0.365),
    )(left, right)


def block_sum(others, axis, chains, first=None):
    if list(chains) == [(2, 2), (1, 2)]:
        near, passed = swap(others[0], axis, 1), swap(others[2], axis, 1)
        passed = add_pair(others[1], passed)
        if first is not None:
            passed = after(passed, first)
        return swap(passed, axis, 2), [near], passed
    parts = [swap(other, axis, k) for k, other in enumerate(others, 1)]
    return parts[-1], parts[:-1], others[-1]


def add_pair(one, other):
    def kernel(one_ref, other_ref, out):
        out[...] = (one_ref[...].astype(F32) + other_ref[...].astype(F32)).astype(BF16)

    return pl.pallas_call(
        kernel,
        out_shape=jax.ShapeDtypeStruct(one.shape, BF16),
        compiler_params=kernel_params(),
        cost_estimate=costs(1.39),
    )(one, other)


def finish_rows(stem_pre, own, parts):
    def kernel(pre_ref, own_ref, *refs):
        total = own_ref[...]
        for part in refs[:-1]:
            total = total + part[...].astype(F32)
        pre = pre_ref[...]
        stem_out = (pre * jax.nn.sigmoid(pre)).astype(BF16).astype(F32)
        refs[-1][...] = (stem_out + total).astype(BF16)

    return pl.pallas_call(
        kernel,
        out_shape=jax.ShapeDtypeStruct(own.shape, BF16),
        compiler_params=kernel_params(),
        cost_estimate=costs(0.527),
    )(stem_pre, own, *parts)


def turn(value):
    rows, columns = value.shape

    def kernel(source, out):
        for c in range(0, columns, 128):
            out[c : c + 128, :] = source[:, c : c + 128].astype(F32).T.astype(BF16)

    return pl.pallas_call(
        kernel,
        out_shape=jax.ShapeDtypeStruct((columns, rows), value.dtype),
        compiler_params=kernel_params(),
        cost_estimate=costs(2.02),
    )(value)


def part_terms(left, right, turned, axis, chains):
    total = lax.axis_size(axis)
    stride, size = chains[-1]
    rows, columns = left.shape[0 if turned else 1] // total, right.shape[1]
    step = max(1, 512 // rows) if turned else max(1, 128 // rows)

    def kernel(left_ref, right_ref, *outs):
        place = (lax.axis_index(axis) // stride) % size
        for i in range(0, total, step):
            block = slice(i * rows, (i + step) * rows)
            if turned:
                term = jnp.dot(left_ref[block, :], right_ref[...], preferred_element_type=F32)
            else:
                term = lax.dot_general(
                    left_ref[:, block],
                    right_ref[...],
                    (((0,), (0,)), ((), ())),
                    preferred_element_type=F32,
                )
            term = term.astype(BF16)
            for n in range(step):
                for k in range(size):

                    @pl.when((i + n) % size ^ place == k)
                    def _():
                        outs[k][(i + n) // size] = term[n * rows : (n + 1) * rows]

    return pl.pallas_call(
        kernel,
        out_shape=[jax.ShapeDtypeStruct((total // size, rows, columns), BF16)] * size,
        compiler_params=kernel_params(),
        cost_estimate=costs(0.818),
    )(left, right)


def swap_all_parts(parts, axis):
    return [parts[0]] + [swap(part, axis, k) for k, part in enumerate(parts[1:], 1)]


def swap_parts(parts, axis, chain):
    stride, _ = chain
    return [parts[0]] + [swap(part, axis, k * stride) for k, part in enumerate(parts[1:], 1)]


def add_parts(parts, axis, chain):
    stride, size = chain
    shape = (parts[0].shape[0] // size,) + parts[0].shape[1:]

    def kernel(*refs):
        place = (lax.axis_index(axis) // stride) % size
        for a in range(shape[0]):
            for k in range(size):
                at = a * size + (place ^ k)
                total = sum(part[at].astype(F32) for part in refs[: len(parts)])
                refs[len(parts) + k][a] = total.astype(BF16)

    return pl.pallas_call(
        kernel,
        out_shape=[jax.ShapeDtypeStruct(shape, BF16)] * size,
        compiler_params=kernel_params(),
        cost_estimate=costs(0.316),
    )(*parts)


def reduce_rest(parts, axis, chains):
    parts = swap_parts(parts, axis, chains[-1])
    for chain in reversed(chains[:-1]):
        parts = swap_parts(add_parts(parts, axis, chain), axis, chain)
    return parts


def cut_columns(first, second, axis):
    count = lax.axis_size(axis)
    terms = len(first)
    _, rows, columns = first[0].shape
    _, below, wide = second[0].shape
    share = columns // count
    folds = wide // columns

    def kernel(*refs):
        place = lax.axis_index(axis)
        upper = sum(part[0].astype(F32) for part in refs[:terms]).astype(BF16)
        lower = sum(part[0].astype(F32) for part in refs[terms : 2 * terms]).astype(BF16)
        for j in range(count):
            for k in range(count):

                @pl.when(place ^ j == k)
                def _():
                    out = refs[2 * terms + k]
                    out[:rows, :] = upper[:, j * share : (j + 1) * share]
                    for f in range(folds):
                        start = (j * folds + f) * share
                        out[rows + f * below : rows + (f + 1) * below, :] = lower[
                            :, start : start + share
                        ]

    return pl.pallas_call(
        kernel,
        out_shape=[jax.ShapeDtypeStruct((rows + folds * below, share), BF16)] * count,
        compiler_params=kernel_params(),
        cost_estimate=costs(1.37),
    )(*first, *second)


def mix_columns(parts, axis, rows, small):
    count = len(parts)
    height, share = parts[0].shape
    span = share * count
    folds = (height - rows) // small

    def kernel(*refs):
        place = lax.axis_index(axis)
        upper, lower = refs[count:]
        at, to = iota((share, span), 0), iota((share, span), 1)
        total = jnp.zeros((rows, span), F32)
        for k in range(count):
            want = at // small * (small * count) + (place ^ k) * small + at % small
            spread = table(to == want)
            total = total + jnp.dot(refs[k][:rows, :], spread, preferred_element_type=F32)
            start = pl.multiple_of((place ^ k) * small, small)
            for f in range(folds):
                lower[pl.ds(start, small), f * share : (f + 1) * share] = refs[k][
                    rows + f * small : rows + (f + 1) * small, :
                ].astype(F32)
        upper[...] = total

    return pl.pallas_call(
        kernel,
        out_shape=[
            jax.ShapeDtypeStruct((rows, span), F32),
            jax.ShapeDtypeStruct((count * small, folds * share), F32),
        ],
        compiler_params=kernel_params(),
        cost_estimate=costs(0.334),
    )(*parts)


def message_terms(left, right, parts, sides):
    rows, columns = left.shape[1] // parts, right.shape[1] // sides
    terms = jnp.dot(left.T, right, preferred_element_type=F32).astype(BF16)
    terms = terms.reshape(parts, rows, sides, columns).transpose(0, 2, 1, 3)
    return terms.reshape(parts * sides, rows, columns)


def regroup_columns(weight, lane, grouped, axis, count):
    rows, columns = weight.shape
    span = lane.shape[0]
    groups = columns // span
    parts = jnp.dot(
        weight.reshape(rows * groups, span), one_hot(grouped, lane), preferred_element_type=F32
    ).astype(BF16)
    parts = parts.reshape(rows, groups, count, 128).transpose(2, 0, 1, 3)
    parts = parts.reshape(count, rows, groups * 128)
    return [
        lax.dynamic_index_in_dim(parts, lax.axis_index(axis) ^ k, 0, keepdims=False)
        for k in range(count)
    ]


def stem_backward(own, parts, stem_pre, grad_out, gain, extra):
    block, channels = own.shape

    def kernel(own_ref, pre_ref, out_grad_ref, gain_ref, *refs):
        out = refs[-1]
        pre = pre_ref[...]
        sigma = jax.nn.sigmoid(pre)
        hat, inverse = standardize((pre * sigma).astype(BF16).astype(F32))
        grad = own_ref[...]
        for part in refs[:-1]:
            grad = grad + part[...].astype(F32)
        out[block:, :] = jnp.concatenate(
            [jnp.sum(grad * hat, axis=0, keepdims=True), jnp.zeros((extra - 1, channels), F32)]
        ).astype(BF16)
        back = grad * gain_ref[...]
        first = jnp.mean(back, axis=-1, keepdims=True)
        second = jnp.mean(back * hat, axis=-1, keepdims=True)
        stem_out = out_grad_ref[...].astype(F32) + (back - first - hat * second) * inverse
        out[:block, :] = (stem_out * (sigma * (1.0 + pre * (1.0 - sigma)))).astype(BF16)

    return pl.pallas_call(
        kernel,
        out_shape=jax.ShapeDtypeStruct((block + extra, channels), BF16),
        compiler_params=kernel_params(),
        cost_estimate=costs(0.391),
    )(own, stem_pre, grad_out, gain, *parts)


def standardize(values):
    centered = values - jnp.mean(values, axis=-1, keepdims=True)
    inverse = lax.rsqrt(jnp.mean(centered * centered, axis=-1, keepdims=True) + NORM_EPS)
    return (centered * inverse, inverse)


def gather_parts(value, axis, chains, first=None):
    if list(chains) == [(2, 2), (1, 2)]:
        far = swap(value, axis, 2)
        if first is not None:
            far = after(far, first)
        return [value, swap(value, axis, 1), far, swap(far, axis, 1)]
    return [value] + [swap(value, axis, k) for k in range(1, lax.axis_size(axis))]


def swap_all(value, axis):
    return [value] + [swap(value, axis, k) for k in range(1, lax.axis_size(axis))]


def split_parts(parts, axis, stride, size, dim, cuts):
    shape = parts[0].shape
    lead = shape[:dim] + (size,) + shape[dim:-2]
    rows = shape[-2]

    def kernel(*refs):
        place = (lax.axis_index(axis) // stride) % size
        inner = (slice(None),) * (len(lead) - dim - 1)
        for k in range(size):
            target = (slice(None),) * dim + (place ^ k,) + inner
            start = 0
            for n, (width, pieces) in enumerate(cuts):
                for q in range(pieces):
                    refs[size + n][target + (q,)] = refs[k][..., start : start + width]
                    start += width

    return pl.pallas_call(
        kernel,
        out_shape=[
            jax.ShapeDtypeStruct(lead + (pieces, rows, width), parts[0].dtype)
            for width, pieces in cuts
        ],
        compiler_params=kernel_params(),
        cost_estimate=costs(0.398),
    )(*parts)


def split_rest(value, axis, chains, cuts):
    for dim, (stride, size) in enumerate(chains[1:], 1):
        parts = [value] + [swap(value, axis, k * stride) for k in range(1, size)]
        if dim == len(chains) - 1:
            return split_parts(parts, axis, stride, size, dim, cuts)
        value = place_parts(parts, axis, stride, size, dim)


def iota(shape, dim):
    return lax.broadcasted_iota(jnp.int32, shape, dim)


def table(flags):
    return jnp.where(flags, 1.0, 0.0).astype(BF16)


def fetch(sources, held, sems):
    copies = [
        pltpu.make_async_copy(source, target, sems.at[k])
        for k, (source, target) in enumerate(zip(sources, held))
    ]
    for copy in copies:
        copy.start()
    for copy in copies:
        copy.wait()


def fetching_call(kernel, inputs, out_shape, cost):
    return pl.pallas_call(
        kernel,
        out_shape=out_shape,
        in_specs=[pl.BlockSpec(memory_space=pl.ANY)] * len(inputs),
        scratch_shapes=[pltpu.VMEM(value.shape, value.dtype) for value in inputs]
        + [pltpu.SemaphoreType.DMA((len(inputs),))],
        cost_estimate=cost,
    )(*inputs)


def up_columns(up, rows, tm_count):
    span = 128 * tm_count
    groups = up.shape[1] // span

    def kernel(source, *refs):
        up_parts, (up_ref, sems) = refs[:tm_count], refs[tm_count:]
        fetch([source], [up_ref], sems)
        place = lax.axis_index("tm")
        at, to = iota((span, 128), 0), iota((span, 128), 1)
        for k in range(tm_count):
            want = to // rows * (rows * tm_count) + (place ^ k) * rows + to % rows
            pick = table(at == want)
            for g in range(groups):
                up_parts[k][:, g * 128 : (g + 1) * 128] = jnp.dot(
                    up_ref[:, g * span : (g + 1) * span], pick, preferred_element_type=F32
                ).astype(BF16)

    return fetching_call(
        kernel,
        (up,),
        [jax.ShapeDtypeStruct((rows, up.shape[1] // tm_count), BF16)] * tm_count,
        costs(0.761),
    )


def prepare(mel, owner, slot, stem, down, taps, gain_one, gain_two, dp_count):
    pieces, values = mel.shape
    capacity = max(2, 2 * pieces // dp_count)
    slots = dp_count * capacity
    stem_rows, channels = stem.shape
    rows, tap_count = taps.shape
    chunks = rows // stem_rows
    beyond = channels + 128 * (chunks + 1)
    inputs = (
        stem, taps, gain_one[None, :], gain_two[None, :], owner[None, :], slot[None, :], mel, down
    )
    count = len(inputs)

    def kernel(*refs):
        sent, pack = refs[count : count + 2]
        held = refs[count + 2 : -1]
        fetch(refs[:count], held, refs[-1])
        stem_ref, taps_ref, one_ref, two_ref, owner_ref, slot_ref, mel_ref, down_ref = held
        pack[:, :channels] = stem_ref[...]
        lane = iota((rows, 128), 1)
        spread = table(lane % rows == iota((rows, 128), 0))
        gain = jnp.broadcast_to(one_ref[...].astype(F32), (stem_rows, rows)).astype(BF16)
        pack[:, channels : channels + 128] = jnp.dot(
            gain, spread, preferred_element_type=F32
        ).astype(BF16)
        tap_lane = table(iota((tap_count, 128), 1) == iota((tap_count, 128), 0))
        square = iota((rows, rows), 0) == iota((rows, rows), 1)
        diagonal = jnp.where(
            square, jnp.broadcast_to(two_ref[...].astype(F32), (rows, rows)), 0.0
        ).astype(BF16)
        small = jnp.dot(taps_ref[...], tap_lane, preferred_element_type=F32)
        small = small + jnp.dot(diagonal, table(lane == tap_count), preferred_element_type=F32)
        for q in range(chunks):
            lanes = slice(channels + 128 * (q + 1), channels + 128 * (q + 2))
            pack[:, lanes] = small[q * stem_rows : (q + 1) * stem_rows].astype(BF16)
            lanes = slice(beyond + channels * q, beyond + channels * (q + 1))
            pack[:, lanes] = down_ref[q * stem_rows : (q + 1) * stem_rows, :]

        owners = jnp.broadcast_to(owner_ref[...].astype(F32), (pieces, pieces))
        earlier = iota((pieces, pieces), 0) < iota((pieces, pieces), 1)
        same = jnp.where(owners.T == owners, jnp.where(earlier, 1.0, 0.0), 0.0)
        target = owners[:1] * float(capacity) + jnp.sum(same, axis=0, keepdims=True)
        target = jnp.broadcast_to(target, (slots, pieces)).astype(jnp.int32)
        chosen = target == iota((slots, pieces), 0)
        pick = table(chosen)
        sent[:, :values] = jnp.dot(pick, mel_ref[...], preferred_element_type=F32).astype(BF16)
        labels = jnp.broadcast_to(slot_ref[...].astype(F32) + 1.0, (slots, pieces))
        label = jnp.sum(jnp.where(chosen, labels, 0.0), axis=1, keepdims=True)
        sent[:, values:] = jnp.broadcast_to(label, (slots, 128)).astype(BF16)

    return fetching_call(
        kernel,
        inputs,
        [
            jax.ShapeDtypeStruct((slots, values + 128), BF16),
            jax.ShapeDtypeStruct((stem_rows, beyond + channels * chunks), BF16),
        ],
        costs(7),
    )


def place_frames(arrived, pieces, features):
    slots, width = arrived.shape
    steps = (width - 128) // features

    def kernel(arrived_ref, out):
        labels = arrived_ref[:, steps * features :].astype(F32).T[:1]
        want = jnp.broadcast_to(labels, (pieces * steps, slots)).astype(jnp.int32)
        row = lax.broadcasted_iota(jnp.int32, (pieces * steps, slots), 0)
        total = jnp.zeros((pieces * steps, features), F32)
        for q in range(steps):
            put = jnp.where(row == (want - 1) * steps + q, 1.0, 0.0).astype(BF16)
            total = total + jnp.dot(
                put, arrived_ref[:, q * features : (q + 1) * features], preferred_element_type=F32
            )
        out[...] = total.astype(BF16)

    return pl.pallas_call(
        kernel,
        out_shape=jax.ShapeDtypeStruct((pieces * steps, features), BF16),
        compiler_params=kernel_params(),
        cost_estimate=costs(0.926),
    )(arrived)


def stem_forward(frames, stem_all, count, axis, rows, extra):
    length = frames.shape[0]
    features, width = stem_all.shape
    channels = width - 128
    block = length // count
    stem_rows = features * rows // channels
    share = features // count

    def kernel(frames_ref, stem_ref, normed, pre_own, gain_out, turned):
        place = lax.axis_index(axis)
        feature = lax.broadcasted_iota(jnp.int32, (features, share), 0)
        chosen = lax.broadcasted_iota(jnp.int32, (features, share), 1)
        chosen = (chosen // stem_rows * count + place) * stem_rows + chosen % stem_rows
        pick = jnp.where(feature == chosen, 1.0, 0.0).astype(BF16)
        corner = lax.broadcasted_iota(jnp.int32, (extra, extra), 0)
        corner = corner + lax.broadcasted_iota(jnp.int32, (extra, extra), 1)
        corner = jnp.where(corner == 0, 1.0, 0.0).astype(BF16)
        for k in range(count):
            start = pl.multiple_of((place ^ k) * block, block)
            turned[k, :share, :block] = lax.dot_general(
                pick,
                frames_ref[pl.ds(start, block), :],
                (((0,), (1,)), ((), ())),
                preferred_element_type=F32,
            ).astype(BF16)
            turned[k, share:, :block] = jnp.zeros((extra, block), BF16)
            turned[k, :share, block:] = jnp.zeros((share, extra), BF16)
            turned[k, share:, block:] = corner
        beside = stem_ref[:, channels:].astype(F32)
        gains = []
        for g in range(channels // 128):
            row = lax.broadcasted_iota(jnp.int32, (features, 128), 0)
            lane = lax.broadcasted_iota(jnp.int32, (features, 128), 1) + g * 128
            gains.append(
                jnp.sum(
                    jnp.where(row == lane // rows * stem_rows, beside, 0.0), axis=0, keepdims=True
                )
            )
        gain_out[...] = jnp.concatenate(gains, axis=1)
        for b in range(count):
            pre = jnp.dot(
                frames_ref[b * block : (b + 1) * block, :],
                stem_ref[:, :channels],
                preferred_element_type=F32,
            )
            hat, _ = standardize((pre * jax.nn.sigmoid(pre)).astype(BF16).astype(F32))
            normed[b * block : (b + 1) * block, :] = (hat * gain_out[...]).astype(BF16)

            @pl.when(place == b)
            def _():
                pre_own[...] = pre

    return pl.pallas_call(
        kernel,
        out_shape=[
            jax.ShapeDtypeStruct((length, channels), BF16),
            jax.ShapeDtypeStruct((block, channels), F32),
            jax.ShapeDtypeStruct((1, channels), F32),
            jax.ShapeDtypeStruct((count, share + extra, block + extra), BF16),
        ],
        compiler_params=kernel_params(),
        cost_estimate=costs(4.22),
    )(frames, stem_all)


PAD = 16


def up_forward(normed, up):
    length = normed.shape[0]
    held = up.shape[1] // 2
    step = min(128, length)

    def kernel(normed_ref, up_ref, linear, gate, gated):
        edge = jnp.zeros((PAD, held), F32)
        gated[:PAD, :] = edge
        gated[PAD + length :, :] = edge
        for b in range(0, length, step):
            proj = jnp.dot(normed_ref[b : b + step, :], up_ref[...], preferred_element_type=F32)
            sigma = jax.nn.sigmoid(proj[:, held:])
            linear[b : b + step, :] = proj[:, :held]
            gate[b : b + step, :] = sigma
            gated[PAD + b : PAD + b + step, :] = (proj[:, :held] * sigma).astype(BF16).astype(F32)

    return pl.pallas_call(
        kernel,
        out_shape=[
            jax.ShapeDtypeStruct((length, held), F32),
            jax.ShapeDtypeStruct((length, held), F32),
            jax.ShapeDtypeStruct((length + 2 * PAD, held), F32),
        ],
        compiler_params=kernel_params(),
        cost_estimate=costs(0.396),
    )(normed, up)


def columns_of(first, second):
    rows = first.shape[0]
    lane = lax.broadcasted_iota(jnp.int32, (rows, 128), 1)
    both = jnp.where(lane == 0, first, jnp.where(lane == 1, second, 0.0))
    return both.T[:8]


def rows_of(table):
    rows = table.shape[1]
    turned = jnp.concatenate([table, jnp.zeros((120, rows), F32)], axis=0).T
    return turned[:, :1], turned[:, 1:2]


def spread_segments(segments):
    length = segments.shape[1]

    def kernel(source, out):
        edge = jnp.full((PAD, 128), -1.0, F32)
        out[:PAD, :] = edge
        out[PAD + length :, :] = edge
        out[PAD : PAD + length, :] = jnp.broadcast_to(
            source[...].astype(F32), (128, length)
        ).T

    return pl.pallas_call(
        kernel,
        out_shape=jax.ShapeDtypeStruct((length + 2 * PAD, 128), F32),
        compiler_params=kernel_params(),
        cost_estimate=costs(0.877),
    )(segments)


def multiply_turned(left, right):
    def kernel(left_ref, right_ref, out):
        out[...] = lax.dot_general(
            left_ref[...], right_ref[...], (((1,), (1,)), ((), ())), preferred_element_type=F32
        )

    return pl.pallas_call(
        kernel,
        out_shape=jax.ShapeDtypeStruct((left.shape[0], right.shape[0]), F32),
        compiler_params=kernel_params(),
        cost_estimate=costs(0.594),
    )(left, right)


TILE = 64


def conv_forward(gated, small, segments, taps):
    length, held = gated.shape[0] - 2 * PAD, gated.shape[1]
    margin = (taps - 1) // 2

    def kernel(gated_ref, small_ref, seg_ref, conv, stats, turned, gated_near, seg_near):
        turned[...] = small_ref[...].astype(F32).T

        def tile(t, carry):
            base = pl.multiple_of(t * TILE, TILE)
            gated_near[...] = gated_ref[pl.ds(base, TILE + 2 * PAD), :]
            seg_near[...] = seg_ref[pl.ds(base, TILE + 2 * PAD), :]
            centre = seg_near[PAD : PAD + TILE, :]
            sums = [jnp.zeros((TILE, 128), F32) for _ in range(held // 128)]
            for k in range(taps):
                shift = PAD + k - margin
                inside = seg_near[shift : shift + TILE, :] == centre
                for g in range(held // 128):
                    lanes = slice(g * 128, (g + 1) * 128)
                    value = gated_near[shift : shift + TILE, lanes]
                    sums[g] = sums[g] + jnp.where(inside, value, 0.0) * turned[k : k + 1, lanes]
            conv[pl.ds(base, TILE), :] = jnp.concatenate(sums, axis=1)
            return carry

        lax.fori_loop(0, length // TILE, tile, 0)
        value = conv[...]
        mean = jnp.mean(value, axis=-1, keepdims=True)
        centered = value - mean
        stats[...] = columns_of(mean, jnp.sum(centered * centered, axis=-1, keepdims=True))

    return pl.pallas_call(
        kernel,
        out_shape=[
            jax.ShapeDtypeStruct((length, held), F32),
            jax.ShapeDtypeStruct((8, length), F32),
            jax.ShapeDtypeStruct((128, held), F32),
        ],
        scratch_shapes=[
            pltpu.VMEM((TILE + 2 * PAD, held), F32),
            pltpu.VMEM((TILE + 2 * PAD, 128), F32),
        ],
        compiler_params=kernel_params(),
        cost_estimate=costs(1.03),
    )(gated, small, segments)


def activate(conv, stats, turned, grad_act, taps):
    length, held = conv.shape
    count = len(stats)

    def kernel(conv_ref, turned_ref, grad_ref, *refs):
        tables, (active, hat_out, grad_hat_out, inverse_out, sums, gain_term) = (
            refs[:count], refs[count:],
        )
        means = [table[0:1, :] for table in tables]
        mean = sum(means) * (1.0 / count)
        squares = sum(table[1:2, :] for table in tables)
        squares = squares + held * sum((one - mean) * (one - mean) for one in means)
        inverse = lax.rsqrt(squares * (1.0 / (held * count)) + NORM_EPS)
        both = jnp.concatenate([mean, inverse, jnp.zeros((6, length), F32)], axis=0)
        mean, inverse = rows_of(both)
        inverse_out[...] = jnp.broadcast_to(inverse, (length, 128))
        gain = turned_ref[taps : taps + 1, :]
        hat = (conv_ref[...] - mean) * inverse
        scaled = hat * gain
        sigma = jax.nn.sigmoid(scaled)
        active[...] = (scaled * sigma).astype(BF16)
        grad_scaled = grad_ref[...] * (sigma * (1.0 + scaled * (1.0 - sigma)))
        gain_term[...] = jnp.sum(grad_scaled * hat, axis=0, keepdims=True)
        grad_hat = grad_scaled * gain
        hat_out[...] = hat
        grad_hat_out[...] = grad_hat
        sums[...] = columns_of(
            jnp.sum(grad_hat, axis=-1, keepdims=True),
            jnp.sum(grad_hat * hat, axis=-1, keepdims=True),
        )

    return pl.pallas_call(
        kernel,
        out_shape=[
            jax.ShapeDtypeStruct((length, held), BF16),
            jax.ShapeDtypeStruct((length, held), F32),
            jax.ShapeDtypeStruct((length, held), F32),
            jax.ShapeDtypeStruct((length, 128), F32),
            jax.ShapeDtypeStruct((8, length), F32),
            jax.ShapeDtypeStruct((1, held), F32),
        ],
        compiler_params=kernel_params(),
        cost_estimate=costs(0.416),
    )(conv, turned, grad_act, *stats)


def conv_backward(grad_hat, hat, inverse, sums, gated, segments, linear, gate, turned, taps, gain_term):
    length, held = hat.shape
    count = len(sums)
    margin = (taps - 1) // 2
    groups = held // 128

    def kernel(
        grad_ref, hat_ref, inverse_ref, gated_ref, seg_ref, linear_ref, gate_ref, turned_ref,
        gain_ref, *refs
    ):
        tables, (proj, terms), (grad_conv, partial, grad_near, gated_near, seg_near) = (
            refs[:count], refs[count : count + 2], refs[count + 2 :],
        )
        total = sum(table[...] for table in tables) * (1.0 / (held * count))
        first, second = rows_of(total)
        edge = jnp.zeros((PAD, held), F32)
        grad_conv[:PAD, :] = edge
        grad_conv[PAD + length :, :] = edge
        value = (grad_ref[...] - first - hat_ref[...] * second) * inverse_ref[:, :1]
        grad_conv[PAD : PAD + length, :] = value.astype(BF16).astype(F32)
        partial[...] = jnp.zeros_like(partial)

        def tile(t, carry):
            base = pl.multiple_of(t * TILE, TILE)
            grad_near[...] = grad_conv[pl.ds(base, TILE + 2 * PAD), :]
            gated_near[...] = gated_ref[pl.ds(base, TILE + 2 * PAD), :]
            seg_near[...] = seg_ref[pl.ds(base, TILE + 2 * PAD), :]
            centre = seg_near[PAD : PAD + TILE, :]
            lanes = [slice(g * 128, (g + 1) * 128) for g in range(groups)]
            here = [grad_near[PAD : PAD + TILE, lanes[g]] for g in range(groups)]
            back = [jnp.zeros((TILE, 128), F32) for _ in range(groups)]
            for k in range(taps):
                shift = PAD + k - margin
                inside = seg_near[shift : shift + TILE, :] == centre
                for g in range(groups):
                    near = grad_near[shift : shift + TILE, lanes[g]]
                    weight = turned_ref[taps - 1 - k : taps - k, lanes[g]]
                    back[g] = back[g] + jnp.where(inside, near, 0.0) * weight
                    source = gated_near[shift : shift + TILE, lanes[g]]
                    product = jnp.where(inside, source, 0.0) * here[g]
                    partial[k, :, lanes[g]] += jnp.sum(
                        product.reshape(TILE // 8, 8, 128), axis=0
                    )
            for g in range(groups):
                sigma = gate_ref[pl.ds(base, TILE), lanes[g]]
                part = back[g] * sigma
                proj[pl.ds(base, TILE), lanes[g]] = part.astype(BF16)
                far = slice(held + g * 128, held + (g + 1) * 128)
                proj[pl.ds(base, TILE), far] = (
                    part * linear_ref[pl.ds(base, TILE), lanes[g]] * (1.0 - sigma)
                ).astype(BF16)
            return carry

        lax.fori_loop(0, length // TILE, tile, 0)
        terms[:taps, :] = jnp.sum(partial[...], axis=1)
        terms[taps : taps + 1, :] = gain_ref[...]

    return pl.pallas_call(
        kernel,
        out_shape=[
            jax.ShapeDtypeStruct((length, 2 * held), BF16),
            jax.ShapeDtypeStruct((taps + 1, held), F32),
        ],
        scratch_shapes=[
            pltpu.VMEM((length + 2 * PAD, held), F32),
            pltpu.VMEM((taps, 8, held), F32),
            pltpu.VMEM((TILE + 2 * PAD, held), F32),
            pltpu.VMEM((TILE + 2 * PAD, held), F32),
            pltpu.VMEM((TILE + 2 * PAD, 128), F32),
        ],
        compiler_params=kernel_params(),
        cost_estimate=costs(4.02),
    )(grad_hat, hat, inverse, gated, segments, linear, gate, turned, gain_term, *sums)


def stem_message(turned, parts, small, axis, chains, stem_rows):
    dp_count = lax.axis_size(axis)
    stride, size = chains[-1]
    count, share, width = turned.shape
    channels = parts[0].shape[1]
    rows = dp_count * stem_rows
    own = channels // dp_count
    height = stem_rows + 16

    folds = channels // small.shape[1]
    below = small.shape[0] // folds

    def kernel(turned_ref, small_ref, *refs):
        outs = refs[count:]
        place = (lax.axis_index(axis) // stride) % size
        total = jnp.zeros((share, channels), F32)
        for k in range(count):
            total = total + jnp.dot(turned_ref[k], refs[k][...], preferred_element_type=F32)
        lower = jnp.concatenate(
            [small_ref[q * below : (q + 1) * below, :] for q in range(folds)], axis=1
        )
        for i in range(dp_count):
            gain = jnp.concatenate(
                [total[rows : rows + 1, i * own : (i + 1) * own], jnp.zeros((1, channels - own), F32)],
                axis=1,
            )
            block = jnp.concatenate(
                [
                    total[i * stem_rows : (i + 1) * stem_rows],
                    lower,
                    gain,
                    jnp.zeros((7, channels), F32),
                ],
                axis=0,
            ).astype(BF16)
            for k in range(size):

                @pl.when(i % size ^ place == k)
                def _():
                    outs[k][i // size] = block

    return pl.pallas_call(
        kernel,
        out_shape=[jax.ShapeDtypeStruct((dp_count // size, height, channels), BF16)] * size,
        compiler_params=kernel_params(),
        cost_estimate=costs(2.73),
    )(turned, small, *parts)


def stem_finish(parts, stem_rows, rows, taps, axis):
    channels = parts[0].shape[2]
    count = len(parts)

    def kernel(*refs):
        stem, kernel_out, post, pre = refs[count:]
        total = sum(jnp.sum(part[...].astype(F32), axis=0) for part in refs[:count])
        stem[...] = total[:stem_rows]
        held = channels // lax.axis_size(axis)
        below = (taps + 1) * held // channels
        pick = iota((held, rows), 0) == iota((held, rows), 1) + lax.axis_index("dp") * rows
        pick = jnp.where(pick, 1.0, 0.0)
        lower = total[stem_rows : stem_rows + below]
        rest = jnp.concatenate(
            [
                jnp.dot(
                    lower[:, q * held : (q + 1) * held],
                    pick,
                    preferred_element_type=F32,
                    precision=lax.Precision.HIGHEST,
                )
                for q in range(channels // held)
            ],
            axis=0,
        )
        kernel_out[...] = rest.T[:, :taps]
        post[...] = rest[taps : taps + 1]
        at, to = iota((channels, rows), 0), iota((channels, rows), 1)
        mine = lax.axis_index(axis) * rows
        own = jnp.where(at == to + mine, 1.0, 0.0)
        line = jnp.broadcast_to(total[stem_rows + below : stem_rows + below + 1], (8, channels))
        pre[...] = jnp.dot(
            line, own, preferred_element_type=F32, precision=lax.Precision.HIGHEST
        )[:1]

    return pl.pallas_call(
        kernel,
        out_shape=[
            jax.ShapeDtypeStruct((stem_rows, channels), F32),
            jax.ShapeDtypeStruct((rows, taps), F32),
            jax.ShapeDtypeStruct((1, rows), F32),
            jax.ShapeDtypeStruct((1, rows), F32),
        ],
        compiler_params=kernel_params(),
        cost_estimate=costs(0.614),
    )(*parts)


def one_hot(rows, columns):
    return (rows[:, None] == columns[None, :]).astype(BF16)


def order_pieces(mel_pieces, dest_owner, dest_slot, dp_count):
    pieces, piece_values = mel_pieces.shape
    capacity = max(2, 2 * pieces // dp_count)
    matches = (dest_owner[:, None] == jnp.arange(dp_count, dtype=jnp.int32)[None, :]).astype(jnp.int32)
    earlier = jnp.cumsum(matches, axis=0) - matches
    position = dest_owner * capacity + jnp.sum(earlier * matches, axis=1)
    pick = one_hot(jnp.arange(dp_count * capacity, dtype=jnp.int32), position)
    label = jnp.broadcast_to((dest_slot + 1).astype(BF16)[:, None], (pieces, 128))
    return jnp.dot(
        pick, jnp.concatenate([mel_pieces, label], axis=1), preferred_element_type=F32
    ).astype(BF16)


def per_device(
    mel_pieces,
    dest_owner,
    dest_slot,
    segment_ids,
    out_grad,
    stem_weight,
    up_weight,
    down_weight,
    depth_kernel,
    gain_pre,
    gain_post,
):
    dp_count = lax.axis_size("dp")
    tm_count = lax.axis_size("tm")
    chains = stages_of({"dp": dp_count, "tm": tm_count})
    dp_chains, tm_chains = chains["dp"], chains["tm"]
    column = lax.axis_index("tm")
    taps = depth_kernel.shape[1]
    margin = (taps - 1) // 2
    block = out_grad.shape[1]
    channels = out_grad.shape[2]
    held = channels // tm_count
    rows = down_weight.shape[0]
    stem_rows = stem_weight.shape[0]
    features = stem_rows * dp_count * tm_count
    length = block * tm_count

    sums_chains = ((4, 2), (2, 2), (1, 2))

    by_parts = stem_rows % 16 == 0 and rows % 16 == 0 and dp_chains == ((2, 4), (1, 2))
    span = 128 * tm_count
    lane = jnp.arange(span, dtype=jnp.int32)
    grouped = (lane // rows) % tm_count * 128 + lane // (rows * tm_count) * rows + lane % rows
    chunks = rows // stem_rows
    if by_parts:
        up_parts = up_columns(up_weight, rows, tm_count)
        sent, pack = prepare(
            mel_pieces[0], dest_owner[0], dest_slot[0], after(stem_weight, up_parts[0]),
            down_weight, depth_kernel, gain_pre, gain_post, dp_count,
        )
    else:
        sent = order_pieces(mel_pieces[0], dest_owner[0], dest_slot[0], dp_count)
        up_parts = regroup_columns(up_weight, lane, grouped, "tm", tm_count)
        beside = jnp.broadcast_to(jnp.tile(gain_pre, 128 // rows)[None, :], (stem_rows, 128))
        small = jnp.concatenate(
            [depth_kernel, gain_post[:, None], jnp.zeros((rows, 128 - taps - 1), BF16)], axis=1
        )
        folded = [
            value[q : q + stem_rows]
            for value in (small, down_weight)
            for q in range(0, rows, stem_rows)
        ]
        pack = jnp.concatenate([stem_weight, beside] + folded, axis=1)

    up_parts = [up_parts[0]] + [swap(up_parts[k], "tm", k) for k in range(1, tm_count)]
    up_mine = place_parts(up_parts, "tm", 1, tm_count, 0).reshape(tm_count * rows, 2 * held)
    pack_near = gather_stage(pack, "dp", *dp_chains[0], 0)
    up_sides = swap_parts([up_mine] * dp_chains[0][1], "dp", dp_chains[0])
    stem_mine, small_all, down_full = split_rest(
        pack_near, "dp", dp_chains, ((channels + 128, 1), (128, chunks), (channels, chunks))
    )
    stem_mine = stem_mine.reshape(dp_count, stem_rows, channels + 128)
    small_all = small_all.reshape(held, 128)
    down_full = down_full.reshape(held, channels)

    pieces = mel_pieces.shape[1]
    capacity = max(2, 2 * pieces // dp_count)
    arrived = lax.all_to_all(
        after(sent, pack_near).reshape(dp_count, capacity, -1),
        "dp",
        split_axis=0,
        concat_axis=0,
        tiled=True,
    ).reshape(dp_count * capacity, -1)
    up_near = place_parts(up_sides, "dp", *dp_chains[0], 0)
    frames = place_frames(after(arrived, up_near), pieces, features)
    frame_parts = gather_parts(frames, "tm", tm_chains)
    stem_parts = gather_parts(stem_mine, "tm", tm_chains, frames)
    frames = place_parts(frame_parts, "tm", 1, tm_count, 0).reshape(length, features)
    stem_all = place_parts(stem_parts, "tm", 1, tm_count, 1)
    stem_all = stem_all.reshape(features, channels + 128)

    grad_out = out_grad[0]
    grad_first = after(grad_out, up_near)
    hierarchical = list(tm_chains) == [(2, 2), (1, 2)]
    if hierarchical:
        grad_parts = [grad_first, swap(grad_first, "tm", 1), swap(grad_first, "tm", 2)]
    else:
        grad_parts = gather_parts(grad_first, "tm", tm_chains)

    segments = spread_segments(segment_ids)

    extra = 16
    normed, stem_pre, gain_one, frames_turned = stem_forward(
        frames, stem_all, tm_count, "tm", rows, extra
    )
    up_full = gather_rest(up_near, "dp", dp_chains).reshape(channels, 2 * held)
    grad_parts = lax.optimization_barrier((grad_parts, normed))[0]
    if hierarchical:
        grad_parts = grad_parts + [swap(grad_parts[2], "tm", 1)]
    linear, gate_sig, gated = up_forward(normed, up_full)
    conv, stats, turned = conv_forward(gated, small_all, segments, taps)
    stats = swap_all(stats, "tm")
    grad_parts = lax.optimization_barrier((grad_parts, conv))[0]
    grad_out_all = place_parts(grad_parts, "tm", 1, tm_count, 0).reshape(length, channels)
    grad_act = multiply_turned(grad_out_all, down_full)
    activated, conv_hat, grad_hat, inverse, sums, gain_post_term = activate(
        conv, stats, turned, grad_act, taps
    )
    sums = swap_all(sums, "tm")
    if by_parts:
        down_terms = part_terms(activated, grad_out_all, False, "dp", sums_chains)
        normed_turned = turn(normed)
        grad_hat = after(grad_hat, normed_turned)
    else:
        down_terms = [message_terms(activated, grad_out_all, dp_count, tm_count)]
    down_terms = lax.optimization_barrier((down_terms, *sums))[0]
    if by_parts:
        down_parts = swap_parts(down_terms, "dp", sums_chains[-1])

    grad_hat = after(grad_hat, *down_terms)
    grad_proj, kernel_term = conv_backward(
        grad_hat, conv_hat, inverse, sums, gated, segments, linear, gate_sig, turned, taps,
        gain_post_term,
    )

    own_terms, *other_terms = block_terms(
        after(grad_proj, *down_parts[1:]) if by_parts else grad_proj, up_full, True, "tm", tm_count
    )
    if by_parts:
        up_terms = part_terms(
            after(normed_turned, *other_terms), grad_proj, True, "dp", sums_chains
        )
        up_parts = swap_parts(up_terms, "dp", sums_chains[-1])
    else:
        up_terms = [message_terms(normed, grad_proj, dp_count, tm_count)]
    grad_far, grad_parts, grad_passed = block_sum(other_terms, "tm", tm_chains, up_terms[-1])
    if by_parts:
        down_parts[0] = after(down_parts[0], grad_passed)
        down_parts = add_parts(down_parts, "dp", sums_chains[1])
        down_parts = swap_parts(down_parts, "dp", sums_chains[1])
        own_terms = own_terms
    y_own, *y_others = block_terms(
        after(activated, grad_passed), down_full, False, "tm", tm_count
    )
    grad_stem_pre = stem_backward(
        own_terms, grad_parts + [grad_far], stem_pre, grad_out, gain_one, extra
    )
    if by_parts:
        up_parts[0] = after(up_parts[0], grad_stem_pre)
        up_parts = add_parts(up_parts, "dp", sums_chains[1])
        down_parts[0] = after(down_parts[0], up_parts[-1])
        down_parts = add_parts(down_parts, "dp", sums_chains[0])
        down_parts = swap_parts(down_parts, "dp", sums_chains[0])
        grad_stem_parts = gather_parts(grad_stem_pre, "tm", tm_chains, down_parts[0])
        up_parts = reduce_rest(up_parts, "dp", sums_chains[:2])
    else:
        grad_stem_parts = gather_parts(grad_stem_pre, "tm", tm_chains)
    y_far, y_parts, _ = block_sum(y_others, "tm", tm_chains, grad_stem_parts[2])
    if by_parts:
        stem_terms = stem_message(
            frames_turned, grad_stem_parts, kernel_term, "dp", sums_chains, stem_rows
        )
        stem_sums = reduce_rest(stem_terms, "dp", sums_chains)
    else:
        stem_sum = sum(
            jnp.dot(frames_turned[k], grad_stem_parts[k], preferred_element_type=F32)
            for k in range(tm_count)
        )
        share = features // tm_count
        gain_term = stem_sum[share].reshape(dp_count, 1, tm_count * rows)
        gain_term = jnp.pad(gain_term, ((0, 0), (0, 0), (0, channels - tm_count * rows)))
        stem_terms = stem_sum[:share].reshape(dp_count, stem_rows, channels)
        folds = channels // held
        small_term = kernel_term.reshape(folds, -1, held).transpose(1, 0, 2).reshape(-1, channels)
        small_term = jnp.broadcast_to(small_term[None], (dp_count,) + small_term.shape)
        stem_terms = jnp.concatenate([stem_terms, small_term, gain_term], axis=1)
        stem_terms = jnp.pad(stem_terms.astype(BF16), ((0, 0), (0, 7), (0, 0)))
        stem_sums = [
            lax.all_to_all(stem_terms, "dp", split_axis=0, concat_axis=0, tiled=True)
        ]
    if by_parts:
        up_parts[0] = after(up_parts[0], *stem_terms)
        up_parts = cut_columns(up_parts, down_parts, "tm")
        up_parts = swap_all_parts(up_parts, "tm")
        grad_up, grad_down = mix_columns(up_parts, "tm", tm_count * rows, rows)
    else:
        down_sums = lax.all_to_all(
            down_terms[0], ("dp", "tm"), split_axis=0, concat_axis=0, tiled=True
        )
        grad_down = jnp.sum(
            down_sums.reshape(dp_count, tm_count * rows, held).astype(F32), axis=0
        )
        up_sums = lax.all_to_all(
            up_terms[0], ("dp", "tm"), split_axis=0, concat_axis=0, tiled=True
        )
        up_sums = up_sums.reshape(dp_count, tm_count, tm_count * rows, 128)
        spread = one_hot(lane, grouped).reshape(tm_count, 128, span)
        grad_up = jnp.einsum("ijab,jbc->ac", up_sums, spread, preferred_element_type=F32)
    y_out = finish_rows(stem_pre, y_own, y_parts + [y_far])
    grad_stem, grad_kernel, grad_gain_post, grad_gain_pre = stem_finish(
        stem_sums, stem_rows, rows, taps, "tm"
    )
    grad_gain_post, grad_gain_pre = grad_gain_post[0], grad_gain_pre[0]
    return (y_out[None], grad_stem, grad_up, grad_down, grad_kernel, grad_gain_pre, grad_gain_post)


def solution(mesh):
    return jax.shard_map(
        per_device,
        mesh=mesh,
        in_specs=(
            P("dp", "tm", None),
            P("dp", "tm"),
            P("dp", "tm"),
            P("dp", None),
            P("dp", "tm", None),
            P(("dp", "tm"), None),
            P(("dp", "tm"), None),
            P(("dp", "tm"), None),
            P(("dp", "tm"), None),
            P(("dp", "tm")),
            P(("dp", "tm")),
        ),
        out_specs=(
            P("dp", "tm", None),
            P(("dp", "tm"), None),
            P("dp", "tm"),
            P("dp", "tm"),
            P(("dp", "tm"), None),
            P(("dp", "tm")),
            P(("dp", "tm")),
        ),
        check_vma=False,
    )
```

```python
import jax
import jax.numpy as jnp
from jax import lax
from jax.experimental import pallas as pl
from jax.experimental.pallas import tpu as pltpu
from jax.sharding import PartitionSpec as P

NORM_EPS = 1e-05
BF16 = jnp.bfloat16
F32 = jnp.float32


def stages_of(sizes):
    if sizes["dp"] == 8 and sizes["tm"] == 4:
        return {"dp": ((2, 4), (1, 2)), "tm": ((2, 2), (1, 2))}
    if sizes["dp"] == 64 and sizes["tm"] == 4:
        return {"dp": ((8, 8), (2, 4), (1, 2)), "tm": ((1, 4),)}
    return {axis: ((1, size),) for axis, size in sizes.items()}


def swap(value, axis, mask):
    size = lax.axis_size(axis)
    return lax.ppermute(value, axis, [(i, i ^ mask) for i in range(size)])


VMEM_LIMIT = 16 << 20


def kernel_params():
    return pltpu.CompilerParams(vmem_limit_bytes=VMEM_LIMIT)


def costs(microseconds):
    return pl.CostEstimate(
        flops=int(microseconds * 2e10), bytes_accessed=1 << 16, transcendentals=0
    )


def after(value, *others):
    return lax.optimization_barrier((value,) + others)[0]


def place_parts(parts, axis, stride, size, dim):
    shape = parts[0].shape
    out_shape = shape[:dim] + (size,) + shape[dim:]

    def kernel(*refs):
        place = (lax.axis_index(axis) // stride) % size
        for k in range(size):
            refs[size][(slice(None),) * dim + (place ^ k,)] = refs[k][...]

    return pl.pallas_call(
        kernel,
        out_shape=jax.ShapeDtypeStruct(out_shape, parts[0].dtype),
        compiler_params=kernel_params(),
        cost_estimate=costs(2.74),
    )(*parts)


def gather_stage(value, axis, stride, size, dim):
    parts = [value] + [swap(value, axis, k * stride) for k in range(1, size)]
    return place_parts(parts, axis, stride, size, dim)


def gather_rest(value, axis, chains):
    shape = value.shape[1:]
    for dim, (stride, size) in enumerate(chains[1:], 1):
        value = gather_stage(value, axis, stride, size, dim)
    return value.reshape((-1,) + shape)


def block_terms(left, right, transposed, axis, count):
    block = left.shape[0] // count
    width = right.shape[0] if transposed else right.shape[1]
    dims = (((1,), (1 if transposed else 0,)), ((), ()))

    def kernel(left_ref, right_ref, own, *refs):
        others, terms = refs[:-1], refs[-1]
        place = lax.axis_index(axis)
        terms[...] = lax.dot_general(
            left_ref[...], right_ref[...], dims, preferred_element_type=F32
        )
        for k in range(count):
            start = pl.multiple_of((place ^ k) * block, block)
            if k == 0:
                own[...] = terms[pl.ds(start, block), :]
            else:
                others[k - 1][...] = terms[pl.ds(start, block), :].astype(BF16)

    return pl.pallas_call(
        kernel,
        out_shape=[jax.ShapeDtypeStruct((block, width), F32)]
        + [jax.ShapeDtypeStruct((block, width), BF16)] * (count - 1),
        scratch_shapes=[pltpu.VMEM((count * block, width), F32)],
        compiler_params=kernel_params(),
        cost_estimate=costs(0.365),
    )(left, right)


def block_sum(others, axis, chains, first=None):
    if list(chains) == [(2, 2), (1, 2)]:
        near, passed = swap(others[0], axis, 1), swap(others[2], axis, 1)
        passed = add_pair(others[1], passed)
        if first is not None:
            passed = after(passed, first)
        return swap(passed, axis, 2), [near], passed
    parts = [swap(other, axis, k) for k, other in enumerate(others, 1)]
    return parts[-1], parts[:-1], others[-1]


def add_pair(one, other):
    def kernel(one_ref, other_ref, out):
        out[...] = (one_ref[...].astype(F32) + other_ref[...].astype(F32)).astype(BF16)

    return pl.pallas_call(
        kernel,
        out_shape=jax.ShapeDtypeStruct(one.shape, BF16),
        compiler_params=kernel_params(),
        cost_estimate=costs(1.39),
    )(one, other)


def finish_rows(stem_pre, own, parts):
    def kernel(pre_ref, own_ref, *refs):
        total = own_ref[...]
        for part in refs[:-1]:
            total = total + part[...].astype(F32)
        pre = pre_ref[...]
        stem_out = (pre * jax.nn.sigmoid(pre)).astype(BF16).astype(F32)
        refs[-1][...] = (stem_out + total).astype(BF16)

    return pl.pallas_call(
        kernel,
        out_shape=jax.ShapeDtypeStruct(own.shape, BF16),
        compiler_params=kernel_params(),
        cost_estimate=costs(0.527),
    )(stem_pre, own, *parts)


def turn(value):
    rows, columns = value.shape

    def kernel(source, out):
        for c in range(0, columns, 128):
            out[c : c + 128, :] = source[:, c : c + 128].astype(F32).T.astype(BF16)

    return pl.pallas_call(
        kernel,
        out_shape=jax.ShapeDtypeStruct((columns, rows), value.dtype),
        compiler_params=kernel_params(),
        cost_estimate=costs(2.02),
    )(value)


def part_terms(left, right, turned, axis, chains):
    total = lax.axis_size(axis)
    stride, size = chains[-1]
    rows, columns = left.shape[0 if turned else 1] // total, right.shape[1]
    step = max(1, 512 // rows) if turned else max(1, 128 // rows)

    def kernel(left_ref, right_ref, *outs):
        place = (lax.axis_index(axis) // stride) % size
        for i in range(0, total, step):
            block = slice(i * rows, (i + step) * rows)
            if turned:
                term = jnp.dot(left_ref[block, :], right_ref[...], preferred_element_type=F32)
            else:
                term = lax.dot_general(
                    left_ref[:, block],
                    right_ref[...],
                    (((0,), (0,)), ((), ())),
                    preferred_element_type=F32,
                )
            term = term.astype(BF16)
            for n in range(step):
                for k in range(size):

                    @pl.when((i + n) % size ^ place == k)
                    def _():
                        outs[k][(i + n) // size] = term[n * rows : (n + 1) * rows]

    return pl.pallas_call(
        kernel,
        out_shape=[jax.ShapeDtypeStruct((total // size, rows, columns), BF16)] * size,
        compiler_params=kernel_params(),
        cost_estimate=costs(0.818),
    )(left, right)


def swap_all_parts(parts, axis):
    return [parts[0]] + [swap(part, axis, k) for k, part in enumerate(parts[1:], 1)]


def swap_parts(parts, axis, chain):
    stride, _ = chain
    return [parts[0]] + [swap(part, axis, k * stride) for k, part in enumerate(parts[1:], 1)]


def add_parts(parts, axis, chain):
    stride, size = chain
    shape = (parts[0].shape[0] // size,) + parts[0].shape[1:]

    def kernel(*refs):
        place = (lax.axis_index(axis) // stride) % size
        for a in range(shape[0]):
            for k in range(size):
                at = a * size + (place ^ k)
                total = sum(part[at].astype(F32) for part in refs[: len(parts)])
                refs[len(parts) + k][a] = total.astype(BF16)

    return pl.pallas_call(
        kernel,
        out_shape=[jax.ShapeDtypeStruct(shape, BF16)] * size,
        compiler_params=kernel_params(),
        cost_estimate=costs(0.316),
    )(*parts)


def reduce_rest(parts, axis, chains):
    parts = swap_parts(parts, axis, chains[-1])
    for chain in reversed(chains[:-1]):
        parts = swap_parts(add_parts(parts, axis, chain), axis, chain)
    return parts


def cut_columns(first, second, axis):
    count = lax.axis_size(axis)
    terms = len(first)
    _, rows, columns = first[0].shape
    _, below, wide = second[0].shape
    share = columns // count
    folds = wide // columns

    def kernel(*refs):
        place = lax.axis_index(axis)
        upper = sum(part[0].astype(F32) for part in refs[:terms]).astype(BF16)
        lower = sum(part[0].astype(F32) for part in refs[terms : 2 * terms]).astype(BF16)
        for j in range(count):
            for k in range(count):

                @pl.when(place ^ j == k)
                def _():
                    out = refs[2 * terms + k]
                    out[:rows, :] = upper[:, j * share : (j + 1) * share]
                    for f in range(folds):
                        start = (j * folds + f) * share
                        out[rows + f * below : rows + (f + 1) * below, :] = lower[
                            :, start : start + share
                        ]

    return pl.pallas_call(
        kernel,
        out_shape=[jax.ShapeDtypeStruct((rows + folds * below, share), BF16)] * count,
        compiler_params=kernel_params(),
        cost_estimate=costs(1.37),
    )(*first, *second)


def mix_columns(parts, axis, rows, small):
    count = len(parts)
    height, share = parts[0].shape
    span = share * count
    folds = (height - rows) // small

    def kernel(*refs):
        place = lax.axis_index(axis)
        upper, lower = refs[count:]
        at, to = iota((share, span), 0), iota((share, span), 1)
        total = jnp.zeros((rows, span), F32)
        for k in range(count):
            want = at // small * (small * count) + (place ^ k) * small + at % small
            spread = table(to == want)
            total = total + jnp.dot(refs[k][:rows, :], spread, preferred_element_type=F32)
            start = pl.multiple_of((place ^ k) * small, small)
            for f in range(folds):
                lower[pl.ds(start, small), f * share : (f + 1) * share] = refs[k][
                    rows + f * small : rows + (f + 1) * small, :
                ].astype(F32)
        upper[...] = total

    return pl.pallas_call(
        kernel,
        out_shape=[
            jax.ShapeDtypeStruct((rows, span), F32),
            jax.ShapeDtypeStruct((count * small, folds * share), F32),
        ],
        compiler_params=kernel_params(),
        cost_estimate=costs(0.334),
    )(*parts)


def message_terms(left, right, parts, sides):
    rows, columns = left.shape[1] // parts, right.shape[1] // sides
    terms = jnp.dot(left.T, right, preferred_element_type=F32).astype(BF16)
    terms = terms.reshape(parts, rows, sides, columns).transpose(0, 2, 1, 3)
    return terms.reshape(parts * sides, rows, columns)


def regroup_columns(weight, lane, grouped, axis, count):
    rows, columns = weight.shape
    span = lane.shape[0]
    groups = columns // span
    parts = jnp.dot(
        weight.reshape(rows * groups, span), one_hot(grouped, lane), preferred_element_type=F32
    ).astype(BF16)
    parts = parts.reshape(rows, groups, count, 128).transpose(2, 0, 1, 3)
    parts = parts.reshape(count, rows, groups * 128)
    return [
        lax.dynamic_index_in_dim(parts, lax.axis_index(axis) ^ k, 0, keepdims=False)
        for k in range(count)
    ]


def stem_backward(own, parts, stem_pre, grad_out, gain, extra):
    block, channels = own.shape

    def kernel(own_ref, pre_ref, out_grad_ref, gain_ref, *refs):
        out = refs[-1]
        pre = pre_ref[...]
        sigma = jax.nn.sigmoid(pre)
        hat, inverse = standardize((pre * sigma).astype(BF16).astype(F32))
        grad = own_ref[...]
        for part in refs[:-1]:
            grad = grad + part[...].astype(F32)
        out[block:, :] = jnp.concatenate(
            [jnp.sum(grad * hat, axis=0, keepdims=True), jnp.zeros((extra - 1, channels), F32)]
        ).astype(BF16)
        back = grad * gain_ref[...]
        first = jnp.mean(back, axis=-1, keepdims=True)
        second = jnp.mean(back * hat, axis=-1, keepdims=True)
        stem_out = out_grad_ref[...].astype(F32) + (back - first - hat * second) * inverse
        out[:block, :] = (stem_out * (sigma * (1.0 + pre * (1.0 - sigma)))).astype(BF16)

    return pl.pallas_call(
        kernel,
        out_shape=jax.ShapeDtypeStruct((block + extra, channels), BF16),
        compiler_params=kernel_params(),
        cost_estimate=costs(0.391),
    )(own, stem_pre, grad_out, gain, *parts)


def standardize(values):
    centered = values - jnp.mean(values, axis=-1, keepdims=True)
    inverse = lax.rsqrt(jnp.mean(centered * centered, axis=-1, keepdims=True) + NORM_EPS)
    return (centered * inverse, inverse)


def gather_parts(value, axis, chains, first=None):
    if list(chains) == [(2, 2), (1, 2)]:
        far = swap(value, axis, 2)
        if first is not None:
            far = after(far, first)
        return [value, swap(value, axis, 1), far, swap(far, axis, 1)]
    return [value] + [swap(value, axis, k) for k in range(1, lax.axis_size(axis))]


def swap_all(value, axis):
    return [value] + [swap(value, axis, k) for k in range(1, lax.axis_size(axis))]


def split_parts(parts, axis, stride, size, dim, cuts):
    shape = parts[0].shape
    lead = shape[:dim] + (size,) + shape[dim:-2]
    rows = shape[-2]

    def kernel(*refs):
        place = (lax.axis_index(axis) // stride) % size
        inner = (slice(None),) * (len(lead) - dim - 1)
        for k in range(size):
            target = (slice(None),) * dim + (place ^ k,) + inner
            start = 0
            for n, (width, pieces) in enumerate(cuts):
                for q in range(pieces):
                    refs[size + n][target + (q,)] = refs[k][..., start : start + width]
                    start += width

    return pl.pallas_call(
        kernel,
        out_shape=[
            jax.ShapeDtypeStruct(lead + (pieces, rows, width), parts[0].dtype)
            for width, pieces in cuts
        ],
        compiler_params=kernel_params(),
        cost_estimate=costs(0.398),
    )(*parts)


def split_rest(value, axis, chains, cuts):
    for dim, (stride, size) in enumerate(chains[1:], 1):
        parts = [value] + [swap(value, axis, k * stride) for k in range(1, size)]
        if dim == len(chains) - 1:
            return split_parts(parts, axis, stride, size, dim, cuts)
        value = place_parts(parts, axis, stride, size, dim)


def iota(shape, dim):
    return lax.broadcasted_iota(jnp.int32, shape, dim)


def table(flags):
    return jnp.where(flags, 1.0, 0.0).astype(BF16)


def fetch(sources, held, sems):
    copies = [
        pltpu.make_async_copy(source, target, sems.at[k])
        for k, (source, target) in enumerate(zip(sources, held))
    ]
    for copy in copies:
        copy.start()
    for copy in copies:
        copy.wait()


def fetching_call(kernel, inputs, out_shape, cost):
    return pl.pallas_call(
        kernel,
        out_shape=out_shape,
        in_specs=[pl.BlockSpec(memory_space=pl.ANY)] * len(inputs),
        scratch_shapes=[pltpu.VMEM(value.shape, value.dtype) for value in inputs]
        + [pltpu.SemaphoreType.DMA((len(inputs),))],
        cost_estimate=cost,
    )(*inputs)


def up_columns(up, rows, tm_count):
    span = 128 * tm_count
    groups = up.shape[1] // span

    def kernel(source, *refs):
        up_parts, (up_ref, sems) = refs[:tm_count], refs[tm_count:]
        fetch([source], [up_ref], sems)
        place = lax.axis_index("tm")
        at, to = iota((span, 128), 0), iota((span, 128), 1)
        for k in range(tm_count):
            want = to // rows * (rows * tm_count) + (place ^ k) * rows + to % rows
            pick = table(at == want)
            for g in range(groups):
                up_parts[k][:, g * 128 : (g + 1) * 128] = jnp.dot(
                    up_ref[:, g * span : (g + 1) * span], pick, preferred_element_type=F32
                ).astype(BF16)

    return fetching_call(
        kernel,
        (up,),
        [jax.ShapeDtypeStruct((rows, up.shape[1] // tm_count), BF16)] * tm_count,
        costs(0.761),
    )


def prepare(mel, owner, slot, stem, down, taps, gain_one, gain_two, dp_count):
    pieces, values = mel.shape
    capacity = max(2, 2 * pieces // dp_count)
    slots = dp_count * capacity
    stem_rows, channels = stem.shape
    rows, tap_count = taps.shape
    chunks = rows // stem_rows
    beyond = channels + 128 * (chunks + 1)
    inputs = (
        stem, taps, gain_one[None, :], gain_two[None, :], owner[None, :], slot[None, :], mel, down
    )
    count = len(inputs)

    def kernel(*refs):
        sent, pack = refs[count : count + 2]
        held = refs[count + 2 : -1]
        fetch(refs[:count], held, refs[-1])
        stem_ref, taps_ref, one_ref, two_ref, owner_ref, slot_ref, mel_ref, down_ref = held
        pack[:, :channels] = stem_ref[...]
        lane = iota((rows, 128), 1)
        spread = table(lane % rows == iota((rows, 128), 0))
        gain = jnp.broadcast_to(one_ref[...].astype(F32), (stem_rows, rows)).astype(BF16)
        pack[:, channels : channels + 128] = jnp.dot(
            gain, spread, preferred_element_type=F32
        ).astype(BF16)
        tap_lane = table(iota((tap_count, 128), 1) == iota((tap_count, 128), 0))
        square = iota((rows, rows), 0) == iota((rows, rows), 1)
        diagonal = jnp.where(
            square, jnp.broadcast_to(two_ref[...].astype(F32), (rows, rows)), 0.0
        ).astype(BF16)
        small = jnp.dot(taps_ref[...], tap_lane, preferred_element_type=F32)
        small = small + jnp.dot(diagonal, table(lane == tap_count), preferred_element_type=F32)
        for q in range(chunks):
            lanes = slice(channels + 128 * (q + 1), channels + 128 * (q + 2))
            pack[:, lanes] = small[q * stem_rows : (q + 1) * stem_rows].astype(BF16)
            lanes = slice(beyond + channels * q, beyond + channels * (q + 1))
            pack[:, lanes] = down_ref[q * stem_rows : (q + 1) * stem_rows, :]

        owners = jnp.broadcast_to(owner_ref[...].astype(F32), (pieces, pieces))
        earlier = iota((pieces, pieces), 0) < iota((pieces, pieces), 1)
        same = jnp.where(owners.T == owners, jnp.where(earlier, 1.0, 0.0), 0.0)
        target = owners[:1] * float(capacity) + jnp.sum(same, axis=0, keepdims=True)
        target = jnp.broadcast_to(target, (slots, pieces)).astype(jnp.int32)
        chosen = target == iota((slots, pieces), 0)
        pick = table(chosen)
        sent[:, :values] = jnp.dot(pick, mel_ref[...], preferred_element_type=F32).astype(BF16)
        labels = jnp.broadcast_to(slot_ref[...].astype(F32) + 1.0, (slots, pieces))
        label = jnp.sum(jnp.where(chosen, labels, 0.0), axis=1, keepdims=True)
        sent[:, values:] = jnp.broadcast_to(label, (slots, 128)).astype(BF16)

    return fetching_call(
        kernel,
        inputs,
        [
            jax.ShapeDtypeStruct((slots, values + 128), BF16),
            jax.ShapeDtypeStruct((stem_rows, beyond + channels * chunks), BF16),
        ],
        costs(7),
    )


def place_frames(arrived, pieces, features):
    slots, width = arrived.shape
    steps = (width - 128) // features

    def kernel(arrived_ref, out):
        labels = arrived_ref[:, steps * features :].astype(F32).T[:1]
        want = jnp.broadcast_to(labels, (pieces * steps, slots)).astype(jnp.int32)
        row = lax.broadcasted_iota(jnp.int32, (pieces * steps, slots), 0)
        total = jnp.zeros((pieces * steps, features), F32)
        for q in range(steps):
            put = jnp.where(row == (want - 1) * steps + q, 1.0, 0.0).astype(BF16)
            total = total + jnp.dot(
                put, arrived_ref[:, q * features : (q + 1) * features], preferred_element_type=F32
            )
        out[...] = total.astype(BF16)

    return pl.pallas_call(
        kernel,
        out_shape=jax.ShapeDtypeStruct((pieces * steps, features), BF16),
        compiler_params=kernel_params(),
        cost_estimate=costs(0.926),
    )(arrived)


def turn_frames(frames, count, axis, stem_rows, extra):
    length, features = frames.shape
    block, share = length // count, features // count

    def kernel(frames_ref, turned):
        place = lax.axis_index(axis)
        feature = lax.broadcasted_iota(jnp.int32, (features, share), 0)
        chosen = lax.broadcasted_iota(jnp.int32, (features, share), 1)
        chosen = (chosen // stem_rows * count + place) * stem_rows + chosen % stem_rows
        pick = jnp.where(feature == chosen, 1.0, 0.0).astype(BF16)
        corner = lax.broadcasted_iota(jnp.int32, (extra, extra), 0)
        corner = corner + lax.broadcasted_iota(jnp.int32, (extra, extra), 1)
        corner = jnp.where(corner == 0, 1.0, 0.0).astype(BF16)
        for k in range(count):
            start = pl.multiple_of((place ^ k) * block, block)
            turned[k, :share, :block] = lax.dot_general(
                pick,
                frames_ref[pl.ds(start, block), :],
                (((0,), (1,)), ((), ())),
                preferred_element_type=F32,
            ).astype(BF16)
            turned[k, share:, :block] = jnp.zeros((extra, block), BF16)
            turned[k, :share, block:] = jnp.zeros((share, extra), BF16)
            turned[k, share:, block:] = corner

    return pl.pallas_call(
        kernel,
        out_shape=jax.ShapeDtypeStruct((count, share + extra, block + extra), BF16),
        compiler_params=kernel_params(),
        cost_estimate=costs(1.0),
    )(frames)


def stem_forward(frames, stem_all, count, axis, rows):
    length = frames.shape[0]
    features, width = stem_all.shape
    channels = width - 128
    block = length // count
    stem_rows = features * rows // channels

    def kernel(frames_ref, stem_ref, normed, pre_own, gain_out):
        place = lax.axis_index(axis)
        beside = stem_ref[:, channels:].astype(F32)
        gains = []
        for g in range(channels // 128):
            row = lax.broadcasted_iota(jnp.int32, (features, 128), 0)
            lane = lax.broadcasted_iota(jnp.int32, (features, 128), 1) + g * 128
            gains.append(
                jnp.sum(
                    jnp.where(row == lane // rows * stem_rows, beside, 0.0), axis=0, keepdims=True
                )
            )
        gain_out[...] = jnp.concatenate(gains, axis=1)
        for b in range(count):
            pre = jnp.dot(
                frames_ref[b * block : (b + 1) * block, :],
                stem_ref[:, :channels],
                preferred_element_type=F32,
            )
            hat, _ = standardize((pre * jax.nn.sigmoid(pre)).astype(BF16).astype(F32))
            normed[b * block : (b + 1) * block, :] = (hat * gain_out[...]).astype(BF16)

            @pl.when(place == b)
            def _():
                pre_own[...] = pre

    return pl.pallas_call(
        kernel,
        out_shape=[
            jax.ShapeDtypeStruct((length, channels), BF16),
            jax.ShapeDtypeStruct((block, channels), F32),
            jax.ShapeDtypeStruct((1, channels), F32),
        ],
        compiler_params=kernel_params(),
        cost_estimate=costs(4.22),
    )(frames, stem_all)


PAD = 16


def up_forward(normed, up):
    length = normed.shape[0]
    held = up.shape[1] // 2
    step = min(128, length)

    def kernel(normed_ref, up_ref, linear, gate, gated):
        edge = jnp.zeros((PAD, held), F32)
        gated[:PAD, :] = edge
        gated[PAD + length :, :] = edge
        for b in range(0, length, step):
            proj = jnp.dot(normed_ref[b : b + step, :], up_ref[...], preferred_element_type=F32)
            sigma = jax.nn.sigmoid(proj[:, held:])
            linear[b : b + step, :] = proj[:, :held]
            gate[b : b + step, :] = sigma
            gated[PAD + b : PAD + b + step, :] = (proj[:, :held] * sigma).astype(BF16).astype(F32)

    return pl.pallas_call(
        kernel,
        out_shape=[
            jax.ShapeDtypeStruct((length, held), F32),
            jax.ShapeDtypeStruct((length, held), F32),
            jax.ShapeDtypeStruct((length + 2 * PAD, held), F32),
        ],
        compiler_params=kernel_params(),
        cost_estimate=costs(0.396),
    )(normed, up)


def columns_of(first, second):
    rows = first.shape[0]
    lane = lax.broadcasted_iota(jnp.int32, (rows, 128), 1)
    both = jnp.where(lane == 0, first, jnp.where(lane == 1, second, 0.0))
    return both.T[:8]


def rows_of(table):
    rows = table.shape[1]
    turned = jnp.concatenate([table, jnp.zeros((120, rows), F32)], axis=0).T
    return turned[:, :1], turned[:, 1:2]


def spread_segments(segments):
    length = segments.shape[1]

    def kernel(source, out):
        edge = jnp.full((PAD, 128), -1.0, F32)
        out[:PAD, :] = edge
        out[PAD + length :, :] = edge
        out[PAD : PAD + length, :] = jnp.broadcast_to(
            source[...].astype(F32), (128, length)
        ).T

    return pl.pallas_call(
        kernel,
        out_shape=jax.ShapeDtypeStruct((length + 2 * PAD, 128), F32),
        compiler_params=kernel_params(),
        cost_estimate=costs(0.877),
    )(segments)


def multiply_turned(left, right):
    def kernel(left_ref, right_ref, out):
        out[...] = lax.dot_general(
            left_ref[...], right_ref[...], (((1,), (1,)), ((), ())), preferred_element_type=F32
        )

    return pl.pallas_call(
        kernel,
        out_shape=jax.ShapeDtypeStruct((left.shape[0], right.shape[0]), F32),
        compiler_params=kernel_params(),
        cost_estimate=costs(0.594),
    )(left, right)


TILE = 64


def conv_forward(gated, small, segments, taps):
    length, held = gated.shape[0] - 2 * PAD, gated.shape[1]
    margin = (taps - 1) // 2

    def kernel(gated_ref, small_ref, seg_ref, conv, stats, turned, gated_near, seg_near):
        turned[...] = small_ref[...].astype(F32).T

        def tile(t, carry):
            base = pl.multiple_of(t * TILE, TILE)
            gated_near[...] = gated_ref[pl.ds(base, TILE + 2 * PAD), :]
            seg_near[...] = seg_ref[pl.ds(base, TILE + 2 * PAD), :]
            centre = seg_near[PAD : PAD + TILE, :]
            sums = [jnp.zeros((TILE, 128), F32) for _ in range(held // 128)]
            for k in range(taps):
                shift = PAD + k - margin
                inside = seg_near[shift : shift + TILE, :] == centre
                for g in range(held // 128):
                    lanes = slice(g * 128, (g + 1) * 128)
                    value = gated_near[shift : shift + TILE, lanes]
                    sums[g] = sums[g] + jnp.where(inside, value, 0.0) * turned[k : k + 1, lanes]
            conv[pl.ds(base, TILE), :] = jnp.concatenate(sums, axis=1)
            return carry

        lax.fori_loop(0, length // TILE, tile, 0)
        value = conv[...]
        mean = jnp.mean(value, axis=-1, keepdims=True)
        centered = value - mean
        stats[...] = columns_of(mean, jnp.sum(centered * centered, axis=-1, keepdims=True))

    return pl.pallas_call(
        kernel,
        out_shape=[
            jax.ShapeDtypeStruct((length, held), F32),
            jax.ShapeDtypeStruct((8, length), F32),
            jax.ShapeDtypeStruct((128, held), F32),
        ],
        scratch_shapes=[
            pltpu.VMEM((TILE + 2 * PAD, held), F32),
            pltpu.VMEM((TILE + 2 * PAD, 128), F32),
        ],
        compiler_params=kernel_params(),
        cost_estimate=costs(1.03),
    )(gated, small, segments)


def activate(conv, stats, turned, grad_act, taps):
    length, held = conv.shape
    count = len(stats)

    def kernel(conv_ref, turned_ref, grad_ref, *refs):
        tables, (active, hat_out, grad_hat_out, inverse_out, sums, gain_term) = (
            refs[:count], refs[count:],
        )
        means = [table[0:1, :] for table in tables]
        mean = sum(means) * (1.0 / count)
        squares = sum(table[1:2, :] for table in tables)
        squares = squares + held * sum((one - mean) * (one - mean) for one in means)
        inverse = lax.rsqrt(squares * (1.0 / (held * count)) + NORM_EPS)
        both = jnp.concatenate([mean, inverse, jnp.zeros((6, length), F32)], axis=0)
        mean, inverse = rows_of(both)
        inverse_out[...] = jnp.broadcast_to(inverse, (length, 128))
        gain = turned_ref[taps : taps + 1, :]
        hat = (conv_ref[...] - mean) * inverse
        scaled = hat * gain
        sigma = jax.nn.sigmoid(scaled)
        active[...] = (scaled * sigma).astype(BF16)
        grad_scaled = grad_ref[...] * (sigma * (1.0 + scaled * (1.0 - sigma)))
        gain_term[...] = jnp.sum(grad_scaled * hat, axis=0, keepdims=True)
        grad_hat = grad_scaled * gain
        hat_out[...] = hat
        grad_hat_out[...] = grad_hat
        sums[...] = columns_of(
            jnp.sum(grad_hat, axis=-1, keepdims=True),
            jnp.sum(grad_hat * hat, axis=-1, keepdims=True),
        )

    return pl.pallas_call(
        kernel,
        out_shape=[
            jax.ShapeDtypeStruct((length, held), BF16),
            jax.ShapeDtypeStruct((length, held), F32),
            jax.ShapeDtypeStruct((length, held), F32),
            jax.ShapeDtypeStruct((length, 128), F32),
            jax.ShapeDtypeStruct((8, length), F32),
            jax.ShapeDtypeStruct((1, held), F32),
        ],
        compiler_params=kernel_params(),
        cost_estimate=costs(0.416),
    )(conv, turned, grad_act, *stats)


def conv_backward(grad_hat, hat, inverse, sums, gated, segments, linear, gate, turned, taps, gain_term):
    length, held = hat.shape
    count = len(sums)
    margin = (taps - 1) // 2
    groups = held // 128

    def kernel(
        grad_ref, hat_ref, inverse_ref, gated_ref, seg_ref, linear_ref, gate_ref, turned_ref,
        gain_ref, *refs
    ):
        tables, (proj, terms), (grad_conv, partial, grad_near, gated_near, seg_near) = (
            refs[:count], refs[count : count + 2], refs[count + 2 :],
        )
        total = sum(table[...] for table in tables) * (1.0 / (held * count))
        first, second = rows_of(total)
        edge = jnp.zeros((PAD, held), F32)
        grad_conv[:PAD, :] = edge
        grad_conv[PAD + length :, :] = edge
        value = (grad_ref[...] - first - hat_ref[...] * second) * inverse_ref[:, :1]
        grad_conv[PAD : PAD + length, :] = value.astype(BF16).astype(F32)
        partial[...] = jnp.zeros_like(partial)

        def tile(t, carry):
            base = pl.multiple_of(t * TILE, TILE)
            grad_near[...] = grad_conv[pl.ds(base, TILE + 2 * PAD), :]
            gated_near[...] = gated_ref[pl.ds(base, TILE + 2 * PAD), :]
            seg_near[...] = seg_ref[pl.ds(base, TILE + 2 * PAD), :]
            centre = seg_near[PAD : PAD + TILE, :]
            lanes = [slice(g * 128, (g + 1) * 128) for g in range(groups)]
            here = [grad_near[PAD : PAD + TILE, lanes[g]] for g in range(groups)]
            back = [jnp.zeros((TILE, 128), F32) for _ in range(groups)]
            for k in range(taps):
                shift = PAD + k - margin
                inside = seg_near[shift : shift + TILE, :] == centre
                for g in range(groups):
                    near = grad_near[shift : shift + TILE, lanes[g]]
                    weight = turned_ref[taps - 1 - k : taps - k, lanes[g]]
                    back[g] = back[g] + jnp.where(inside, near, 0.0) * weight
                    source = gated_near[shift : shift + TILE, lanes[g]]
                    product = jnp.where(inside, source, 0.0) * here[g]
                    partial[k, :, lanes[g]] += jnp.sum(
                        product.reshape(TILE // 8, 8, 128), axis=0
                    )
            for g in range(groups):
                sigma = gate_ref[pl.ds(base, TILE), lanes[g]]
                part = back[g] * sigma
                proj[pl.ds(base, TILE), lanes[g]] = part.astype(BF16)
                far = slice(held + g * 128, held + (g + 1) * 128)
                proj[pl.ds(base, TILE), far] = (
                    part * linear_ref[pl.ds(base, TILE), lanes[g]] * (1.0 - sigma)
                ).astype(BF16)
            return carry

        lax.fori_loop(0, length // TILE, tile, 0)
        terms[:taps, :] = jnp.sum(partial[...], axis=1)
        terms[taps : taps + 1, :] = gain_ref[...]

    return pl.pallas_call(
        kernel,
        out_shape=[
            jax.ShapeDtypeStruct((length, 2 * held), BF16),
            jax.ShapeDtypeStruct((taps + 1, held), F32),
        ],
        scratch_shapes=[
            pltpu.VMEM((length + 2 * PAD, held), F32),
            pltpu.VMEM((taps, 8, held), F32),
            pltpu.VMEM((TILE + 2 * PAD, held), F32),
            pltpu.VMEM((TILE + 2 * PAD, held), F32),
            pltpu.VMEM((TILE + 2 * PAD, 128), F32),
        ],
        compiler_params=kernel_params(),
        cost_estimate=costs(4.02),
    )(grad_hat, hat, inverse, gated, segments, linear, gate, turned, gain_term, *sums)


def stem_message(turned, parts, small, axis, chains, stem_rows):
    dp_count = lax.axis_size(axis)
    stride, size = chains[-1]
    count, share, width = turned.shape
    channels = parts[0].shape[1]
    rows = dp_count * stem_rows
    own = channels // dp_count
    height = stem_rows + 16

    folds = channels // small.shape[1]
    below = small.shape[0] // folds

    def kernel(turned_ref, small_ref, *refs):
        outs = refs[count:]
        place = (lax.axis_index(axis) // stride) % size
        total = jnp.zeros((share, channels), F32)
        for k in range(count):
            total = total + jnp.dot(turned_ref[k], refs[k][...], preferred_element_type=F32)
        lower = jnp.concatenate(
            [small_ref[q * below : (q + 1) * below, :] for q in range(folds)], axis=1
        )
        for i in range(dp_count):
            gain = jnp.concatenate(
                [total[rows : rows + 1, i * own : (i + 1) * own], jnp.zeros((1, channels - own), F32)],
                axis=1,
            )
            block = jnp.concatenate(
                [
                    total[i * stem_rows : (i + 1) * stem_rows],
                    lower,
                    gain,
                    jnp.zeros((7, channels), F32),
                ],
                axis=0,
            ).astype(BF16)
            for k in range(size):

                @pl.when(i % size ^ place == k)
                def _():
                    outs[k][i // size] = block

    return pl.pallas_call(
        kernel,
        out_shape=[jax.ShapeDtypeStruct((dp_count // size, height, channels), BF16)] * size,
        compiler_params=kernel_params(),
        cost_estimate=costs(2.73),
    )(turned, small, *parts)


def stem_finish(parts, stem_rows, rows, taps, axis):
    channels = parts[0].shape[2]
    count = len(parts)

    def kernel(*refs):
        stem, kernel_out, post, pre = refs[count:]
        total = sum(jnp.sum(part[...].astype(F32), axis=0) for part in refs[:count])
        stem[...] = total[:stem_rows]
        held = channels // lax.axis_size(axis)
        below = (taps + 1) * held // channels
        pick = iota((held, rows), 0) == iota((held, rows), 1) + lax.axis_index("dp") * rows
        pick = jnp.where(pick, 1.0, 0.0)
        lower = total[stem_rows : stem_rows + below]
        rest = jnp.concatenate(
            [
                jnp.dot(
                    lower[:, q * held : (q + 1) * held],
                    pick,
                    preferred_element_type=F32,
                    precision=lax.Precision.HIGHEST,
                )
                for q in range(channels // held)
            ],
            axis=0,
        )
        kernel_out[...] = rest.T[:, :taps]
        post[...] = rest[taps : taps + 1]
        at, to = iota((channels, rows), 0), iota((channels, rows), 1)
        mine = lax.axis_index(axis) * rows
        own = jnp.where(at == to + mine, 1.0, 0.0)
        line = jnp.broadcast_to(total[stem_rows + below : stem_rows + below + 1], (8, channels))
        pre[...] = jnp.dot(
            line, own, preferred_element_type=F32, precision=lax.Precision.HIGHEST
        )[:1]

    return pl.pallas_call(
        kernel,
        out_shape=[
            jax.ShapeDtypeStruct((stem_rows, channels), F32),
            jax.ShapeDtypeStruct((rows, taps), F32),
            jax.ShapeDtypeStruct((1, rows), F32),
            jax.ShapeDtypeStruct((1, rows), F32),
        ],
        compiler_params=kernel_params(),
        cost_estimate=costs(0.614),
    )(*parts)


def one_hot(rows, columns):
    return (rows[:, None] == columns[None, :]).astype(BF16)


def order_pieces(mel_pieces, dest_owner, dest_slot, dp_count):
    pieces, piece_values = mel_pieces.shape
    capacity = max(2, 2 * pieces // dp_count)
    matches = (dest_owner[:, None] == jnp.arange(dp_count, dtype=jnp.int32)[None, :]).astype(jnp.int32)
    earlier = jnp.cumsum(matches, axis=0) - matches
    position = dest_owner * capacity + jnp.sum(earlier * matches, axis=1)
    pick = one_hot(jnp.arange(dp_count * capacity, dtype=jnp.int32), position)
    label = jnp.broadcast_to((dest_slot + 1).astype(BF16)[:, None], (pieces, 128))
    return jnp.dot(
        pick, jnp.concatenate([mel_pieces, label], axis=1), preferred_element_type=F32
    ).astype(BF16)


def per_device(
    mel_pieces,
    dest_owner,
    dest_slot,
    segment_ids,
    out_grad,
    stem_weight,
    up_weight,
    down_weight,
    depth_kernel,
    gain_pre,
    gain_post,
):
    dp_count = lax.axis_size("dp")
    tm_count = lax.axis_size("tm")
    chains = stages_of({"dp": dp_count, "tm": tm_count})
    dp_chains, tm_chains = chains["dp"], chains["tm"]
    column = lax.axis_index("tm")
    taps = depth_kernel.shape[1]
    margin = (taps - 1) // 2
    block = out_grad.shape[1]
    channels = out_grad.shape[2]
    held = channels // tm_count
    rows = down_weight.shape[0]
    stem_rows = stem_weight.shape[0]
    features = stem_rows * dp_count * tm_count
    length = block * tm_count

    sums_chains = ((4, 2), (2, 2), (1, 2))

    by_parts = stem_rows % 16 == 0 and rows % 16 == 0 and dp_chains == ((2, 4), (1, 2))
    span = 128 * tm_count
    lane = jnp.arange(span, dtype=jnp.int32)
    grouped = (lane // rows) % tm_count * 128 + lane // (rows * tm_count) * rows + lane % rows
    chunks = rows // stem_rows
    if by_parts:
        up_parts = up_columns(up_weight, rows, tm_count)
        sent, pack = prepare(
            mel_pieces[0], dest_owner[0], dest_slot[0], after(stem_weight, up_parts[0]),
            down_weight, depth_kernel, gain_pre, gain_post, dp_count,
        )
    else:
        sent = order_pieces(mel_pieces[0], dest_owner[0], dest_slot[0], dp_count)
        up_parts = regroup_columns(up_weight, lane, grouped, "tm", tm_count)
        beside = jnp.broadcast_to(jnp.tile(gain_pre, 128 // rows)[None, :], (stem_rows, 128))
        small = jnp.concatenate(
            [depth_kernel, gain_post[:, None], jnp.zeros((rows, 128 - taps - 1), BF16)], axis=1
        )
        folded = [
            value[q : q + stem_rows]
            for value in (small, down_weight)
            for q in range(0, rows, stem_rows)
        ]
        pack = jnp.concatenate([stem_weight, beside] + folded, axis=1)

    up_parts = [up_parts[0]] + [swap(up_parts[k], "tm", k) for k in range(1, tm_count)]
    up_mine = place_parts(up_parts, "tm", 1, tm_count, 0).reshape(tm_count * rows, 2 * held)
    pack_near = gather_stage(pack, "dp", *dp_chains[0], 0)
    up_sides = swap_parts([up_mine] * dp_chains[0][1], "dp", dp_chains[0])
    stem_mine, small_all, down_full = split_rest(
        pack_near, "dp", dp_chains, ((channels + 128, 1), (128, chunks), (channels, chunks))
    )
    stem_mine = stem_mine.reshape(dp_count, stem_rows, channels + 128)
    small_all = small_all.reshape(held, 128)
    down_full = down_full.reshape(held, channels)

    pieces = mel_pieces.shape[1]
    capacity = max(2, 2 * pieces // dp_count)
    arrived = lax.all_to_all(
        after(sent, pack_near).reshape(dp_count, capacity, -1),
        "dp",
        split_axis=0,
        concat_axis=0,
        tiled=True,
    ).reshape(dp_count * capacity, -1)
    up_near = place_parts(up_sides, "dp", *dp_chains[0], 0)
    frames = place_frames(after(arrived, up_near), pieces, features)
    frame_parts = gather_parts(frames, "tm", tm_chains)
    stem_parts = gather_parts(stem_mine, "tm", tm_chains, frames)
    frames = place_parts(frame_parts, "tm", 1, tm_count, 0).reshape(length, features)
    stem_all = place_parts(stem_parts, "tm", 1, tm_count, 1)
    stem_all = stem_all.reshape(features, channels + 128)

    grad_out = out_grad[0]
    grad_first = after(grad_out, up_near)
    hierarchical = list(tm_chains) == [(2, 2), (1, 2)]
    if hierarchical:
        grad_parts = [grad_first, swap(grad_first, "tm", 1), swap(grad_first, "tm", 2)]
    else:
        grad_parts = gather_parts(grad_first, "tm", tm_chains)

    segments = spread_segments(segment_ids)

    extra = 16
    normed, stem_pre, gain_one = stem_forward(frames, stem_all, tm_count, "tm", rows)
    frames_turned = turn_frames(after(frames, normed), tm_count, "tm", stem_rows, extra)
    up_full = gather_rest(up_near, "dp", dp_chains).reshape(channels, 2 * held)
    grad_parts = lax.optimization_barrier((grad_parts, normed))[0]
    if hierarchical:
        grad_parts = grad_parts + [swap(grad_parts[2], "tm", 1)]
    linear, gate_sig, gated = up_forward(normed, up_full)
    conv, stats, turned = conv_forward(gated, small_all, segments, taps)
    stats = swap_all(stats, "tm")
    grad_parts = lax.optimization_barrier((grad_parts, conv))[0]
    grad_out_all = place_parts(grad_parts, "tm", 1, tm_count, 0).reshape(length, channels)
    grad_act = multiply_turned(grad_out_all, down_full)
    activated, conv_hat, grad_hat, inverse, sums, gain_post_term = activate(
        conv, stats, turned, grad_act, taps
    )
    sums = swap_all(sums, "tm")
    if by_parts:
        down_terms = part_terms(activated, grad_out_all, False, "dp", sums_chains)
        normed_turned = turn(normed)
        grad_hat = after(grad_hat, normed_turned)
    else:
        down_terms = [message_terms(activated, grad_out_all, dp_count, tm_count)]
    down_terms = lax.optimization_barrier((down_terms, *sums))[0]
    if by_parts:
        down_parts = swap_parts(down_terms, "dp", sums_chains[-1])

    grad_hat = after(grad_hat, *down_terms)
    grad_proj, kernel_term = conv_backward(
        grad_hat, conv_hat, inverse, sums, gated, segments, linear, gate_sig, turned, taps,
        gain_post_term,
    )

    own_terms, *other_terms = block_terms(
        after(grad_proj, *down_parts[1:]) if by_parts else grad_proj, up_full, True, "tm", tm_count
    )
    if by_parts:
        up_terms = part_terms(
            after(normed_turned, *other_terms), grad_proj, True, "dp", sums_chains
        )
        up_parts = swap_parts(up_terms, "dp", sums_chains[-1])
    else:
        up_terms = [message_terms(normed, grad_proj, dp_count, tm_count)]
    grad_far, grad_parts, grad_passed = block_sum(other_terms, "tm", tm_chains, up_terms[-1])
    if by_parts:
        down_parts[0] = after(down_parts[0], grad_passed)
        down_parts = add_parts(down_parts, "dp", sums_chains[1])
        down_parts = swap_parts(down_parts, "dp", sums_chains[1])
        own_terms = own_terms
    y_own, *y_others = block_terms(
        after(activated, grad_passed), down_full, False, "tm", tm_count
    )
    grad_stem_pre = stem_backward(
        own_terms, grad_parts + [grad_far], stem_pre, grad_out, gain_one, extra
    )
    if by_parts:
        up_parts[0] = after(up_parts[0], grad_stem_pre)
        up_parts = add_parts(up_parts, "dp", sums_chains[1])
        down_parts[0] = after(down_parts[0], up_parts[-1])
        down_parts = add_parts(down_parts, "dp", sums_chains[0])
        down_parts = swap_parts(down_parts, "dp", sums_chains[0])
        grad_stem_parts = gather_parts(grad_stem_pre, "tm", tm_chains, down_parts[0])
        up_parts = reduce_rest(up_parts, "dp", sums_chains[:2])
    else:
        grad_stem_parts = gather_parts(grad_stem_pre, "tm", tm_chains)
    y_far, y_parts, _ = block_sum(y_others, "tm", tm_chains, grad_stem_parts[2])
    if by_parts:
        stem_terms = stem_message(
            frames_turned, grad_stem_parts, kernel_term, "dp", sums_chains, stem_rows
        )
        stem_sums = reduce_rest(stem_terms, "dp", sums_chains)
    else:
        stem_sum = sum(
            jnp.dot(frames_turned[k], grad_stem_parts[k], preferred_element_type=F32)
            for k in range(tm_count)
        )
        share = features // tm_count
        gain_term = stem_sum[share].reshape(dp_count, 1, tm_count * rows)
        gain_term = jnp.pad(gain_term, ((0, 0), (0, 0), (0, channels - tm_count * rows)))
        stem_terms = stem_sum[:share].reshape(dp_count, stem_rows, channels)
        folds = channels // held
        small_term = kernel_term.reshape(folds, -1, held).transpose(1, 0, 2).reshape(-1, channels)
        small_term = jnp.broadcast_to(small_term[None], (dp_count,) + small_term.shape)
        stem_terms = jnp.concatenate([stem_terms, small_term, gain_term], axis=1)
        stem_terms = jnp.pad(stem_terms.astype(BF16), ((0, 0), (0, 7), (0, 0)))
        stem_sums = [
            lax.all_to_all(stem_terms, "dp", split_axis=0, concat_axis=0, tiled=True)
        ]
    if by_parts:
        up_parts[0] = after(up_parts[0], *stem_terms)
        up_parts = cut_columns(up_parts, down_parts, "tm")
        up_parts = swap_all_parts(up_parts, "tm")
        grad_up, grad_down = mix_columns(up_parts, "tm", tm_count * rows, rows)
    else:
        down_sums = lax.all_to_all(
            down_terms[0], ("dp", "tm"), split_axis=0, concat_axis=0, tiled=True
        )
        grad_down = jnp.sum(
            down_sums.reshape(dp_count, tm_count * rows, held).astype(F32), axis=0
        )
        up_sums = lax.all_to_all(
            up_terms[0], ("dp", "tm"), split_axis=0, concat_axis=0, tiled=True
        )
        up_sums = up_sums.reshape(dp_count, tm_count, tm_count * rows, 128)
        spread = one_hot(lane, grouped).reshape(tm_count, 128, span)
        grad_up = jnp.einsum("ijab,jbc->ac", up_sums, spread, preferred_element_type=F32)
    y_out = finish_rows(stem_pre, y_own, y_parts + [y_far])
    grad_stem, grad_kernel, grad_gain_post, grad_gain_pre = stem_finish(
        stem_sums, stem_rows, rows, taps, "tm"
    )
    grad_gain_post, grad_gain_pre = grad_gain_post[0], grad_gain_pre[0]
    return (y_out[None], grad_stem, grad_up, grad_down, grad_kernel, grad_gain_pre, grad_gain_post)


def solution(mesh):
    return jax.shard_map(
        per_device,
        mesh=mesh,
        in_specs=(
            P("dp", "tm", None),
            P("dp", "tm"),
            P("dp", "tm"),
            P("dp", None),
            P("dp", "tm", None),
            P(("dp", "tm"), None),
            P(("dp", "tm"), None),
            P(("dp", "tm"), None),
            P(("dp", "tm"), None),
            P(("dp", "tm")),
            P(("dp", "tm")),
        ),
        out_specs=(
            P("dp", "tm", None),
            P(("dp", "tm"), None),
            P("dp", "tm"),
            P("dp", "tm"),
            P(("dp", "tm"), None),
            P(("dp", "tm")),
            P(("dp", "tm")),
        ),
        check_vma=False,
    )
```
